128 devices in a mesh: wide: 16 (over x, z), narrow: 8 (over y, core).
Axes of the slice: x: 4, y: 4, z: 4, core: 2. Of those that a mesh axis runs over, the one named last changes fastest.
Arguments:
- activations: bfloat16 [4096, 16384], P('wide', 'narrow'), may hold values from -6 to 6
- grad_out: bfloat16 [4096, 8192], P('narrow', 'wide'), may hold values from -0.09375 to 0.09375
- momentum: float32 [8192, 16384], P('wide', 'narrow'), may hold values from -90 to 90
- right_factor: float32 [16384, 512], P('narrow'), may hold values from -0.046875 to 0.046875
Outputs:
- new_momentum: float32 [8192, 16384], P('wide', 'narrow')
- new_right: float32 [16384, 512], P('narrow')
- update: bfloat16 [8192, 16384], P('wide', 'narrow')
The draws below stay inside these ranges and needn't reach their ends.
All inputs are finite; a program needn't handle non-finite values.
Results may differ from the reference program's by a relative error of at most 0.0012.
Values may be sent and summed in bfloat16 or wider, within the bound.
A program may use at most 128 MiB of HBM per device.

```python
import math
import jax
import jax.numpy as jnp
from jax import lax

DOUT = 8192
DIN = 16384
RANK = 512
TOKENS = 4096


def draw_momentum(key, part):
    base = jax.random.fold_in(key, 31)
    first = jax.random.fold_in(base, 0)
    row_scale = 0.5 + jnp.arange(DOUT, dtype=jnp.float32) / (DOUT - 1)
    col_scale = 0.5 + jnp.arange(DIN, dtype=jnp.float32) / (DIN - 1)
    values = jax.random.truncated_normal(first, -4.0, 4.0, (DOUT, DIN), jnp.float32)
    return (values * row_scale[:, None] * col_scale[None, :]).astype(jnp.float32)


def block_scale(stream_key, shape, cuts, least, largest):
    def one(position, shards_of):
        draws = jax.random.uniform(jax.random.fold_in(jax.random.fold_in(stream_key, 6), position), (shards_of,), jnp.float32, least / len(cuts), largest / len(cuts))
        return jnp.repeat(jnp.exp(draws), shape[position] // shards_of).reshape((-1,) + (1,) * (len(shape) - position - 1))

    gain = one(*cuts[0])
    for cut in cuts[1:]:
        gain = gain * one(*cut)
    return gain


def bell_draw(stream_key, extent, spread, bound, shards=(), held_as=jnp.bfloat16):
    drawn = spread * jax.random.normal(stream_key, extent, jnp.float32)
    if shards:
        drawn = drawn * block_scale(stream_key, extent, shards, -0.22, 0.18)
    return jnp.clip(drawn, -bound, bound).astype(held_as)


def setup_inputs(seed: int = 0) -> dict:
    key_list = jax.random.split(jax.random.key(seed), 5)
    return {
        "activations": bell_draw(key_list[0], (TOKENS, DIN), 1.0, 6.0, ((0, 16), (1, 8))),
        "grad_out": bell_draw(key_list[1], (TOKENS, DOUT), TOKENS ** -0.5, 0.09375, ((0, 8), (1, 16))),
        "momentum": draw_momentum(jax.random.fold_in(key_list[4], 71), 0),
        "right_factor": bell_draw(key_list[3], (DIN, RANK), DIN ** -0.5, 0.046875, ((0, 8),), jnp.float32),
    }


FEEDBACK = 0.05
EPSILON = 1e-06

def reference(activations, grad_out, momentum, right_factor):
    highest = lax.Precision.HIGHEST
    gradient = lax.dot_general(grad_out.astype(jnp.float32), activations.astype(jnp.float32), (((0,), (0,)), ((), ())), preferred_element_type=jnp.float32)
    buffer = momentum + gradient
    left_factor = jnp.dot(buffer.astype(jnp.float32), right_factor.astype(jnp.float32), precision=highest, preferred_element_type=jnp.float32)
    gram_matrix = jnp.dot(left_factor.T.astype(jnp.float32), left_factor.astype(jnp.float32), precision=highest, preferred_element_type=jnp.float32)
    lower_factor = jnp.linalg.cholesky(gram_matrix)
    ortho_left = jax.scipy.linalg.solve_triangular(lower_factor, left_factor.T, lower=True).T
    right_raw = lax.dot_general(buffer.astype(jnp.float32), ortho_left.astype(jnp.float32), (((0,), (0,)), ((), ())), precision=highest, preferred_element_type=jnp.float32)
    feedback = lax.dot_general(ortho_left.astype(jnp.float32), right_raw.astype(jnp.float32), (((1,), (1,)), ((), ())), precision=highest, preferred_element_type=jnp.float32)
    new_momentum = buffer - FEEDBACK * feedback
    col_squares = lax.optimization_barrier(jnp.sum(right_raw * right_raw, axis=0))
    new_right = right_raw / (jnp.sqrt(col_squares) + EPSILON)
    update_scale = math.sqrt(DOUT * DIN / RANK)
    product = lax.dot_general(ortho_left.astype(jnp.float32), new_right.astype(jnp.float32), (((1,), (1,)), ((), ())), precision=highest, preferred_element_type=jnp.float32)
    update = (update_scale * product).astype(jnp.bfloat16)
    return (new_momentum, new_right, update)
```

```python
import math

import jax
import jax.numpy as jnp
from jax import lax
from jax.experimental import pallas as pl
from jax.experimental.pallas import tpu as pltpu
from jax.sharding import Mesh
from jax.sharding import PartitionSpec as P

DOUT = 8192
DIN = 16384
RANK = 512
X, Z, Y, C = "wide_0", "wide_1", "narrow_0", "narrow_1"
NARROW = (Y, C)
WIDE = (X, Z)
FEEDBACK = 0.05
EPSILON = 1e-06
F32 = jnp.float32
BF16 = jnp.bfloat16
VMEM = pl.BlockSpec(memory_space=pltpu.VMEM)
MESH = pl.DeviceIdType.MESH

def eliminated(rows):
    lane = lax.broadcasted_iota(jnp.int32, (8, 128), 1)
    sub = lax.broadcasted_iota(jnp.int32, (8, 128), 0)
    groups = len(rows)
    for p in range(groups):
        here = rows[p]
        cols = [jnp.broadcast_to(here[:, 8 * p + k : 8 * p + k + 1], (8, 128)) for k in range(8)]
        a = [[jnp.broadcast_to(cols[k][i : i + 1, :], (8, 128)) if k <= i else None for k in range(8)] for i in range(8)]
        low = [[None] * 8 for _ in range(8)]
        root = [None] * 8
        for k in range(8):
            root[k] = lax.rsqrt(a[k][k])
            for i in range(k + 1, 8):
                low[i][k] = a[i][k] * root[k]
            for i in range(k + 1, 8):
                for j in range(k + 1, i + 1):
                    a[i][j] = a[i][j] - low[i][k] * low[j][k]
        inside = (lane >= 8 * p) & (lane < 8 * p + 8)
        unit = jnp.where(lane == sub + 8 * p, 1.0, 0.0).astype(F32)
        source = jnp.where(inside, unit, here)
        y = []
        for k in range(8):
            value = jnp.broadcast_to(source[k : k + 1, :], (8, 128))
            for m in range(k):
                value = value - low[k][m] * y[m]
            y.append(value * root[k])
        done = y[0]
        for k in range(1, 8):
            done = jnp.where(sub == k, y[k], done)
        rows[p] = done
        for g in range(p + 1, groups):
            c = []
            total = jnp.where(inside, 0.0, rows[g])
            for k in range(8):
                value = jnp.broadcast_to(rows[g][:, 8 * p + k : 8 * p + k + 1], (8, 128))
                for m in range(k):
                    value = value - low[k][m] * c[m]
                c.append(value * root[k])
                total = total - c[k] * y[k]
            rows[g] = total
    return rows

def factor_kernel(c_ref, out_ref, s_ref):
    hi = lax.Precision.HIGHEST
    s_ref[...] = c_ref[...]
    row = lax.broadcasted_iota(jnp.int32, (128, 128), 0)
    col = lax.broadcasted_iota(jnp.int32, (128, 128), 1)
    for b in range(4):
        o = 128 * b
        rows = [s_ref[o + 8 * g : o + 8 * g + 8, o : o + 128] for g in range(16)]
        inv = jnp.concatenate(eliminated(rows), axis=0)
        inv = jnp.where(row >= col, inv, 0.0)
        s_ref[o : o + 128, o : o + 128] = jnp.where(row == col, 1.0, 0.0).astype(F32)
        y = jnp.dot(inv, s_ref[o : o + 128, :], precision=hi, preferred_element_type=F32)
        s_ref[o : o + 128, :] = y
        if b < 3:
            rest = y[:, o + 128 :]
            s_ref[o + 128 :, o : o + 128] = jnp.zeros((384 - o, 128), F32)
            s_ref[o + 128 :, :] = s_ref[o + 128 :, :] - lax.dot_general(
                rest, y, (((0,), (0,)), ((), ())), precision=hi, preferred_element_type=F32)
    row = lax.broadcasted_iota(jnp.int32, (512, 512), 0)
    col = lax.broadcasted_iota(jnp.int32, (512, 512), 1)
    out_ref[...] = jnp.where(row >= col, s_ref[...], 0.0)

def inverse_factor(c):
    return pl.pallas_call(factor_kernel, out_shape=jax.ShapeDtypeStruct((512,512),F32),
        in_specs=[pl.BlockSpec(memory_space=pltpu.VMEM)], out_specs=pl.BlockSpec(memory_space=pltpu.VMEM),
        scratch_shapes=[pltpu.VMEM((512,512),F32)],
        compiler_params=pltpu.CompilerParams(vmem_limit_bytes=32<<20))(c)


def halves(value):
    high = value.astype(BF16)
    return high, (value - high.astype(F32)).astype(BF16)


def dot3(left, right, dims):
    a, b = halves(left)
    c, d = halves(right)
    one = lambda u, v: lax.dot_general(u, v, (dims, ((), ())), preferred_element_type=F32)
    return one(a, c) + (one(a, d) + one(b, c))


def partner(axis, step):
    size = 2 if axis == C else 4
    return lax.rem(lax.axis_index(axis) + step, size)


def greet(peers):
    barrier = pltpu.get_barrier_semaphore()
    for peer in peers:
        pl.semaphore_signal(barrier, inc=1, device_id=peer, device_id_type=MESH)
    pl.semaphore_wait(barrier, len(peers))


def line_peers(axes):
    peers = []
    for axis in axes:
        for step in range(1, 2 if axis == C else 4):
            peers.append({axis: partner(axis, step)})
    return peers


def sent(send, recv, phase, axis, source, target):
    copies = []
    for step in range(1, 2 if axis == C else 4):
        to = partner(axis, step)
        copy = pltpu.make_async_remote_copy(
            src_ref=source(to),
            dst_ref=target(to),
            send_sem=send.at[phase, step - 1],
            recv_sem=recv.at[phase, step - 1],
            device_id={axis: to},
            device_id_type=MESH,
        )
        copy.start()
        copies.append(copy)
    return copies


def all_of(copies):
    for copy in copies:
        copy.wait()


def left_kernel(part, left, gram, pair, half, share, block, gx, gz, send, recv):
    x, z, y, c = (lax.axis_index(a) for a in (X, Z, Y, C))
    greet(line_peers((X, Z, Y, C)))
    all_of(sent(send, recv, 0, C, lambda to: part.at[to], lambda to: pair))
    half[...] = part[c] + pair[...]
    copies = sent(send, recv, 1, Y, lambda to: half.at[to], lambda to: share.at[y])
    share[y] = half[y]
    all_of(copies)
    left[c, y] = (share[0] + share[1]) + (share[2] + share[3])
    all_of(sent(send, recv, 2, Y, lambda to: left.at[c, y], lambda to: left.at[c, y]))
    all_of(sent(send, recv, 3, C, lambda to: left.at[c], lambda to: left.at[c]))
    whole = left[...].reshape(RANK, RANK)
    for index in range(4):
        @pl.when(y == index)
        def _():
            own = whole[:, 128 * index : 128 * index + 128]
            block[...] = dot3(own, whole, ((0,), (0,))).reshape(2, 4, 16, RANK)
    copies = sent(send, recv, 4, X, lambda to: block.at[c, to], lambda to: gx.at[x])
    gx[x] = block[c, x]
    all_of(copies)
    gz[z] = (gx[0] + gx[1]) + (gx[2] + gx[3])
    all_of(sent(send, recv, 5, Z, lambda to: gz.at[z], lambda to: gz.at[z]))
    gram[y, c, x] = (gz[0] + gz[1]) + (gz[2] + gz[3])
    all_of(sent(send, recv, 6, X, lambda to: gram.at[y, c, x], lambda to: gram.at[y, c, x]))
    all_of(sent(send, recv, 7, Y, lambda to: gram.at[y, c], lambda to: gram.at[y, c]))
    all_of(sent(send, recv, 8, C, lambda to: gram.at[:, c], lambda to: gram.at[:, c]))


def left_and_gram(part):
    left, gram = pl.pallas_call(
        left_kernel,
        out_shape=(
            jax.ShapeDtypeStruct((2, 4, 64, RANK), F32),
            jax.ShapeDtypeStruct((4, 2, 4, 16, RANK), F32),
        ),
        in_specs=[VMEM],
        out_specs=(VMEM, VMEM),
        scratch_shapes=[
            pltpu.VMEM((4, 64, RANK), F32),
            pltpu.VMEM((4, 64, RANK), F32),
            pltpu.VMEM((4, 64, RANK), F32),
            pltpu.VMEM((2, 4, 16, RANK), F32),
            pltpu.VMEM((4, 16, RANK), F32),
            pltpu.VMEM((4, 16, RANK), F32),
            pltpu.SemaphoreType.DMA((9, 3)),
            pltpu.SemaphoreType.DMA((9, 3)),
        ],
        compiler_params=pltpu.CompilerParams(
            collective_id=1, has_side_effects=True, vmem_limit_bytes=40 << 20
        ),
        cost_estimate=pl.CostEstimate(flops=1 << 26, bytes_accessed=64 << 20, transcendentals=0),
    )(part.reshape(2, 4, 64, RANK))
    return left.reshape(RANK, RANK), gram.reshape(RANK, RANK)


def right_kernel(part, out, from_x, from_z, sum_x, sum_z, end_x, end_z, send, recv):
    x, z = lax.axis_index(X), lax.axis_index(Z)
    greet(line_peers((X, Z)))
    a = sent(send, recv, 0, X, lambda to: part.at[to, :, 0], lambda to: from_x.at[x])
    b = sent(send, recv, 1, Z, lambda to: part.at[:, to, 1], lambda to: from_z.at[z])
    from_x[x] = part[x, :, 0]
    from_z[z] = part[:, z, 1]
    all_of(a)
    sum_x[...] = (from_x[0] + from_x[1]) + (from_x[2] + from_x[3])
    a = sent(send, recv, 2, Z, lambda to: sum_x.at[to], lambda to: end_z.at[z])
    all_of(b)
    sum_z[...] = (from_z[0] + from_z[1]) + (from_z[2] + from_z[3])
    b = sent(send, recv, 3, X, lambda to: sum_z.at[to], lambda to: end_x.at[x])
    end_z[z] = sum_x[z]
    end_x[x] = sum_z[x]
    all_of(a)
    out[x, z, 0] = (end_z[0] + end_z[1]) + (end_z[2] + end_z[3])
    a = sent(send, recv, 4, Z, lambda to: out.at[x, z, 0], lambda to: out.at[x, z, 0])
    all_of(b)
    out[x, z, 1] = (end_x[0] + end_x[1]) + (end_x[2] + end_x[3])
    b = sent(send, recv, 5, X, lambda to: out.at[x, z, 1], lambda to: out.at[x, z, 1])
    all_of(a)
    a = sent(send, recv, 6, X, lambda to: out.at[x, :, 0], lambda to: out.at[x, :, 0])
    all_of(b)
    b = sent(send, recv, 7, Z, lambda to: out.at[:, z, 1], lambda to: out.at[:, z, 1])
    all_of(a)
    all_of(b)


def right_sum(part):
    out = pl.pallas_call(
        right_kernel,
        out_shape=jax.ShapeDtypeStruct((4, 4, 2, 64, RANK), F32),
        in_specs=[VMEM],
        out_specs=VMEM,
        scratch_shapes=[
            pltpu.VMEM((4, 4, 64, RANK), F32),
            pltpu.VMEM((4, 4, 64, RANK), F32),
            pltpu.VMEM((4, 64, RANK), F32),
            pltpu.VMEM((4, 64, RANK), F32),
            pltpu.VMEM((4, 64, RANK), F32),
            pltpu.VMEM((4, 64, RANK), F32),
            pltpu.SemaphoreType.DMA((8, 3)),
            pltpu.SemaphoreType.DMA((8, 3)),
        ],
        compiler_params=pltpu.CompilerParams(
            collective_id=2, has_side_effects=True, vmem_limit_bytes=40 << 20
        ),
        cost_estimate=pl.CostEstimate(flops=1 << 22, bytes_accessed=128 << 20, transcendentals=0),
    )(part.reshape(4, 4, 2, 64, RANK))
    return out.reshape(-1, RANK)


def raw_kernel(w_ref, p_ref, inv_ref, right, left, scale, seen, send, recv):
    y, c = lax.axis_index(Y), lax.axis_index(C)
    greet(line_peers((Y, C)))
    right[...] = dot3(w_ref[...], inv_ref[...], ((1,), (1,)))
    squares = right[...] * right[...]
    seen[4 + c] = jnp.sum(squares.reshape(-1, 8, RANK), axis=0)
    all_of(sent(send, recv, 0, C, lambda to: seen.at[4 + c], lambda to: seen.at[4 + c]))
    seen[y] = seen[4] + seen[5]
    copies = sent(send, recv, 1, Y, lambda to: seen.at[y], lambda to: seen.at[y])
    left[...] = dot3(p_ref[...], inv_ref[...], ((1,), (1,)))
    all_of(copies)
    total = jnp.sum((seen[0] + seen[1]) + (seen[2] + seen[3]), axis=0, keepdims=True)
    scale[...] = jnp.broadcast_to(jnp.sqrt(total) + EPSILON, (8, RANK))


def raw_factors(w, p, inv):
    return pl.pallas_call(
        raw_kernel,
        out_shape=(
            jax.ShapeDtypeStruct(w.shape, F32),
            jax.ShapeDtypeStruct(p.shape, F32),
            jax.ShapeDtypeStruct((8, RANK), F32),
        ),
        in_specs=[VMEM] * 3,
        out_specs=(VMEM,) * 3,
        scratch_shapes=[
            pltpu.VMEM((6, 8, RANK), F32),
            pltpu.SemaphoreType.DMA((2, 3)),
            pltpu.SemaphoreType.DMA((2, 3)),
        ],
        compiler_params=pltpu.CompilerParams(
            collective_id=3, has_side_effects=True, vmem_limit_bytes=40 << 20
        ),
        cost_estimate=pl.CostEstimate(flops=1 << 30, bytes_accessed=16 << 20, transcendentals=0),
    )(w, p, inv)


def sent_to_all(array, axis):
    devices = lax.axis_size(axis)
    return lax.all_to_all(
        jnp.broadcast_to(array[None], (devices, *array.shape)), axis, 0, 0, tiled=True
    )


def gathered_by_axis(array, axes):
    far, near = axes
    tiles = sent_to_all(sent_to_all(array, far), near)
    return tiles.swapaxes(0, 1).reshape(-1, *array.shape[1:])


def body(activations, grad_out, momentum, right_factor):
    high = lax.Precision.HIGH
    out_rows = gathered_by_axis(grad_out, NARROW)
    gradient = lax.dot_general(
        out_rows,
        lax.all_gather(activations, WIDE, axis=0, tiled=True),
        (((0,), (0,)), ((), ())),
        preferred_element_type=F32,
    )
    buffer = momentum + gradient
    part = jnp.dot(buffer, right_factor, precision=high, preferred_element_type=F32)
    left_factor, gram_matrix = left_and_gram(part)
    inverse = inverse_factor(gram_matrix)
    right_part = lax.dot_general(
        buffer, left_factor, (((0,), (0,)), ((), ())), precision=high, preferred_element_type=F32
    )
    unscaled = right_sum(right_part)
    right_raw, ortho_left, norms = raw_factors(unscaled, left_factor, inverse)
    feedback = lax.dot_general(
        ortho_left.astype(BF16),
        right_raw.astype(BF16),
        (((1,), (1,)), ((), ())),
        preferred_element_type=F32,
    )
    new_momentum = buffer - FEEDBACK * feedback
    new_right = right_raw / norms[:1]
    update_scale = math.sqrt(DOUT * DIN / RANK)
    product = lax.dot_general(
        ortho_left,
        new_right,
        (((1,), (1,)), ((), ())),
        precision=high,
        preferred_element_type=F32,
    )
    update = (update_scale * product).astype(BF16)
    return (new_momentum, new_right, update)


def solution(mesh):
    finer = Mesh(mesh.devices.reshape(4, 4, 4, 2), (X, Z, Y, C))
    in_specs = (P(WIDE, NARROW), P(NARROW, WIDE), P(WIDE, NARROW), P(NARROW, None))
    out_specs = (P(WIDE, NARROW), P(NARROW, None), P(WIDE, NARROW))
    return jax.shard_map(body, mesh=finer, in_specs=in_specs, out_specs=out_specs, check_vma=False)
```

```python
import math

import jax
import jax.numpy as jnp
from jax import lax
from jax.experimental import pallas as pl
from jax.experimental.pallas import tpu as pltpu
from jax.sharding import Mesh
from jax.sharding import PartitionSpec as P

DOUT = 8192
DIN = 16384
RANK = 512
X, Z, Y, C = "wide_0", "wide_1", "narrow_0", "narrow_1"
NARROW = (Y, C)
WIDE = (X, Z)
FEEDBACK = 0.05
EPSILON = 1e-06
F32 = jnp.float32
BF16 = jnp.bfloat16
VMEM = pl.BlockSpec(memory_space=pltpu.VMEM)
MESH = pl.DeviceIdType.MESH

def eliminated(rows):
    lane = lax.broadcasted_iota(jnp.int32, (8, 128), 1)
    sub = lax.broadcasted_iota(jnp.int32, (8, 128), 0)
    groups = len(rows)
    for p in range(groups):
        here = rows[p]
        cols = [jnp.broadcast_to(here[:, 8 * p + k : 8 * p + k + 1], (8, 128)) for k in range(8)]
        a = [[jnp.broadcast_to(cols[k][i : i + 1, :], (8, 128)) if k <= i else None for k in range(8)] for i in range(8)]
        low = [[None] * 8 for _ in range(8)]
        root = [None] * 8
        for k in range(8):
            root[k] = lax.rsqrt(a[k][k])
            for i in range(k + 1, 8):
                low[i][k] = a[i][k] * root[k]
            for i in range(k + 1, 8):
                for j in range(k + 1, i + 1):
                    a[i][j] = a[i][j] - low[i][k] * low[j][k]
        inside = (lane >= 8 * p) & (lane < 8 * p + 8)
        unit = jnp.where(lane == sub + 8 * p, 1.0, 0.0).astype(F32)
        source = jnp.where(inside, unit, here)
        y = []
        for k in range(8):
            value = jnp.broadcast_to(source[k : k + 1, :], (8, 128))
            for m in range(k):
                value = value - low[k][m] * y[m]
            y.append(value * root[k])
        done = y[0]
        for k in range(1, 8):
            done = jnp.where(sub == k, y[k], done)
        rows[p] = done
        for g in range(p + 1, groups):
            c = []
            total = jnp.where(inside, 0.0, rows[g])
            for k in range(8):
                value = jnp.broadcast_to(rows[g][:, 8 * p + k : 8 * p + k + 1], (8, 128))
                for m in range(k):
                    value = value - low[k][m] * c[m]
                c.append(value * root[k])
                total = total - c[k] * y[k]
            rows[g] = total
    return rows

def factor_kernel(c_ref, out_ref, s_ref):
    hi = lax.Precision.HIGHEST
    s_ref[...] = c_ref[...]
    row = lax.broadcasted_iota(jnp.int32, (128, 128), 0)
    col = lax.broadcasted_iota(jnp.int32, (128, 128), 1)
    for b in range(4):
        o = 128 * b
        rows = [s_ref[o + 8 * g : o + 8 * g + 8, o : o + 128] for g in range(16)]
        inv = jnp.concatenate(eliminated(rows), axis=0)
        inv = jnp.where(row >= col, inv, 0.0)
        s_ref[o : o + 128, o : o + 128] = jnp.where(row == col, 1.0, 0.0).astype(F32)
        y = jnp.dot(inv, s_ref[o : o + 128, :], precision=hi, preferred_element_type=F32)
        s_ref[o : o + 128, :] = y
        if b < 3:
            rest = y[:, o + 128 :]
            s_ref[o + 128 :, o : o + 128] = jnp.zeros((384 - o, 128), F32)
            s_ref[o + 128 :, :] = s_ref[o + 128 :, :] - lax.dot_general(
                rest, y, (((0,), (0,)), ((), ())), precision=hi, preferred_element_type=F32)
    row = lax.broadcasted_iota(jnp.int32, (512, 512), 0)
    col = lax.broadcasted_iota(jnp.int32, (512, 512), 1)
    out_ref[...] = jnp.where(row >= col, s_ref[...], 0.0)

def inverse_factor(c):
    return pl.pallas_call(factor_kernel, out_shape=jax.ShapeDtypeStruct((512,512),F32),
        in_specs=[pl.BlockSpec(memory_space=pltpu.VMEM)], out_specs=pl.BlockSpec(memory_space=pltpu.VMEM),
        scratch_shapes=[pltpu.VMEM((512,512),F32)],
        compiler_params=pltpu.CompilerParams(vmem_limit_bytes=32<<20))(c)


def halves(value):
    high = value.astype(BF16)
    return high, (value - high.astype(F32)).astype(BF16)


def one(left, right, dims=((1,), (0,))):
    return lax.dot_general(left, right, (dims, ((), ())), preferred_element_type=F32)


def dot3(left, right, dims=((1,), (0,))):
    a, b = halves(left)
    c, d = halves(right)
    return one(a, c, dims) + (one(a, d, dims) + one(b, c, dims))


def partner(axis, step):
    size = 2 if axis == C else 4
    return lax.rem(lax.axis_index(axis) + step, size)


def line_peers(axes):
    peers = []
    for axis in axes:
        for step in range(1, 2 if axis == C else 4):
            peers.append({axis: partner(axis, step)})
    return peers


def hail(peer):
    pl.semaphore_signal(
        pltpu.get_barrier_semaphore(), inc=1, device_id=peer, device_id_type=MESH
    )


def greet(peers):
    for peer in peers:
        hail(peer)
    pl.semaphore_wait(pltpu.get_barrier_semaphore(), len(peers))


def sent(send, recv, phase, axis, source, target):
    copies = []
    for step in range(1, 2 if axis == C else 4):
        to = partner(axis, step)
        copy = pltpu.make_async_remote_copy(
            src_ref=source(to),
            dst_ref=target(to),
            send_sem=send.at[phase, step - 1],
            recv_sem=recv.at[phase, step - 1],
            device_id={axis: to},
            device_id_type=MESH,
        )
        copy.start()
        copies.append(copy)
    return copies


def all_of(copies):
    for copy in copies:
        copy.wait()


def sum4(ref):
    return (ref[0] + ref[1]) + (ref[2] + ref[3])


def chain_kernel(
    a_ref, g_ref, m_ref, q_ref,
    wt, left, gram,
    q_hi, q_lo, z_part, z_pair, z_half, z_seen, z_own, z_all,
    part, pair, half, share,
    block, gx, gz,
    v_part, v_x, v_z, v_sx, v_sz, v_ex, v_ez, v_own, v_all,
    send, recv, z_send, z_recv, v_send, v_recv,
):
    x, z, y, c = (lax.axis_index(a) for a in (X, Z, Y, C))
    z_self = (x == y) & (lax.div(z, 2) == c)
    v_self = (x == y) & (z == 2 * c + lax.div(x, 2))
    barrier = pltpu.get_barrier_semaphore()

    def apart(first, alone, there, here):
        if not first:
            there()
            return
        pl.when(jnp.logical_not(alone))(there)
        pl.when(alone)(here)

    def z_sources(act):
        for dz in range(2):
            for dy in range(4):
                for dc in range(2):
                    act(dz == dy == dc == 0, lax.rem(z + dz, 2), partner(C, dc), partner(Y, dy))

    def v_sources(act):
        for dx in range(2):
            for dz in range(4):
                act(dx == dz == 0, lax.rem(x + dx, 2), partner(Z, dz))

    for peer in line_peers((X, Z, Y, C)):
        hail(peer)

    def nothing():
        pass

    z_sources(
        lambda first, zz, cc, yy: apart(
            first, z_self, lambda: hail({X: y, Z: 2 * c + zz, Y: yy, C: cc}), nothing
        )
    )
    v_sources(
        lambda first, xx, zz: apart(
            first,
            v_self,
            lambda: hail({X: 2 * lax.rem(z, 2) + xx, Z: zz, Y: x, C: lax.div(z, 2)}),
            nothing,
        )
    )

    @pl.loop(0, 4)
    def _(i):
        rows = pl.ds(pl.multiple_of(512 * i, 512), 512)
        q_hi[rows, :], q_lo[rows, :] = halves(q_ref[rows, :])

    z_part[...] = (one(a_ref[...], q_hi[...]) + one(a_ref[...], q_lo[...])).reshape(2, 4, 32, RANK)
    pl.semaphore_wait(barrier, 34 - z_self.astype(jnp.int32) - v_self.astype(jnp.int32))
    all_of(sent(send, recv, 0, C, lambda to: z_part.at[to], lambda to: z_pair))
    z_half[...] = z_part[c] + z_pair[...]
    copies = sent(send, recv, 1, Y, lambda to: z_half.at[to], lambda to: z_seen.at[y])
    z_seen[y] = z_half[y]
    all_of(copies)
    z_own[...] = sum4(z_seen)

    def z_copy(dx, dz):
        return pltpu.make_async_remote_copy(
            src_ref=z_own,
            dst_ref=z_all.at[lax.rem(z, 2), c, y],
            send_sem=z_send.at[dx, dz],
            recv_sem=z_recv.at[lax.rem(z, 2), c, y],
            device_id={X: partner(X, dx), Z: partner(Z, dz), Y: x, C: lax.div(z, 2)},
            device_id_type=MESH,
        )

    def z_keep():
        z_all[lax.rem(z, 2), c, y] = z_own[...]

    def z_arrived(first, zz, cc, yy):
        copy = pltpu.make_async_remote_copy(
            src_ref=z_own,
            dst_ref=z_all.at[zz, cc, yy],
            send_sem=z_send.at[0, 0],
            recv_sem=z_recv.at[zz, cc, yy],
            device_id={X: y, Z: 2 * c + zz, Y: yy, C: cc},
            device_id_type=MESH,
        )
        apart(first, z_self, copy.wait_recv, nothing)

    for dx in range(4):
        for dz in range(4):
            apart(dx == dz == 0, z_self, z_copy(dx, dz).start, z_keep)

    @pl.loop(0, 4)
    def _(i):
        rows = pl.ds(pl.multiple_of(128 * i, 128), 128)
        high, low = halves(m_ref[rows, :])
        total = one(high, q_hi[...]) + (one(low, q_hi[...]) + one(high, q_lo[...]))
        part[lax.div(i, 2), pl.ds(2 * lax.rem(i, 2), 2)] = total.reshape(2, 64, RANK)

    z_sources(z_arrived)
    for dx in range(4):
        for dz in range(4):
            apart(dx == dz == 0, z_self, z_copy(dx, dz).wait_send, nothing)
    high, low = halves(z_all[...].reshape(RANK, RANK))
    first = ((0,), (0,))
    gz_product = one(g_ref[...], high, first) + one(g_ref[...], low, first)
    part[...] = part[...] + gz_product.reshape(2, 4, 64, RANK)

    all_of(sent(send, recv, 2, C, lambda to: part.at[to], lambda to: pair))
    half[...] = part[c] + pair[...]
    copies = sent(send, recv, 3, Y, lambda to: half.at[to], lambda to: share.at[y])
    share[y] = half[y]
    all_of(copies)
    left[c, y] = sum4(share)
    all_of(sent(send, recv, 4, Y, lambda to: left.at[c, y], lambda to: left.at[c, y]))
    all_of(sent(send, recv, 5, C, lambda to: left.at[c], lambda to: left.at[c]))
    whole = left[...].reshape(RANK, RANK)
    p_hi, p_lo = halves(whole)

    for index in range(4):
        @pl.when(y == index)
        def _():
            own = whole[:, 128 * index : 128 * index + 128]
            block[...] = dot3(own, whole, first).reshape(2, 4, 16, RANK)
    g = sent(send, recv, 6, X, lambda to: block.at[c, to], lambda to: gx.at[x])
    gx[x] = block[c, x]
    v_part[...] = (one(g_ref[...], p_hi) + one(g_ref[...], p_lo)).reshape(4, 4, 2, 16, RANK)
    va = sent(send, recv, 11, X, lambda to: v_part.at[to, :, 0], lambda to: v_x.at[x])
    vb = sent(send, recv, 12, Z, lambda to: v_part.at[:, to, 1], lambda to: v_z.at[z])
    v_x[x] = v_part[x, :, 0]
    v_z[z] = v_part[:, z, 1]
    all_of(g)
    gz[z] = sum4(gx)
    g = sent(send, recv, 7, Z, lambda to: gz.at[z], lambda to: gz.at[z])
    turned = whole.T
    t_hi, t_lo = halves(turned)
    q_hi[0:RANK, :] = t_hi
    q_lo[0:RANK, :] = t_lo

    def momentum_part(begin, end):
        @pl.loop(begin, end)
        def _(j):
            columns = pl.ds(pl.multiple_of(256 * j, 256), 256)
            high, low = halves(m_ref[:, columns])
            left_hi, left_lo = q_hi[0:RANK, :], q_lo[0:RANK, :]
            total = one(left_hi, high) + (one(left_lo, high) + one(left_hi, low))
            for k in range(2):
                piece = total[:, 128 * k : 128 * k + 128].reshape(2, 256, 128)
                wt[lax.div(j, 2), 2 * lax.rem(j, 2) + k] = piece

    momentum_part(0, 2)
    all_of(va)
    v_sx[...] = sum4(v_x)
    va = sent(send, recv, 13, Z, lambda to: v_sx.at[to], lambda to: v_ez.at[z])
    all_of(vb)
    v_sz[...] = sum4(v_z)
    vb = sent(send, recv, 14, X, lambda to: v_sz.at[to], lambda to: v_ex.at[x])
    v_ez[z] = v_sx[z]
    v_ex[x] = v_sz[x]
    all_of(g)
    gram[y, c, x] = sum4(gz)
    g = sent(send, recv, 8, X, lambda to: gram.at[y, c, x], lambda to: gram.at[y, c, x])
    all_of(va)
    v_own[0] = sum4(v_ez)
    all_of(vb)
    v_own[1] = sum4(v_ex)

    def v_copy(dy, dc):
        return pltpu.make_async_remote_copy(
            src_ref=v_own,
            dst_ref=v_all.at[lax.rem(x, 2), z],
            send_sem=v_send.at[dy, dc],
            recv_sem=v_recv.at[lax.rem(x, 2), z],
            device_id={X: y, Z: 2 * c + lax.div(x, 2), Y: partner(Y, dy), C: partner(C, dc)},
            device_id_type=MESH,
        )

    def v_keep():
        v_all[lax.rem(x, 2), z] = v_own[...]

    def v_arrived(first, xx, zz):
        copy = pltpu.make_async_remote_copy(
            src_ref=v_own,
            dst_ref=v_all.at[xx, zz],
            send_sem=v_send.at[0, 0],
            recv_sem=v_recv.at[xx, zz],
            device_id={X: 2 * lax.rem(z, 2) + xx, Z: zz, Y: x, C: lax.div(z, 2)},
            device_id_type=MESH,
        )
        apart(first, v_self, copy.wait_recv, nothing)

    for dy in range(4):
        for dc in range(2):
            apart(dy == dc == 0, v_self, v_copy(dy, dc).start, v_keep)
    all_of(g)
    g = sent(send, recv, 9, Y, lambda to: gram.at[y, c], lambda to: gram.at[y, c])
    momentum_part(2, 8)
    all_of(g)
    g = sent(send, recv, 10, C, lambda to: gram.at[:, c], lambda to: gram.at[:, c])
    v_sources(v_arrived)
    for dy in range(4):
        for dc in range(2):
            apart(dy == dc == 0, v_self, v_copy(dy, dc).wait_send, nothing)
    t_hi, t_lo = halves(v_all[...].reshape(256, RANK).T)
    q_hi[RANK : 2 * RANK, 0:256] = t_hi
    q_lo[RANK : 2 * RANK, 0:256] = t_lo

    @pl.loop(0, 8)
    def _(j):
        columns = pl.ds(pl.multiple_of(256 * j, 256), 256)
        tokens = a_ref[:, columns]
        high, low = q_hi[RANK : 2 * RANK, 0:256], q_lo[RANK : 2 * RANK, 0:256]
        total = one(high, tokens) + one(low, tokens)
        for k in range(2):
            piece = total[:, 128 * k : 128 * k + 128].reshape(2, 256, 128)
            at = (lax.div(j, 2), 2 * lax.rem(j, 2) + k)
            wt[at] = wt[at] + piece

    all_of(g)


def chain(activations, grad_out, momentum, right_factor):
    shapes = [
        ((2048, RANK), BF16), ((2048, RANK), BF16),
        ((2, 4, 32, RANK), F32), ((4, 32, RANK), F32), ((4, 32, RANK), F32), ((4, 32, RANK), F32),
        ((32, RANK), F32), ((2, 2, 4, 32, RANK), F32),
        ((2, 4, 64, RANK), F32), ((4, 64, RANK), F32), ((4, 64, RANK), F32), ((4, 64, RANK), F32),
        ((2, 4, 16, RANK), F32), ((4, 16, RANK), F32), ((4, 16, RANK), F32),
        ((4, 4, 2, 16, RANK), F32), ((4, 4, 16, RANK), F32), ((4, 4, 16, RANK), F32),
        ((4, 16, RANK), F32), ((4, 16, RANK), F32), ((4, 16, RANK), F32), ((4, 16, RANK), F32),
        ((2, 16, RANK), F32), ((2, 4, 2, 16, RANK), F32),
    ]
    semaphores = [(15, 3), (15, 3), (4, 4), (2, 2, 4), (4, 2), (2, 4)]
    return pl.pallas_call(
        chain_kernel,
        out_shape=(
            jax.ShapeDtypeStruct((4, 4, 2, 256, 128), F32),
            jax.ShapeDtypeStruct((2, 4, 64, RANK), F32),
            jax.ShapeDtypeStruct((4, 2, 4, 16, RANK), F32),
        ),
        in_specs=[VMEM] * 4,
        out_specs=(VMEM,) * 3,
        scratch_shapes=[pltpu.VMEM(*s) for s in shapes]
        + [pltpu.SemaphoreType.DMA(s) for s in semaphores],
        compiler_params=pltpu.CompilerParams(
            collective_id=1, has_side_effects=True, vmem_limit_bytes=48 << 20
        ),
        cost_estimate=pl.CostEstimate(flops=1 << 34, bytes_accessed=128 << 20, transcendentals=0),
    )(activations, grad_out, momentum, right_factor)


def right_kernel(part, out, from_x, from_z, sum_x, sum_z, end_x, end_z, send, recv):
    x, z = lax.axis_index(X), lax.axis_index(Z)
    greet(line_peers((X, Z)))
    a = sent(send, recv, 0, X, lambda to: part.at[to, :, 0], lambda to: from_x.at[x])
    b = sent(send, recv, 1, Z, lambda to: part.at[:, to, 1], lambda to: from_z.at[z])
    from_x[x] = part[x, :, 0]
    from_z[z] = part[:, z, 1]
    all_of(a)
    sum_x[...] = sum4(from_x)
    a = sent(send, recv, 2, Z, lambda to: sum_x.at[to], lambda to: end_z.at[z])
    all_of(b)
    sum_z[...] = sum4(from_z)
    b = sent(send, recv, 3, X, lambda to: sum_z.at[to], lambda to: end_x.at[x])
    end_z[z] = sum_x[z]
    end_x[x] = sum_z[x]
    all_of(a)
    out[x, z, 0] = sum4(end_z)
    a = sent(send, recv, 4, Z, lambda to: out.at[x, z, 0], lambda to: out.at[x, z, 0])
    all_of(b)
    out[x, z, 1] = sum4(end_x)
    b = sent(send, recv, 5, X, lambda to: out.at[x, z, 1], lambda to: out.at[x, z, 1])
    all_of(a)
    a = sent(send, recv, 6, X, lambda to: out.at[x, :, 0], lambda to: out.at[x, :, 0])
    all_of(b)
    b = sent(send, recv, 7, Z, lambda to: out.at[:, z, 1], lambda to: out.at[:, z, 1])
    all_of(a)
    all_of(b)


def right_sum(part):
    return pl.pallas_call(
        right_kernel,
        out_shape=jax.ShapeDtypeStruct((4, 4, 2, 256, 128), F32),
        in_specs=[VMEM],
        out_specs=VMEM,
        scratch_shapes=[pltpu.VMEM((4, 4, 256, 128), F32)] * 2
        + [pltpu.VMEM((4, 256, 128), F32)] * 4
        + [pltpu.SemaphoreType.DMA((8, 3))] * 2,
        compiler_params=pltpu.CompilerParams(
            collective_id=2, has_side_effects=True, vmem_limit_bytes=40 << 20
        ),
        cost_estimate=pl.CostEstimate(flops=1 << 22, bytes_accessed=128 << 20, transcendentals=0),
    )(part)


def raw_kernel(w_ref, p_ref, inv_ref, right_t, left, scale, squares, seen, send, recv):
    y, c = lax.axis_index(Y), lax.axis_index(C)
    for peer in line_peers((Y, C)):
        hail(peer)
    squares[...] = jnp.zeros_like(squares)
    inv_hi, inv_lo = halves(inv_ref[...])

    @pl.loop(0, 8)
    def _(j):
        at = 2 * lax.rem(j, 2)
        pieces = [w_ref[lax.div(j, 2), at + k].reshape(RANK, 128) for k in range(2)]
        high, low = halves(jnp.concatenate(pieces, axis=1))
        total = one(inv_hi, high) + (one(inv_hi, low) + one(inv_lo, high))
        right_t[:, pl.ds(pl.multiple_of(256 * j, 256), 256)] = total
        square = total * total
        squares[...] += square[:, :128] + square[:, 128:]

    ones = jnp.ones((8, 128), F32)
    seen[4 + c] = lax.dot_general(
        ones, squares[...], (((1,), (1,)), ((), ())),
        precision=lax.Precision.HIGHEST, preferred_element_type=F32,
    )
    pl.semaphore_wait(pltpu.get_barrier_semaphore(), 4)
    all_of(sent(send, recv, 0, C, lambda to: seen.at[4 + c], lambda to: seen.at[4 + c]))
    seen[y] = seen[4] + seen[5]
    copies = sent(send, recv, 1, Y, lambda to: seen.at[y], lambda to: seen.at[y])
    left[...] = dot3(p_ref[...].reshape(RANK, RANK), inv_ref[...], ((1,), (1,)))
    all_of(copies)
    scale[...] = jnp.sqrt(sum4(seen)) + EPSILON


def raw_factors(w, p, inv):
    return pl.pallas_call(
        raw_kernel,
        out_shape=(
            jax.ShapeDtypeStruct((RANK, 2048), F32),
            jax.ShapeDtypeStruct((RANK, RANK), F32),
            jax.ShapeDtypeStruct((8, RANK), F32),
        ),
        in_specs=[VMEM] * 3,
        out_specs=(VMEM,) * 3,
        scratch_shapes=[
            pltpu.VMEM((RANK, 128), F32),
            pltpu.VMEM((6, 8, RANK), F32),
            pltpu.SemaphoreType.DMA((2, 3)),
            pltpu.SemaphoreType.DMA((2, 3)),
        ],
        compiler_params=pltpu.CompilerParams(
            collective_id=3, has_side_effects=True, vmem_limit_bytes=40 << 20
        ),
        cost_estimate=pl.CostEstimate(flops=1 << 30, bytes_accessed=16 << 20, transcendentals=0),
    )(w, p, inv)


def final_kernel(b_ref, r_ref, l_ref, n_ref, momentum, right, update):
    norms = n_ref[0:1, :]
    raw = r_ref[...]
    ortho = l_ref[...]
    r_hi, r_lo = halves(raw)
    momentum[...] = b_ref[...] - FEEDBACK * one(ortho.astype(BF16), r_hi)
    s_hi, s_lo = halves(ortho * (math.sqrt(DOUT * DIN / RANK) / norms))
    update[...] = (one(s_hi, r_hi) + (one(s_hi, r_lo) + one(s_lo, r_hi))).astype(BF16)
    right[...] = raw.T / norms


def final(buffer, right_t, left, norms):
    wide = 256
    return pl.pallas_call(
        final_kernel,
        grid=(2048 // wide,),
        in_specs=[
            pl.BlockSpec((RANK, wide), lambda j: (0, j)),
            pl.BlockSpec((RANK, wide), lambda j: (0, j)),
            pl.BlockSpec((RANK, RANK), lambda j: (0, 0)),
            pl.BlockSpec((8, RANK), lambda j: (0, 0)),
        ],
        out_specs=(
            pl.BlockSpec((RANK, wide), lambda j: (0, j)),
            pl.BlockSpec((wide, RANK), lambda j: (j, 0)),
            pl.BlockSpec((RANK, wide), lambda j: (0, j)),
        ),
        out_shape=(
            jax.ShapeDtypeStruct((RANK, 2048), F32),
            jax.ShapeDtypeStruct((2048, RANK), F32),
            jax.ShapeDtypeStruct((RANK, 2048), BF16),
        ),
        compiler_params=pltpu.CompilerParams(vmem_limit_bytes=40 << 20),
        cost_estimate=pl.CostEstimate(flops=1 << 32, bytes_accessed=20 << 20, transcendentals=0),
    )(buffer, right_t, left, norms)


def body(activations, grad_out, momentum, right_factor):
    all_activations = lax.all_gather(activations, WIDE, axis=0, tiled=True)
    all_grads = lax.all_gather(grad_out, NARROW, axis=0, tiled=True)
    part, left_factor, gram_matrix = chain(activations, grad_out, momentum, right_factor)
    inverse = inverse_factor(gram_matrix.reshape(RANK, RANK))
    unscaled = right_sum(part)
    gradient = lax.dot_general(
        all_grads, all_activations, (((0,), (0,)), ((), ())), preferred_element_type=F32
    )
    buffer = momentum + gradient
    right_t, ortho_left, norms = raw_factors(unscaled, left_factor, inverse)
    return final(buffer, right_t, ortho_left, norms)


def solution(mesh):
    finer = Mesh(mesh.devices.reshape(4, 4, 4, 2), (X, Z, Y, C))
    in_specs = (P(WIDE, NARROW), P(NARROW, WIDE), P(WIDE, NARROW), P(NARROW, None))
    out_specs = (P(WIDE, NARROW), P(NARROW, None), P(WIDE, NARROW))
    return jax.shard_map(body, mesh=finer, in_specs=in_specs, out_specs=out_specs, check_vma=False)
```

```python
import math

import jax
import jax.numpy as jnp
from jax import lax
from jax.experimental import pallas as pl
from jax.experimental.pallas import tpu as pltpu
from jax.sharding import Mesh
from jax.sharding import PartitionSpec as P

DOUT = 8192
DIN = 16384
RANK = 512
X, Z, Y, C = "wide_0", "wide_1", "narrow_0", "narrow_1"
NARROW = (Y, C)
WIDE = (X, Z)
FEEDBACK = 0.05
EPSILON = 1e-06
F32 = jnp.float32
BF16 = jnp.bfloat16
VMEM = pl.BlockSpec(memory_space=pltpu.VMEM)
MESH = pl.DeviceIdType.MESH

def eliminated(rows):
    lane = lax.broadcasted_iota(jnp.int32, (8, 128), 1)
    sub = lax.broadcasted_iota(jnp.int32, (8, 128), 0)
    groups = len(rows)
    for p in range(groups):
        here = rows[p]
        cols = [jnp.broadcast_to(here[:, 8 * p + k : 8 * p + k + 1], (8, 128)) for k in range(8)]
        a = [[jnp.broadcast_to(cols[k][i : i + 1, :], (8, 128)) if k <= i else None for k in range(8)] for i in range(8)]
        low = [[None] * 8 for _ in range(8)]
        root = [None] * 8
        for k in range(8):
            root[k] = lax.rsqrt(a[k][k])
            for i in range(k + 1, 8):
                low[i][k] = a[i][k] * root[k]
            for i in range(k + 1, 8):
                for j in range(k + 1, i + 1):
                    a[i][j] = a[i][j] - low[i][k] * low[j][k]
        inside = (lane >= 8 * p) & (lane < 8 * p + 8)
        unit = jnp.where(lane == sub + 8 * p, 1.0, 0.0).astype(F32)
        source = jnp.where(inside, unit, here)
        y = []
        for k in range(8):
            value = jnp.broadcast_to(source[k : k + 1, :], (8, 128))
            for m in range(k):
                value = value - low[k][m] * y[m]
            y.append(value * root[k])
        done = y[0]
        for k in range(1, 8):
            done = jnp.where(sub == k, y[k], done)
        rows[p] = done
        for g in range(p + 1, groups):
            c = []
            total = jnp.where(inside, 0.0, rows[g])
            for k in range(8):
                value = jnp.broadcast_to(rows[g][:, 8 * p + k : 8 * p + k + 1], (8, 128))
                for m in range(k):
                    value = value - low[k][m] * c[m]
                c.append(value * root[k])
                total = total - c[k] * y[k]
            rows[g] = total
    return rows

def factor_kernel(c_ref, out_ref, s_ref):
    hi = lax.Precision.HIGHEST
    s_ref[...] = c_ref[...]
    row = lax.broadcasted_iota(jnp.int32, (128, 128), 0)
    col = lax.broadcasted_iota(jnp.int32, (128, 128), 1)
    for b in range(4):
        o = 128 * b
        rows = [s_ref[o + 8 * g : o + 8 * g + 8, o : o + 128] for g in range(16)]
        inv = jnp.concatenate(eliminated(rows), axis=0)
        inv = jnp.where(row >= col, inv, 0.0)
        s_ref[o : o + 128, o : o + 128] = jnp.where(row == col, 1.0, 0.0).astype(F32)
        y = jnp.dot(inv, s_ref[o : o + 128, :], precision=hi, preferred_element_type=F32)
        s_ref[o : o + 128, :] = y
        if b < 3:
            rest = y[:, o + 128 :]
            s_ref[o + 128 :, o : o + 128] = jnp.zeros((384 - o, 128), F32)
            s_ref[o + 128 :, :] = s_ref[o + 128 :, :] - lax.dot_general(
                rest, y, (((0,), (0,)), ((), ())), precision=hi, preferred_element_type=F32)
    row = lax.broadcasted_iota(jnp.int32, (512, 512), 0)
    col = lax.broadcasted_iota(jnp.int32, (512, 512), 1)
    out_ref[...] = jnp.where(row >= col, s_ref[...], 0.0)

def inverse_factor(c):
    return pl.pallas_call(factor_kernel, out_shape=jax.ShapeDtypeStruct((512,512),F32),
        in_specs=[pl.BlockSpec(memory_space=pltpu.VMEM)], out_specs=pl.BlockSpec(memory_space=pltpu.VMEM),
        scratch_shapes=[pltpu.VMEM((512,512),F32)],
        compiler_params=pltpu.CompilerParams(vmem_limit_bytes=32<<20))(c)


def halves(value):
    high = value.astype(BF16)
    return high, (value - high.astype(F32)).astype(BF16)


def one(left, right, dims=((1,), (0,))):
    return lax.dot_general(left, right, (dims, ((), ())), preferred_element_type=F32)


def dot3(left, right, dims=((1,), (0,))):
    a, b = halves(left)
    c, d = halves(right)
    return one(a, c, dims) + (one(a, d, dims) + one(b, c, dims))


def partner(axis, step):
    size = 2 if axis == C else 4
    return lax.rem(lax.axis_index(axis) + step, size)


def line_peers(axes):
    peers = []
    for axis in axes:
        for step in range(1, 2 if axis == C else 4):
            peers.append({axis: partner(axis, step)})
    return peers


def hail(peer):
    pl.semaphore_signal(
        pltpu.get_barrier_semaphore(), inc=1, device_id=peer, device_id_type=MESH
    )


def greet(peers):
    for peer in peers:
        hail(peer)
    pl.semaphore_wait(pltpu.get_barrier_semaphore(), len(peers))


def sent(send, recv, phase, axis, source, target):
    copies = []
    for step in range(1, 2 if axis == C else 4):
        to = partner(axis, step)
        copy = pltpu.make_async_remote_copy(
            src_ref=source(to),
            dst_ref=target(to),
            send_sem=send.at[phase, step - 1],
            recv_sem=recv.at[phase, step - 1],
            device_id={axis: to},
            device_id_type=MESH,
        )
        copy.start()
        copies.append(copy)
    return copies


def all_of(copies):
    for copy in copies:
        copy.wait()


def sum4(ref):
    return (ref[0] + ref[1]) + (ref[2] + ref[3])


def chain_kernel(
    a_ref, g_ref, m_ref, q_ref,
    wt, left, gram,
    q_hi, q_lo, z_part, z_pair, z_half, z_seen, z_own, z_all,
    part, pair, half, share,
    block, gx, gz,
    v_part, v_x, v_z, v_sx, v_sz, v_ex, v_ez, v_own, v_all,
    send, recv, z_send, z_recv, v_send, v_recv,
):
    x, z, y, c = (lax.axis_index(a) for a in (X, Z, Y, C))
    z_self = (x == y) & (lax.div(z, 2) == c)
    v_self = (x == y) & (z == 2 * c + lax.div(x, 2))
    barrier = pltpu.get_barrier_semaphore()

    def apart(first, alone, there, here):
        if not first:
            there()
            return
        pl.when(jnp.logical_not(alone))(there)
        pl.when(alone)(here)

    def z_sources(act):
        for dz in range(2):
            for dy in range(4):
                for dc in range(2):
                    act(dz == dy == dc == 0, lax.rem(z + dz, 2), partner(C, dc), partner(Y, dy))

    def v_sources(act):
        for dx in range(2):
            for dz in range(4):
                act(dx == dz == 0, lax.rem(x + dx, 2), partner(Z, dz))

    for peer in line_peers((X, Z, Y, C)):
        hail(peer)

    def nothing():
        pass

    z_sources(
        lambda first, zz, cc, yy: apart(
            first, z_self, lambda: hail({X: y, Z: 2 * c + zz, Y: yy, C: cc}), nothing
        )
    )
    v_sources(
        lambda first, xx, zz: apart(
            first,
            v_self,
            lambda: hail({X: 2 * lax.rem(z, 2) + xx, Z: zz, Y: x, C: lax.div(z, 2)}),
            nothing,
        )
    )

    @pl.loop(0, 4)
    def _(i):
        rows = pl.ds(pl.multiple_of(512 * i, 512), 512)
        q_hi[rows, :], q_lo[rows, :] = halves(q_ref[rows, :])

    z_part[...] = (one(a_ref[...], q_hi[...]) + one(a_ref[...], q_lo[...])).reshape(2, 4, 32, RANK)
    pl.semaphore_wait(barrier, 34 - z_self.astype(jnp.int32) - v_self.astype(jnp.int32))
    all_of(sent(send, recv, 0, C, lambda to: z_part.at[to], lambda to: z_pair))
    z_half[...] = z_part[c] + z_pair[...]
    copies = sent(send, recv, 1, Y, lambda to: z_half.at[to], lambda to: z_seen.at[y])
    z_seen[y] = z_half[y]
    all_of(copies)
    z_own[...] = sum4(z_seen)

    def z_copy(dx, dz):
        return pltpu.make_async_remote_copy(
            src_ref=z_own,
            dst_ref=z_all.at[lax.rem(z, 2), c, y],
            send_sem=z_send.at[dx, dz],
            recv_sem=z_recv.at[lax.rem(z, 2), c, y],
            device_id={X: partner(X, dx), Z: partner(Z, dz), Y: x, C: lax.div(z, 2)},
            device_id_type=MESH,
        )

    def z_keep():
        z_all[lax.rem(z, 2), c, y] = z_own[...]

    def z_arrived(first, zz, cc, yy):
        copy = pltpu.make_async_remote_copy(
            src_ref=z_own,
            dst_ref=z_all.at[zz, cc, yy],
            send_sem=z_send.at[0, 0],
            recv_sem=z_recv.at[zz, cc, yy],
            device_id={X: y, Z: 2 * c + zz, Y: yy, C: cc},
            device_id_type=MESH,
        )
        apart(first, z_self, copy.wait_recv, nothing)

    for dx in range(4):
        for dz in range(4):
            apart(dx == dz == 0, z_self, z_copy(dx, dz).start, z_keep)

    @pl.loop(0, 4)
    def _(i):
        rows = pl.ds(pl.multiple_of(128 * i, 128), 128)
        high, low = halves(m_ref[rows, :])
        total = one(high, q_hi[...]) + (one(low, q_hi[...]) + one(high, q_lo[...]))
        part[lax.div(i, 2), pl.ds(2 * lax.rem(i, 2), 2)] = total.reshape(2, 64, RANK)

    z_sources(z_arrived)
    for dx in range(4):
        for dz in range(4):
            apart(dx == dz == 0, z_self, z_copy(dx, dz).wait_send, nothing)
    high, low = halves(z_all[...].reshape(RANK, RANK))
    first = ((0,), (0,))
    gz_product = one(g_ref[...], high, first) + one(g_ref[...], low, first)
    part[...] = part[...] + gz_product.reshape(2, 4, 64, RANK)

    all_of(sent(send, recv, 2, C, lambda to: part.at[to], lambda to: pair))
    half[...] = part[c] + pair[...]
    copies = sent(send, recv, 3, Y, lambda to: half.at[to], lambda to: share.at[y])
    share[y] = half[y]
    all_of(copies)
    left[c, y] = sum4(share)
    all_of(sent(send, recv, 4, Y, lambda to: left.at[c, y], lambda to: left.at[c, y]))
    all_of(sent(send, recv, 5, C, lambda to: left.at[c], lambda to: left.at[c]))
    whole = left[...].reshape(RANK, RANK)
    p_hi, p_lo = halves(whole)

    for index in range(4):
        @pl.when(y == index)
        def _():
            own = whole[:, 128 * index : 128 * index + 128]
            block[...] = dot3(own, whole, first).reshape(2, 4, 16, RANK)
    g = sent(send, recv, 6, X, lambda to: block.at[c, to], lambda to: gx.at[x])
    gx[x] = block[c, x]
    v_part[...] = (one(g_ref[...], p_hi) + one(g_ref[...], p_lo)).reshape(4, 4, 2, 16, RANK)
    va = sent(send, recv, 11, X, lambda to: v_part.at[to, :, 0], lambda to: v_x.at[x])
    vb = sent(send, recv, 12, Z, lambda to: v_part.at[:, to, 1], lambda to: v_z.at[z])
    v_x[x] = v_part[x, :, 0]
    v_z[z] = v_part[:, z, 1]
    all_of(g)
    gz[z] = sum4(gx)
    g = sent(send, recv, 7, Z, lambda to: gz.at[z], lambda to: gz.at[z])
    turned = whole.T
    t_hi, t_lo = halves(turned)
    q_hi[0:RANK, :] = t_hi
    q_lo[0:RANK, :] = t_lo

    def momentum_part(begin, end):
        @pl.loop(begin, end)
        def _(j):
            columns = pl.ds(pl.multiple_of(256 * j, 256), 256)
            high, low = halves(m_ref[:, columns])
            left_hi, left_lo = q_hi[0:RANK, :], q_lo[0:RANK, :]
            total = one(left_hi, high) + (one(left_lo, high) + one(left_hi, low))
            for k in range(2):
                piece = total[:, 128 * k : 128 * k + 128].reshape(2, 256, 128)
                wt[lax.div(j, 2), 2 * lax.rem(j, 2) + k] = piece

    momentum_part(0, 2)
    all_of(va)
    v_sx[...] = sum4(v_x)
    va = sent(send, recv, 13, Z, lambda to: v_sx.at[to], lambda to: v_ez.at[z])
    all_of(vb)
    v_sz[...] = sum4(v_z)
    vb = sent(send, recv, 14, X, lambda to: v_sz.at[to], lambda to: v_ex.at[x])
    v_ez[z] = v_sx[z]
    v_ex[x] = v_sz[x]
    all_of(g)
    gram[y, c, x] = sum4(gz)
    g = sent(send, recv, 8, X, lambda to: gram.at[y, c, x], lambda to: gram.at[y, c, x])
    all_of(va)
    v_own[0] = sum4(v_ez)
    all_of(vb)
    v_own[1] = sum4(v_ex)

    def v_copy(dy, dc):
        return pltpu.make_async_remote_copy(
            src_ref=v_own,
            dst_ref=v_all.at[lax.rem(x, 2), z],
            send_sem=v_send.at[dy, dc],
            recv_sem=v_recv.at[lax.rem(x, 2), z],
            device_id={X: y, Z: 2 * c + lax.div(x, 2), Y: partner(Y, dy), C: partner(C, dc)},
            device_id_type=MESH,
        )

    def v_keep():
        v_all[lax.rem(x, 2), z] = v_own[...]

    def v_arrived(first, xx, zz):
        copy = pltpu.make_async_remote_copy(
            src_ref=v_own,
            dst_ref=v_all.at[xx, zz],
            send_sem=v_send.at[0, 0],
            recv_sem=v_recv.at[xx, zz],
            device_id={X: 2 * lax.rem(z, 2) + xx, Z: zz, Y: x, C: lax.div(z, 2)},
            device_id_type=MESH,
        )
        apart(first, v_self, copy.wait_recv, nothing)

    for dy in range(4):
        for dc in range(2):
            apart(dy == dc == 0, v_self, v_copy(dy, dc).start, v_keep)
    all_of(g)
    g = sent(send, recv, 9, Y, lambda to: gram.at[y, c], lambda to: gram.at[y, c])
    momentum_part(2, 8)
    all_of(g)
    g = sent(send, recv, 10, C, lambda to: gram.at[:, c], lambda to: gram.at[:, c])
    v_sources(v_arrived)
    for dy in range(4):
        for dc in range(2):
            apart(dy == dc == 0, v_self, v_copy(dy, dc).wait_send, nothing)
    t_hi, t_lo = halves(v_all[...].reshape(256, RANK).T)
    q_hi[RANK : 2 * RANK, 0:256] = t_hi
    q_lo[RANK : 2 * RANK, 0:256] = t_lo

    @pl.loop(0, 8)
    def _(j):
        columns = pl.ds(pl.multiple_of(256 * j, 256), 256)
        tokens = a_ref[:, columns]
        high, low = q_hi[RANK : 2 * RANK, 0:256], q_lo[RANK : 2 * RANK, 0:256]
        total = one(high, tokens) + one(low, tokens)
        for k in range(2):
            piece = total[:, 128 * k : 128 * k + 128].reshape(2, 256, 128)
            at = (lax.div(j, 2), 2 * lax.rem(j, 2) + k)
            wt[at] = wt[at] + piece

    all_of(g)


def chain(activations, grad_out, momentum, right_factor):
    shapes = [
        ((2048, RANK), BF16), ((2048, RANK), BF16),
        ((2, 4, 32, RANK), F32), ((4, 32, RANK), F32), ((4, 32, RANK), F32), ((4, 32, RANK), F32),
        ((32, RANK), F32), ((2, 2, 4, 32, RANK), F32),
        ((2, 4, 64, RANK), F32), ((4, 64, RANK), F32), ((4, 64, RANK), F32), ((4, 64, RANK), F32),
        ((2, 4, 16, RANK), F32), ((4, 16, RANK), F32), ((4, 16, RANK), F32),
        ((4, 4, 2, 16, RANK), F32), ((4, 4, 16, RANK), F32), ((4, 4, 16, RANK), F32),
        ((4, 16, RANK), F32), ((4, 16, RANK), F32), ((4, 16, RANK), F32), ((4, 16, RANK), F32),
        ((2, 16, RANK), F32), ((2, 4, 2, 16, RANK), F32),
    ]
    semaphores = [(15, 3), (15, 3), (4, 4), (2, 2, 4), (4, 2), (2, 4)]
    return pl.pallas_call(
        chain_kernel,
        out_shape=(
            jax.ShapeDtypeStruct((4, 4, 2, 256, 128), F32),
            jax.ShapeDtypeStruct((2, 4, 64, RANK), F32),
            jax.ShapeDtypeStruct((4, 2, 4, 16, RANK), F32),
        ),
        in_specs=[VMEM] * 4,
        out_specs=(VMEM,) * 3,
        scratch_shapes=[pltpu.VMEM(*s) for s in shapes]
        + [pltpu.SemaphoreType.DMA(s) for s in semaphores],
        compiler_params=pltpu.CompilerParams(
            collective_id=1, has_side_effects=True, vmem_limit_bytes=48 << 20
        ),
        cost_estimate=pl.CostEstimate(flops=1 << 34, bytes_accessed=128 << 20, transcendentals=0),
    )(activations, grad_out, momentum, right_factor)


def right_kernel(
    part, g_ref, a_all, m_ref, inv_ref, p_ref,
    right_t, left, scale, buffer,
    from_x, from_z, sum_x, sum_z, end_x, end_z, out,
    g_all, g_turned, tokens, squares, seen, send, recv, tile_sem,
):
    x, z, y, c = (lax.axis_index(a) for a in (X, Z, Y, C))

    def tile(j):
        slot = lax.rem(j, 2)
        columns = pl.ds(pl.multiple_of(256 * j, 256), 256)
        return pltpu.make_async_copy(a_all.at[:, columns], tokens.at[slot], tile_sem.at[slot])

    tile(0).start()
    tile(1).start()
    greet(line_peers((X, Z, Y, C)))
    a = sent(send, recv, 0, X, lambda to: part.at[to, :, 0], lambda to: from_x.at[x])
    b = sent(send, recv, 1, Z, lambda to: part.at[:, to, 1], lambda to: from_z.at[z])
    g = sent(send, recv, 8, Y, lambda to: g_ref, lambda to: g_all.at[y, c])
    from_x[x] = part[x, :, 0]
    from_z[z] = part[:, z, 1]
    g_all[y, c] = g_ref[...]
    left[...] = dot3(p_ref[...].reshape(RANK, RANK), inv_ref[...], ((1,), (1,)))
    squares[...] = jnp.zeros_like(squares)
    all_of(a)
    sum_x[...] = sum4(from_x)
    a = sent(send, recv, 2, Z, lambda to: sum_x.at[to], lambda to: end_z.at[z])
    all_of(b)
    sum_z[...] = sum4(from_z)
    b = sent(send, recv, 3, X, lambda to: sum_z.at[to], lambda to: end_x.at[x])
    end_z[z] = sum_x[z]
    end_x[x] = sum_z[x]
    all_of(g)
    g = sent(send, recv, 9, C, lambda to: g_all.at[:, c], lambda to: g_all.at[:, c])
    all_of(a)
    out[x, z, 0] = sum4(end_z)
    a = sent(send, recv, 4, Z, lambda to: out.at[x, z, 0], lambda to: out.at[x, z, 0])
    all_of(b)
    out[x, z, 1] = sum4(end_x)
    b = sent(send, recv, 5, X, lambda to: out.at[x, z, 1], lambda to: out.at[x, z, 1])
    all_of(a)
    a = sent(send, recv, 6, X, lambda to: out.at[x, :, 0], lambda to: out.at[x, :, 0])
    all_of(b)
    b = sent(send, recv, 7, Z, lambda to: out.at[:, z, 1], lambda to: out.at[:, z, 1])
    all_of(g)
    for n in range(8):
        g_turned[:, 512 * n : 512 * n + 512] = g_all[n // 2, n % 2].T

    @pl.loop(0, 8)
    def _(j):
        tile(j).wait()
        columns = pl.ds(pl.multiple_of(256 * j, 256), 256)
        buffer[:, columns] = m_ref[:, columns] + one(g_turned[...], tokens[lax.rem(j, 2)])

        @pl.when(j < 6)
        def _():
            tile(j + 2).start()

    all_of(a)
    all_of(b)
    inv_hi, inv_lo = halves(inv_ref[...])

    @pl.loop(0, 8)
    def _(j):
        at = 2 * lax.rem(j, 2)
        pieces = [out[lax.div(j, 2), at + k].reshape(RANK, 128) for k in range(2)]
        high, low = halves(jnp.concatenate(pieces, axis=1))
        total = one(inv_hi, high) + (one(inv_hi, low) + one(inv_lo, high))
        right_t[:, pl.ds(pl.multiple_of(256 * j, 256), 256)] = total
        square = total * total
        squares[...] += square[:, :128] + square[:, 128:]

    ones = jnp.ones((8, 128), F32)
    seen[4 + c] = lax.dot_general(
        ones, squares[...], (((1,), (1,)), ((), ())),
        precision=lax.Precision.HIGHEST, preferred_element_type=F32,
    )
    all_of(sent(send, recv, 10, C, lambda to: seen.at[4 + c], lambda to: seen.at[4 + c]))
    seen[y] = seen[4] + seen[5]
    all_of(sent(send, recv, 11, Y, lambda to: seen.at[y], lambda to: seen.at[y]))
    scale[...] = jnp.sqrt(sum4(seen)) + EPSILON


def right_factors(part, grad_out, all_activations, momentum, inverse, left):
    return pl.pallas_call(
        right_kernel,
        out_shape=(
            jax.ShapeDtypeStruct((RANK, 2048), F32),
            jax.ShapeDtypeStruct((RANK, RANK), F32),
            jax.ShapeDtypeStruct((8, RANK), F32),
            jax.ShapeDtypeStruct((RANK, 2048), F32),
        ),
        in_specs=[VMEM, VMEM, pl.BlockSpec(memory_space=pl.ANY), VMEM, VMEM, VMEM],
        out_specs=(VMEM,) * 4,
        scratch_shapes=[pltpu.VMEM((4, 4, 256, 128), F32)] * 2
        + [pltpu.VMEM((4, 256, 128), F32)] * 4
        + [
            pltpu.VMEM((4, 4, 2, 256, 128), F32),
            pltpu.VMEM((4, 2, 512, 512), BF16),
            pltpu.VMEM((512, 4096), BF16),
            pltpu.VMEM((2, 4096, 256), BF16),
            pltpu.VMEM((RANK, 128), F32),
            pltpu.VMEM((6, 8, RANK), F32),
            pltpu.SemaphoreType.DMA((12, 3)),
            pltpu.SemaphoreType.DMA((12, 3)),
            pltpu.SemaphoreType.DMA((2,)),
        ],
        compiler_params=pltpu.CompilerParams(
            collective_id=2, has_side_effects=True, vmem_limit_bytes=56 << 20
        ),
        cost_estimate=pl.CostEstimate(flops=1 << 34, bytes_accessed=128 << 20, transcendentals=0),
    )(part, grad_out, all_activations, momentum, inverse, left)


def final_kernel(b_ref, r_ref, l_ref, n_ref, momentum, right, update):
    norms = n_ref[0:1, :]
    raw = r_ref[...]
    ortho = l_ref[...]
    r_hi, r_lo = halves(raw)
    momentum[...] = b_ref[...] - FEEDBACK * one(ortho.astype(BF16), r_hi)
    s_hi, s_lo = halves(ortho * (math.sqrt(DOUT * DIN / RANK) / norms))
    update[...] = (one(s_hi, r_hi) + (one(s_hi, r_lo) + one(s_lo, r_hi))).astype(BF16)
    right[...] = raw.T / norms


def final(buffer, right_t, left, norms):
    wide = 256
    return pl.pallas_call(
        final_kernel,
        grid=(2048 // wide,),
        in_specs=[
            pl.BlockSpec((RANK, wide), lambda j: (0, j)),
            pl.BlockSpec((RANK, wide), lambda j: (0, j)),
            pl.BlockSpec((RANK, RANK), lambda j: (0, 0)),
            pl.BlockSpec((8, RANK), lambda j: (0, 0)),
        ],
        out_specs=(
            pl.BlockSpec((RANK, wide), lambda j: (0, j)),
            pl.BlockSpec((wide, RANK), lambda j: (j, 0)),
            pl.BlockSpec((RANK, wide), lambda j: (0, j)),
        ),
        out_shape=(
            jax.ShapeDtypeStruct((RANK, 2048), F32),
            jax.ShapeDtypeStruct((2048, RANK), F32),
            jax.ShapeDtypeStruct((RANK, 2048), BF16),
        ),
        compiler_params=pltpu.CompilerParams(vmem_limit_bytes=60 << 20),
        cost_estimate=pl.CostEstimate(flops=1 << 32, bytes_accessed=20 << 20, transcendentals=0),
    )(buffer, right_t, left, norms)


def body(activations, grad_out, momentum, right_factor):
    all_activations = lax.all_gather(activations, WIDE, axis=0, tiled=True)
    part, left_factor, gram_matrix = chain(activations, grad_out, momentum, right_factor)
    inverse = inverse_factor(gram_matrix.reshape(RANK, RANK))
    right_t, ortho_left, norms, buffer = right_factors(
        part, grad_out, all_activations, momentum, inverse, left_factor
    )
    return final(buffer, right_t, ortho_left, norms)


def solution(mesh):
    finer = Mesh(mesh.devices.reshape(4, 4, 4, 2), (X, Z, Y, C))
    in_specs = (P(WIDE, NARROW), P(NARROW, WIDE), P(WIDE, NARROW), P(NARROW, None))
    out_specs = (P(WIDE, NARROW), P(NARROW, None), P(WIDE, NARROW))
    return jax.shard_map(body, mesh=finer, in_specs=in_specs, out_specs=out_specs, check_vma=False)
```

```python
import math

import jax
import jax.numpy as jnp
from jax import lax
from jax.experimental import pallas as pl
from jax.experimental.pallas import tpu as pltpu
from jax.sharding import Mesh
from jax.sharding import PartitionSpec as P

DOUT = 8192
DIN = 16384
RANK = 512
X, Z, Y, C = "wide_0", "wide_1", "narrow_0", "narrow_1"
NARROW = (Y, C)
WIDE = (X, Z)
FEEDBACK = 0.05
EPSILON = 1e-06
F32 = jnp.float32
BF16 = jnp.bfloat16
VMEM = pl.BlockSpec(memory_space=pltpu.VMEM)
MESH = pl.DeviceIdType.MESH

def eliminated(rows):
    lane = lax.broadcasted_iota(jnp.int32, (8, 128), 1)
    sub = lax.broadcasted_iota(jnp.int32, (8, 128), 0)
    groups = len(rows)
    for p in range(groups):
        here = rows[p]
        cols = [jnp.broadcast_to(here[:, 8 * p + k : 8 * p + k + 1], (8, 128)) for k in range(8)]
        a = [[jnp.broadcast_to(cols[k][i : i + 1, :], (8, 128)) if k <= i else None for k in range(8)] for i in range(8)]
        low = [[None] * 8 for _ in range(8)]
        root = [None] * 8
        for k in range(8):
            root[k] = lax.rsqrt(a[k][k])
            for i in range(k + 1, 8):
                low[i][k] = a[i][k] * root[k]
            for i in range(k + 1, 8):
                for j in range(k + 1, i + 1):
                    a[i][j] = a[i][j] - low[i][k] * low[j][k]
        inside = (lane >= 8 * p) & (lane < 8 * p + 8)
        unit = jnp.where(lane == sub + 8 * p, 1.0, 0.0).astype(F32)
        source = jnp.where(inside, unit, here)
        y = []
        for k in range(8):
            value = jnp.broadcast_to(source[k : k + 1, :], (8, 128))
            for m in range(k):
                value = value - low[k][m] * y[m]
            y.append(value * root[k])
        done = y[0]
        for k in range(1, 8):
            done = jnp.where(sub == k, y[k], done)
        rows[p] = done
        for g in range(p + 1, groups):
            c = []
            total = jnp.where(inside, 0.0, rows[g])
            for k in range(8):
                value = jnp.broadcast_to(rows[g][:, 8 * p + k : 8 * p + k + 1], (8, 128))
                for m in range(k):
                    value = value - low[k][m] * c[m]
                c.append(value * root[k])
                total = total - c[k] * y[k]
            rows[g] = total
    return rows

def factor_kernel(c_ref, out_ref, s_ref):
    hi = lax.Precision.HIGHEST
    s_ref[...] = c_ref[...]
    row = lax.broadcasted_iota(jnp.int32, (128, 128), 0)
    col = lax.broadcasted_iota(jnp.int32, (128, 128), 1)
    for b in range(4):
        o = 128 * b
        rows = [s_ref[o + 8 * g : o + 8 * g + 8, o : o + 128] for g in range(16)]
        inv = jnp.concatenate(eliminated(rows), axis=0)
        inv = jnp.where(row >= col, inv, 0.0)
        s_ref[o : o + 128, o : o + 128] = jnp.where(row == col, 1.0, 0.0).astype(F32)
        y = jnp.dot(inv, s_ref[o : o + 128, :], precision=hi, preferred_element_type=F32)
        s_ref[o : o + 128, :] = y
        if b < 3:
            rest = y[:, o + 128 :]
            s_ref[o + 128 :, o : o + 128] = jnp.zeros((384 - o, 128), F32)
            s_ref[o + 128 :, :] = s_ref[o + 128 :, :] - lax.dot_general(
                rest, y, (((0,), (0,)), ((), ())), precision=hi, preferred_element_type=F32)
    row = lax.broadcasted_iota(jnp.int32, (512, 512), 0)
    col = lax.broadcasted_iota(jnp.int32, (512, 512), 1)
    out_ref[...] = jnp.where(row >= col, s_ref[...], 0.0)

def inverse_factor(c):
    return pl.pallas_call(factor_kernel, out_shape=jax.ShapeDtypeStruct((512,512),F32),
        in_specs=[pl.BlockSpec(memory_space=pltpu.VMEM)], out_specs=pl.BlockSpec(memory_space=pltpu.VMEM),
        scratch_shapes=[pltpu.VMEM((512,512),F32)],
        compiler_params=pltpu.CompilerParams(vmem_limit_bytes=32<<20))(c)


def halves(value):
    high = value.astype(BF16)
    return high, (value - high.astype(F32)).astype(BF16)


def one(left, right, dims=((1,), (0,))):
    return lax.dot_general(left, right, (dims, ((), ())), preferred_element_type=F32)


def dot3(left, right, dims=((1,), (0,))):
    a, b = halves(left)
    c, d = halves(right)
    return one(a, c, dims) + (one(a, d, dims) + one(b, c, dims))


def partner(axis, step):
    size = 2 if axis == C else 4
    return lax.rem(lax.axis_index(axis) + step, size)


def line_peers(axes):
    peers = []
    for axis in axes:
        for step in range(1, 2 if axis == C else 4):
            peers.append({axis: partner(axis, step)})
    return peers


def hail(peer):
    pl.semaphore_signal(
        pltpu.get_barrier_semaphore(), inc=1, device_id=peer, device_id_type=MESH
    )


def greet(peers):
    for peer in peers:
        hail(peer)
    pl.semaphore_wait(pltpu.get_barrier_semaphore(), len(peers))


def sent(send, recv, phase, axis, source, target):
    copies = []
    for step in range(1, 2 if axis == C else 4):
        to = partner(axis, step)
        copy = pltpu.make_async_remote_copy(
            src_ref=source(to),
            dst_ref=target(to),
            send_sem=send.at[phase, step - 1],
            recv_sem=recv.at[phase, step - 1],
            device_id={axis: to},
            device_id_type=MESH,
        )
        copy.start()
        copies.append(copy)
    return copies


def all_of(copies):
    for copy in copies:
        copy.wait()


def sum4(ref):
    return (ref[0] + ref[1]) + (ref[2] + ref[3])


def chain_kernel(
    a_ref, g_ref, m_ref, q_ref,
    wt, left, gram,
    q_hi, q_lo, g_mine, z_part, z_pair, z_half, z_seen, z_all,
    part, pair, half, share,
    block, gx, gz,
    v_part, v_x, v_z, v_sx, v_sz, v_ex, v_ez, v_all,
    send, recv, g_send, g_recv,
):
    x, z, y, c = (lax.axis_index(a) for a in (X, Z, Y, C))
    first = ((0,), (0,))
    others = [(dy, dc) for dy in range(4) for dc in range(2) if dy or dc]
    greet(line_peers((X, Z)) + [{Y: partner(Y, dy), C: partner(C, dc)} for dy, dc in others])

    deals = []
    mine = pl.ds(2 * (2 * y + c), 2)
    for dy, dc in others:
        to_y, to_c = partner(Y, dy), partner(C, dc)
        deals.append(
            pltpu.make_async_remote_copy(
                src_ref=g_ref.at[:, to_c, to_y],
                dst_ref=g_mine.at[mine],
                send_sem=g_send.at[dy, dc],
                recv_sem=g_recv.at[dy, dc],
                device_id={Y: to_y, C: to_c},
                device_id_type=MESH,
            )
        )
        deals[-1].start()
    g_mine[mine] = g_ref[:, c, y]

    @pl.loop(0, 4)
    def _(i):
        rows = pl.ds(pl.multiple_of(512 * i, 512), 512)
        q_hi[rows, :], q_lo[rows, :] = halves(q_ref[rows, :])

    z_part[...] = (one(a_ref[...], q_hi[...]) + one(a_ref[...], q_lo[...])).reshape(2, 4, 32, RANK)
    all_of(sent(send, recv, 0, C, lambda to: z_part.at[to], lambda to: z_pair))
    z_half[...] = z_part[c] + z_pair[...]
    copies = sent(send, recv, 1, Y, lambda to: z_half.at[to], lambda to: z_seen.at[y])
    z_seen[y] = z_half[y]
    all_of(copies)
    z_all[x, z] = sum4(z_seen).reshape(2, 16, RANK)
    za = sent(send, recv, 15, Z, lambda to: z_all.at[x, z, 0], lambda to: z_all.at[x, z, 0])
    zb = sent(send, recv, 16, X, lambda to: z_all.at[x, z, 1], lambda to: z_all.at[x, z, 1])

    def momentum_left(begin, end):
        @pl.loop(begin, end)
        def _(i):
            rows = pl.ds(pl.multiple_of(128 * i, 128), 128)
            high, low = halves(m_ref[rows, :])
            total = one(high, q_hi[...]) + (one(low, q_hi[...]) + one(high, q_lo[...]))
            part[lax.div(i, 2), pl.ds(2 * lax.rem(i, 2), 2)] = total.reshape(2, 64, RANK)

    momentum_left(0, 1)
    all_of(za)
    za = sent(send, recv, 17, X, lambda to: z_all.at[x, :, 0], lambda to: z_all.at[x, :, 0])
    all_of(zb)
    zb = sent(send, recv, 18, Z, lambda to: z_all.at[:, z, 1], lambda to: z_all.at[:, z, 1])
    momentum_left(1, 4)
    for deal in deals:
        deal.wait()
    all_of(za)
    all_of(zb)
    high, low = halves(z_all[...].reshape(RANK, RANK))
    grads = g_mine[...].reshape(512, 512)
    gz_product = one(grads, high, first) + one(grads, low, first)
    part[...] = part[...] + gz_product.reshape(2, 4, 64, RANK)

    all_of(sent(send, recv, 2, C, lambda to: part.at[to], lambda to: pair))
    half[...] = part[c] + pair[...]
    copies = sent(send, recv, 3, Y, lambda to: half.at[to], lambda to: share.at[y])
    share[y] = half[y]
    all_of(copies)
    left[c, y] = sum4(share)
    all_of(sent(send, recv, 4, Y, lambda to: left.at[c, y], lambda to: left.at[c, y]))
    all_of(sent(send, recv, 5, C, lambda to: left.at[c], lambda to: left.at[c]))
    whole = left[...].reshape(RANK, RANK)
    p_hi, p_lo = halves(whole)

    v_part[...] = (one(grads, p_hi) + one(grads, p_lo)).reshape(4, 4, 2, 16, RANK)
    va = sent(send, recv, 11, X, lambda to: v_part.at[to, :, 0], lambda to: v_x.at[x])
    vb = sent(send, recv, 12, Z, lambda to: v_part.at[:, to, 1], lambda to: v_z.at[z])
    for index in range(4):
        @pl.when(y == index)
        def _():
            own = whole[:, 128 * index : 128 * index + 128]
            block[...] = dot3(own, whole, first).reshape(2, 4, 16, RANK)
    g = sent(send, recv, 6, X, lambda to: block.at[c, to], lambda to: gx.at[x])
    gx[x] = block[c, x]
    v_x[x] = v_part[x, :, 0]
    v_z[z] = v_part[:, z, 1]
    t_hi, t_lo = halves(whole.T)
    q_hi[0:RANK, :] = t_hi
    q_lo[0:RANK, :] = t_lo

    def momentum_right(begin, end):
        @pl.loop(begin, end)
        def _(j):
            columns = pl.ds(pl.multiple_of(256 * j, 256), 256)
            high, low = halves(m_ref[:, columns])
            left_hi, left_lo = q_hi[0:RANK, :], q_lo[0:RANK, :]
            total = one(left_hi, high) + (one(left_lo, high) + one(left_hi, low))
            for k in range(2):
                piece = total[:, 128 * k : 128 * k + 128].reshape(2, 256, 128)
                wt[lax.div(j, 2), 2 * lax.rem(j, 2) + k] = piece

    momentum_right(0, 2)
    all_of(va)
    v_sx[...] = sum4(v_x)
    va = sent(send, recv, 13, Z, lambda to: v_sx.at[to], lambda to: v_ez.at[z])
    all_of(vb)
    v_sz[...] = sum4(v_z)
    vb = sent(send, recv, 14, X, lambda to: v_sz.at[to], lambda to: v_ex.at[x])
    v_ez[z] = v_sx[z]
    v_ex[x] = v_sz[x]
    all_of(g)
    gz[z] = sum4(gx)
    g = sent(send, recv, 7, Z, lambda to: gz.at[z], lambda to: gz.at[z])
    momentum_right(2, 3)
    all_of(va)
    v_all[c, y, 0] = sum4(v_ez)
    all_of(vb)
    v_all[c, y, 1] = sum4(v_ex)
    v = sent(send, recv, 19, Y, lambda to: v_all.at[c, y], lambda to: v_all.at[c, y])
    all_of(g)
    gram[y, c, x] = sum4(gz)
    g = sent(send, recv, 8, X, lambda to: gram.at[y, c, x], lambda to: gram.at[y, c, x])
    momentum_right(3, 5)
    all_of(v)
    v = sent(send, recv, 20, C, lambda to: v_all.at[c], lambda to: v_all.at[c])
    all_of(g)
    g = sent(send, recv, 9, Y, lambda to: gram.at[y, c], lambda to: gram.at[y, c])
    momentum_right(5, 8)
    all_of(v)
    t_hi, t_lo = halves(v_all[...].reshape(256, RANK).T)
    q_hi[RANK : 2 * RANK, 0:256] = t_hi
    q_lo[RANK : 2 * RANK, 0:256] = t_lo
    all_of(g)
    g = sent(send, recv, 10, C, lambda to: gram.at[:, c], lambda to: gram.at[:, c])

    @pl.loop(0, 8)
    def _(j):
        columns = pl.ds(pl.multiple_of(256 * j, 256), 256)
        tokens = a_ref[:, columns]
        high, low = q_hi[RANK : 2 * RANK, 0:256], q_lo[RANK : 2 * RANK, 0:256]
        total = one(high, tokens) + one(low, tokens)
        for k in range(2):
            piece = total[:, 128 * k : 128 * k + 128].reshape(2, 256, 128)
            at = (lax.div(j, 2), 2 * lax.rem(j, 2) + k)
            wt[at] = wt[at] + piece

    all_of(g)


def chain(activations, grad_out, momentum, right_factor):
    shapes = [
        ((2048, RANK), BF16), ((2048, RANK), BF16), ((16, 32, 512), BF16),
        ((2, 4, 32, RANK), F32), ((4, 32, RANK), F32), ((4, 32, RANK), F32), ((4, 32, RANK), F32),
        ((4, 4, 2, 16, RANK), F32),
        ((2, 4, 64, RANK), F32), ((4, 64, RANK), F32), ((4, 64, RANK), F32), ((4, 64, RANK), F32),
        ((2, 4, 16, RANK), F32), ((4, 16, RANK), F32), ((4, 16, RANK), F32),
        ((4, 4, 2, 16, RANK), F32), ((4, 4, 16, RANK), F32), ((4, 4, 16, RANK), F32),
        ((4, 16, RANK), F32), ((4, 16, RANK), F32), ((4, 16, RANK), F32), ((4, 16, RANK), F32),
        ((2, 4, 2, 16, RANK), F32),
    ]
    semaphores = [(21, 3), (21, 3), (4, 2), (4, 2)]
    return pl.pallas_call(
        chain_kernel,
        out_shape=(
            jax.ShapeDtypeStruct((4, 4, 2, 256, 128), F32),
            jax.ShapeDtypeStruct((2, 4, 64, RANK), F32),
            jax.ShapeDtypeStruct((4, 2, 4, 16, RANK), F32),
        ),
        in_specs=[VMEM] * 4,
        out_specs=(VMEM,) * 3,
        scratch_shapes=[pltpu.VMEM(*s) for s in shapes]
        + [pltpu.SemaphoreType.DMA(s) for s in semaphores],
        compiler_params=pltpu.CompilerParams(
            collective_id=1, has_side_effects=True, vmem_limit_bytes=58 << 20
        ),
        cost_estimate=pl.CostEstimate(flops=1 << 34, bytes_accessed=128 << 20, transcendentals=0),
    )(activations, grad_out.reshape(2, 2, 4, 32, 512), momentum, right_factor)


def right_kernel(
    part, g_ref, inv_ref, p_ref,
    right_t, left, scale, g_turned,
    from_x, from_z, sum_x, sum_z, end_x, end_z, out,
    g_all, squares, seen, send, recv,
):
    x, z, y, c = (lax.axis_index(a) for a in (X, Z, Y, C))
    greet(line_peers((X, Z, Y, C)))
    a = sent(send, recv, 0, X, lambda to: part.at[to, :, 0], lambda to: from_x.at[x])
    b = sent(send, recv, 1, Z, lambda to: part.at[:, to, 1], lambda to: from_z.at[z])
    g = sent(send, recv, 8, Y, lambda to: g_ref, lambda to: g_all.at[y, c])
    from_x[x] = part[x, :, 0]
    from_z[z] = part[:, z, 1]
    g_all[y, c] = g_ref[...]
    left[...] = dot3(p_ref[...].reshape(RANK, RANK), inv_ref[...], ((1,), (1,)))
    squares[...] = jnp.zeros_like(squares)
    all_of(a)
    sum_x[...] = sum4(from_x)
    a = sent(send, recv, 2, Z, lambda to: sum_x.at[to], lambda to: end_z.at[z])
    all_of(b)
    sum_z[...] = sum4(from_z)
    b = sent(send, recv, 3, X, lambda to: sum_z.at[to], lambda to: end_x.at[x])
    end_z[z] = sum_x[z]
    end_x[x] = sum_z[x]
    all_of(g)
    g = sent(send, recv, 9, C, lambda to: g_all.at[:, c], lambda to: g_all.at[:, c])
    all_of(a)
    out[x, z, 0] = sum4(end_z)
    a = sent(send, recv, 4, Z, lambda to: out.at[x, z, 0], lambda to: out.at[x, z, 0])
    all_of(b)
    out[x, z, 1] = sum4(end_x)
    b = sent(send, recv, 5, X, lambda to: out.at[x, z, 1], lambda to: out.at[x, z, 1])
    all_of(a)
    a = sent(send, recv, 6, X, lambda to: out.at[x, :, 0], lambda to: out.at[x, :, 0])
    all_of(b)
    b = sent(send, recv, 7, Z, lambda to: out.at[:, z, 1], lambda to: out.at[:, z, 1])
    all_of(g)
    for n in range(8):
        g_turned[:, 512 * n : 512 * n + 512] = g_all[n // 2, n % 2].T
    all_of(a)
    all_of(b)
    inv_hi, inv_lo = halves(inv_ref[...])

    @pl.loop(0, 8)
    def _(j):
        at = 2 * lax.rem(j, 2)
        pieces = [out[lax.div(j, 2), at + k].reshape(RANK, 128) for k in range(2)]
        high, low = halves(jnp.concatenate(pieces, axis=1))
        total = one(inv_hi, high) + (one(inv_hi, low) + one(inv_lo, high))
        right_t[:, pl.ds(pl.multiple_of(256 * j, 256), 256)] = total
        square = total * total
        squares[...] += square[:, :128] + square[:, 128:]

    ones = jnp.ones((8, 128), F32)
    seen[4 + c] = lax.dot_general(
        ones, squares[...], (((1,), (1,)), ((), ())),
        precision=lax.Precision.HIGHEST, preferred_element_type=F32,
    )
    all_of(sent(send, recv, 10, C, lambda to: seen.at[4 + c], lambda to: seen.at[4 + c]))
    seen[y] = seen[4] + seen[5]
    all_of(sent(send, recv, 11, Y, lambda to: seen.at[y], lambda to: seen.at[y]))
    scale[...] = jnp.sqrt(sum4(seen)) + EPSILON


def right_factors(part, grad_out, inverse, left):
    return pl.pallas_call(
        right_kernel,
        out_shape=(
            jax.ShapeDtypeStruct((RANK, 2048), F32),
            jax.ShapeDtypeStruct((RANK, RANK), F32),
            jax.ShapeDtypeStruct((8, RANK), F32),
            jax.ShapeDtypeStruct((512, 4096), BF16),
        ),
        in_specs=[VMEM] * 4,
        out_specs=(VMEM,) * 4,
        scratch_shapes=[pltpu.VMEM((4, 4, 256, 128), F32)] * 2
        + [pltpu.VMEM((4, 256, 128), F32)] * 4
        + [
            pltpu.VMEM((4, 4, 2, 256, 128), F32),
            pltpu.VMEM((4, 2, 512, 512), BF16),
            pltpu.VMEM((RANK, 128), F32),
            pltpu.VMEM((6, 8, RANK), F32),
            pltpu.SemaphoreType.DMA((12, 3)),
            pltpu.SemaphoreType.DMA((12, 3)),
        ],
        compiler_params=pltpu.CompilerParams(
            collective_id=2, has_side_effects=True, vmem_limit_bytes=58 << 20
        ),
        cost_estimate=pl.CostEstimate(flops=1 << 34, bytes_accessed=128 << 20, transcendentals=0),
    )(part, grad_out, inverse, left)


def final_kernel(a_ref, g_ref, m_ref, r_ref, l_ref, n_ref, momentum, right, update, low_ref, s_hi, s_lo):
    norms = n_ref[0:1, :]

    @pl.when(pl.program_id(0) == 0)
    def _():
        ortho = l_ref[...]
        low_ref[...] = (FEEDBACK * ortho).astype(BF16)
        s_hi[...], s_lo[...] = halves(ortho * (math.sqrt(DOUT * DIN / RANK) / norms))

    raw = r_ref[...]
    r_hi, r_lo = halves(raw)
    buffer = m_ref[...] + one(g_ref[...], a_ref[...])
    momentum[...] = buffer - one(low_ref[...], r_hi)
    update[...] = (one(s_hi[...], r_hi) + (one(s_hi[...], r_lo) + one(s_lo[...], r_hi))).astype(BF16)
    right[...] = raw.T / norms


def final(activations, grads, momentum, right_t, left, norms):
    wide = 256
    tile = pl.BlockSpec((RANK, wide), lambda j: (0, j))
    return pl.pallas_call(
        final_kernel,
        grid=(2048 // wide,),
        in_specs=[
            pl.BlockSpec((4096, wide), lambda j: (0, j)),
            pl.BlockSpec((512, 4096), lambda j: (0, 0), pipeline_mode=pl.Buffered(1)),
            tile,
            tile,
            pl.BlockSpec((RANK, RANK), lambda j: (0, 0)),
            pl.BlockSpec((8, RANK), lambda j: (0, 0)),
        ],
        out_specs=(tile, pl.BlockSpec((wide, RANK), lambda j: (j, 0)), tile),
        out_shape=(
            jax.ShapeDtypeStruct((RANK, 2048), F32),
            jax.ShapeDtypeStruct((2048, RANK), F32),
            jax.ShapeDtypeStruct((RANK, 2048), BF16),
        ),
        scratch_shapes=[pltpu.VMEM((RANK, RANK), BF16)] * 3,
        compiler_params=pltpu.CompilerParams(vmem_limit_bytes=60 << 20),
        cost_estimate=pl.CostEstimate(flops=1 << 34, bytes_accessed=40 << 20, transcendentals=0),
    )(activations, grads, momentum, right_t, left, norms)


def body(activations, grad_out, momentum, right_factor):
    all_activations = lax.all_gather(activations, WIDE, axis=0, tiled=True)
    part, left_factor, gram_matrix = chain(activations, grad_out, momentum, right_factor)
    inverse = inverse_factor(gram_matrix.reshape(RANK, RANK))
    right_t, ortho_left, norms, grads = right_factors(part, grad_out, inverse, left_factor)
    return final(all_activations, grads, momentum, right_t, ortho_left, norms)


def solution(mesh):
    finer = Mesh(mesh.devices.reshape(4, 4, 4, 2), (X, Z, Y, C))
    in_specs = (P(WIDE, NARROW), P(NARROW, WIDE), P(WIDE, NARROW), P(NARROW, None))
    out_specs = (P(WIDE, NARROW), P(NARROW, None), P(WIDE, NARROW))
    return jax.shard_map(body, mesh=finer, in_specs=in_specs, out_specs=out_specs, check_vma=False)
```

```python
import math

import jax
import jax.numpy as jnp
from jax import lax
from jax.experimental import pallas as pl
from jax.experimental.pallas import tpu as pltpu
from jax.sharding import Mesh
from jax.sharding import PartitionSpec as P

DOUT = 8192
DIN = 16384
RANK = 512
X, Z, Y, C = "wide_0", "wide_1", "narrow_0", "narrow_1"
NARROW = (Y, C)
WIDE = (X, Z)
FEEDBACK = 0.05
EPSILON = 1e-06
F32 = jnp.float32
BF16 = jnp.bfloat16
VMEM = pl.BlockSpec(memory_space=pltpu.VMEM)
MESH = pl.DeviceIdType.MESH

def eliminated(rows):
    lane = lax.broadcasted_iota(jnp.int32, (8, 128), 1)
    sub = lax.broadcasted_iota(jnp.int32, (8, 128), 0)
    groups = len(rows)
    for p in range(groups):
        here = rows[p]
        cols = [jnp.broadcast_to(here[:, 8 * p + k : 8 * p + k + 1], (8, 128)) for k in range(8)]
        a = [[jnp.broadcast_to(cols[k][i : i + 1, :], (8, 128)) if k <= i else None for k in range(8)] for i in range(8)]
        low = [[None] * 8 for _ in range(8)]
        root = [None] * 8
        for k in range(8):
            root[k] = lax.rsqrt(a[k][k])
            for i in range(k + 1, 8):
                low[i][k] = a[i][k] * root[k]
            for i in range(k + 1, 8):
                for j in range(k + 1, i + 1):
                    a[i][j] = a[i][j] - low[i][k] * low[j][k]
        inside = (lane >= 8 * p) & (lane < 8 * p + 8)
        unit = jnp.where(lane == sub + 8 * p, 1.0, 0.0).astype(F32)
        source = jnp.where(inside, unit, here)
        y = []
        for k in range(8):
            value = jnp.broadcast_to(source[k : k + 1, :], (8, 128))
            for m in range(k):
                value = value - low[k][m] * y[m]
            y.append(value * root[k])
        done = y[0]
        for k in range(1, 8):
            done = jnp.where(sub == k, y[k], done)
        rows[p] = done
        for g in range(p + 1, groups):
            c = []
            total = jnp.where(inside, 0.0, rows[g])
            for k in range(8):
                value = jnp.broadcast_to(rows[g][:, 8 * p + k : 8 * p + k + 1], (8, 128))
                for m in range(k):
                    value = value - low[k][m] * c[m]
                c.append(value * root[k])
                total = total - c[k] * y[k]
            rows[g] = total
    return rows


def inverse_factor(s_ref, out_ref):
    highest = lax.Precision.HIGHEST
    row = lax.broadcasted_iota(jnp.int32, (128, 128), 0)
    col = lax.broadcasted_iota(jnp.int32, (128, 128), 1)
    tall = lax.broadcasted_iota(jnp.int32, (RANK, 128), 0)
    wide = lax.broadcasted_iota(jnp.int32, (128, RANK), 1)

    @pl.loop(0, 4)
    def _(b):
        o = pl.multiple_of(128 * b, 128)
        here = pl.ds(o, 128)
        rows = [s_ref[pl.ds(pl.multiple_of(o + 8 * g, 8), 8), here] for g in range(16)]
        inv = jnp.where(row >= col, jnp.concatenate(eliminated(rows), axis=0), 0.0)
        s_ref[here, here] = jnp.where(row == col, 1.0, 0.0).astype(F32)
        y = jnp.dot(inv, s_ref[here, :], precision=highest, preferred_element_type=F32)
        s_ref[here, :] = y
        s_ref[:, here] = jnp.where(tall >= o + 128, 0.0, s_ref[:, here])
        rest = jnp.where(wide >= o + 128, y, 0.0)
        s_ref[...] = s_ref[...] - lax.dot_general(
            rest, y, (((0,), (0,)), ((), ())), precision=highest, preferred_element_type=F32
        )

    row = lax.broadcasted_iota(jnp.int32, (RANK, RANK), 0)
    col = lax.broadcasted_iota(jnp.int32, (RANK, RANK), 1)
    out_ref[...] = jnp.where(row >= col, s_ref[...], 0.0)


def halves(value):
    high = value.astype(BF16)
    return high, (value - high.astype(F32)).astype(BF16)


def one(left, right, dims=((1,), (0,))):
    return lax.dot_general(left, right, (dims, ((), ())), preferred_element_type=F32)


def dot3(left, right, dims=((1,), (0,))):
    a, b = halves(left)
    c, d = halves(right)
    return one(a, c, dims) + (one(a, d, dims) + one(b, c, dims))


def partner(axis, step):
    size = 2 if axis == C else 4
    return lax.rem(lax.axis_index(axis) + step, size)


def line_peers(axes):
    peers = []
    for axis in axes:
        for step in range(1, 2 if axis == C else 4):
            peers.append({axis: partner(axis, step)})
    return peers


def hail(peer):
    pl.semaphore_signal(
        pltpu.get_barrier_semaphore(), inc=1, device_id=peer, device_id_type=MESH
    )


def greet(peers):
    for peer in peers:
        hail(peer)
    pl.semaphore_wait(pltpu.get_barrier_semaphore(), len(peers))


def sent(send, recv, phase, axis, source, target):
    copies = []
    for step in range(1, 2 if axis == C else 4):
        to = partner(axis, step)
        copy = pltpu.make_async_remote_copy(
            src_ref=source(to),
            dst_ref=target(to),
            send_sem=send.at[phase, step - 1],
            recv_sem=recv.at[phase, step - 1],
            device_id={axis: to},
            device_id_type=MESH,
        )
        copy.start()
        copies.append(copy)
    return copies


def all_of(copies):
    for copy in copies:
        copy.wait()


def sum4(ref):
    return (ref[0] + ref[1]) + (ref[2] + ref[3])


def chain_kernel(
    a_ref, g_ref, m_ref, q_ref,
    wt, left, gram,
    q_hi, q_lo, g_mine, z_part, z_pair, z_half, z_seen, z_all,
    part, pair, half, share,
    block, gx, gz,
    v_part, v_x, v_z, v_sx, v_sz, v_ex, v_ez, v_all,
    send, recv, g_send, g_recv,
):
    x, z, y, c = (lax.axis_index(a) for a in (X, Z, Y, C))
    first = ((0,), (0,))
    others = [(dy, dc) for dy in range(4) for dc in range(2) if dy or dc]
    greet(line_peers((X, Z)) + [{Y: partner(Y, dy), C: partner(C, dc)} for dy, dc in others])

    deals = []
    mine = pl.ds(2 * (2 * y + c), 2)
    for dy, dc in others:
        to_y, to_c = partner(Y, dy), partner(C, dc)
        deals.append(
            pltpu.make_async_remote_copy(
                src_ref=g_ref.at[:, to_c, to_y],
                dst_ref=g_mine.at[mine],
                send_sem=g_send.at[dy, dc],
                recv_sem=g_recv.at[dy, dc],
                device_id={Y: to_y, C: to_c},
                device_id_type=MESH,
            )
        )
        deals[-1].start()
    g_mine[mine] = g_ref[:, c, y]

    @pl.loop(0, 4)
    def _(i):
        rows = pl.ds(pl.multiple_of(512 * i, 512), 512)
        q_hi[rows, :], q_lo[rows, :] = halves(q_ref[rows, :])

    z_part[...] = (one(a_ref[...], q_hi[...]) + one(a_ref[...], q_lo[...])).reshape(2, 4, 32, RANK)
    all_of(sent(send, recv, 0, C, lambda to: z_part.at[to], lambda to: z_pair))
    z_half[...] = z_part[c] + z_pair[...]
    copies = sent(send, recv, 1, Y, lambda to: z_half.at[to], lambda to: z_seen.at[y])
    z_seen[y] = z_half[y]
    all_of(copies)
    z_all[x, z] = sum4(z_seen).reshape(2, 16, RANK)
    za = sent(send, recv, 15, Z, lambda to: z_all.at[x, z, 0], lambda to: z_all.at[x, z, 0])
    zb = sent(send, recv, 16, X, lambda to: z_all.at[x, z, 1], lambda to: z_all.at[x, z, 1])

    def momentum_left(begin, end):
        @pl.loop(begin, end)
        def _(i):
            rows = pl.ds(pl.multiple_of(128 * i, 128), 128)
            high, low = halves(m_ref[rows, :])
            total = one(high, q_hi[...]) + (one(low, q_hi[...]) + one(high, q_lo[...]))
            part[lax.div(i, 2), pl.ds(2 * lax.rem(i, 2), 2)] = total.reshape(2, 64, RANK)

    momentum_left(0, 1)
    all_of(za)
    za = sent(send, recv, 17, X, lambda to: z_all.at[x, :, 0], lambda to: z_all.at[x, :, 0])
    all_of(zb)
    zb = sent(send, recv, 18, Z, lambda to: z_all.at[:, z, 1], lambda to: z_all.at[:, z, 1])
    momentum_left(1, 4)
    for deal in deals:
        deal.wait()
    all_of(za)
    all_of(zb)
    high, low = halves(z_all[...].reshape(RANK, RANK))
    grads = g_mine[...].reshape(512, 512)
    gz_product = one(grads, high, first) + one(grads, low, first)
    part[...] = part[...] + gz_product.reshape(2, 4, 64, RANK)

    all_of(sent(send, recv, 2, C, lambda to: part.at[to], lambda to: pair))
    half[...] = part[c] + pair[...]
    copies = sent(send, recv, 3, Y, lambda to: half.at[to], lambda to: share.at[y])
    share[y] = half[y]
    all_of(copies)
    left[c, y] = sum4(share)
    all_of(sent(send, recv, 4, Y, lambda to: left.at[c, y], lambda to: left.at[c, y]))
    all_of(sent(send, recv, 5, C, lambda to: left.at[c], lambda to: left.at[c]))
    whole = left[...].reshape(RANK, RANK)
    p_hi, p_lo = halves(whole)

    v_part[...] = (one(grads, p_hi) + one(grads, p_lo)).reshape(4, 4, 2, 16, RANK)
    va = sent(send, recv, 11, X, lambda to: v_part.at[to, :, 0], lambda to: v_x.at[x])
    vb = sent(send, recv, 12, Z, lambda to: v_part.at[:, to, 1], lambda to: v_z.at[z])
    for index in range(4):
        @pl.when(y == index)
        def _():
            own = whole[:, 128 * index : 128 * index + 128]
            block[...] = dot3(own, whole, first).reshape(2, 4, 16, RANK)
    g = sent(send, recv, 6, X, lambda to: block.at[c, to], lambda to: gx.at[x])
    gx[x] = block[c, x]
    v_x[x] = v_part[x, :, 0]
    v_z[z] = v_part[:, z, 1]
    t_hi, t_lo = halves(whole.T)
    q_hi[0:RANK, :] = t_hi
    q_lo[0:RANK, :] = t_lo

    def momentum_right(begin, end):
        @pl.loop(begin, end)
        def _(j):
            columns = pl.ds(pl.multiple_of(256 * j, 256), 256)
            high, low = halves(m_ref[:, columns])
            left_hi, left_lo = q_hi[0:RANK, :], q_lo[0:RANK, :]
            total = one(left_hi, high) + (one(left_lo, high) + one(left_hi, low))
            for k in range(2):
                piece = total[:, 128 * k : 128 * k + 128].reshape(2, 256, 128)
                wt[lax.div(j, 2), 2 * lax.rem(j, 2) + k] = piece

    momentum_right(0, 2)
    all_of(va)
    v_sx[...] = sum4(v_x)
    va = sent(send, recv, 13, Z, lambda to: v_sx.at[to], lambda to: v_ez.at[z])
    all_of(vb)
    v_sz[...] = sum4(v_z)
    vb = sent(send, recv, 14, X, lambda to: v_sz.at[to], lambda to: v_ex.at[x])
    v_ez[z] = v_sx[z]
    v_ex[x] = v_sz[x]
    all_of(g)
    gz[z] = sum4(gx)
    g = sent(send, recv, 7, Z, lambda to: gz.at[z], lambda to: gz.at[z])
    momentum_right(2, 3)
    all_of(va)
    v_all[c, y, 0] = sum4(v_ez)
    all_of(vb)
    v_all[c, y, 1] = sum4(v_ex)
    v = sent(send, recv, 19, Y, lambda to: v_all.at[c, y], lambda to: v_all.at[c, y])
    all_of(g)
    gram[y, c, x] = sum4(gz)
    g = sent(send, recv, 8, X, lambda to: gram.at[y, c, x], lambda to: gram.at[y, c, x])
    momentum_right(3, 5)
    all_of(v)
    v = sent(send, recv, 20, C, lambda to: v_all.at[c], lambda to: v_all.at[c])
    all_of(g)
    g = sent(send, recv, 9, Y, lambda to: gram.at[y, c], lambda to: gram.at[y, c])
    momentum_right(5, 8)
    all_of(v)
    t_hi, t_lo = halves(v_all[...].reshape(256, RANK).T)
    q_hi[RANK : 2 * RANK, 0:256] = t_hi
    q_lo[RANK : 2 * RANK, 0:256] = t_lo
    all_of(g)
    g = sent(send, recv, 10, C, lambda to: gram.at[:, c], lambda to: gram.at[:, c])

    @pl.loop(0, 8)
    def _(j):
        columns = pl.ds(pl.multiple_of(256 * j, 256), 256)
        tokens = a_ref[:, columns]
        high, low = q_hi[RANK : 2 * RANK, 0:256], q_lo[RANK : 2 * RANK, 0:256]
        total = one(high, tokens) + one(low, tokens)
        for k in range(2):
            piece = total[:, 128 * k : 128 * k + 128].reshape(2, 256, 128)
            at = (lax.div(j, 2), 2 * lax.rem(j, 2) + k)
            wt[at] = wt[at] + piece

    all_of(g)


def chain(activations, grad_out, momentum, right_factor):
    shapes = [
        ((2048, RANK), BF16), ((2048, RANK), BF16), ((16, 32, 512), BF16),
        ((2, 4, 32, RANK), F32), ((4, 32, RANK), F32), ((4, 32, RANK), F32), ((4, 32, RANK), F32),
        ((4, 4, 2, 16, RANK), F32),
        ((2, 4, 64, RANK), F32), ((4, 64, RANK), F32), ((4, 64, RANK), F32), ((4, 64, RANK), F32),
        ((2, 4, 16, RANK), F32), ((4, 16, RANK), F32), ((4, 16, RANK), F32),
        ((4, 4, 2, 16, RANK), F32), ((4, 4, 16, RANK), F32), ((4, 4, 16, RANK), F32),
        ((4, 16, RANK), F32), ((4, 16, RANK), F32), ((4, 16, RANK), F32), ((4, 16, RANK), F32),
        ((2, 4, 2, 16, RANK), F32),
    ]
    semaphores = [(21, 3), (21, 3), (4, 2), (4, 2)]
    return pl.pallas_call(
        chain_kernel,
        out_shape=(
            jax.ShapeDtypeStruct((4, 4, 2, 256, 128), F32),
            jax.ShapeDtypeStruct((2, 4, 64, RANK), F32),
            jax.ShapeDtypeStruct((4, 2, 4, 16, RANK), F32),
        ),
        in_specs=[VMEM] * 4,
        out_specs=(VMEM,) * 3,
        scratch_shapes=[pltpu.VMEM(*s) for s in shapes]
        + [pltpu.SemaphoreType.DMA(s) for s in semaphores],
        compiler_params=pltpu.CompilerParams(
            collective_id=1, has_side_effects=True, vmem_limit_bytes=58 << 20
        ),
        cost_estimate=pl.CostEstimate(flops=1 << 34, bytes_accessed=128 << 20, transcendentals=0),
    )(activations, grad_out.reshape(2, 2, 4, 32, 512), momentum, right_factor)


def right_kernel(
    part, g_ref, gram_ref, p_ref,
    out, left, scale, g_turned,
    from_x, from_z, sum_x, sum_z, end_x, end_z,
    g_all, factor, inverse, seen, send, recv,
):
    x, z, y, c = (lax.axis_index(a) for a in (X, Z, Y, C))
    greet(line_peers((X, Z, Y, C)))
    a = sent(send, recv, 0, X, lambda to: part.at[to, :, 0], lambda to: from_x.at[x])
    b = sent(send, recv, 1, Z, lambda to: part.at[:, to, 1], lambda to: from_z.at[z])
    g = sent(send, recv, 8, Y, lambda to: g_ref, lambda to: g_all.at[y, c])
    from_x[x] = part[x, :, 0]
    from_z[z] = part[:, z, 1]
    g_all[y, c] = g_ref[...]
    factor[...] = gram_ref[...].reshape(RANK, RANK)
    inverse_factor(factor, inverse)
    inv_hi, inv_lo = halves(inverse[...])
    all_of(a)
    sum_x[...] = sum4(from_x)
    a = sent(send, recv, 2, Z, lambda to: sum_x.at[to], lambda to: end_z.at[z])
    all_of(b)
    sum_z[...] = sum4(from_z)
    b = sent(send, recv, 3, X, lambda to: sum_z.at[to], lambda to: end_x.at[x])
    end_z[z] = sum_x[z]
    end_x[x] = sum_z[x]
    all_of(g)
    g = sent(send, recv, 9, C, lambda to: g_all.at[:, c], lambda to: g_all.at[:, c])
    all_of(a)
    all_of(b)

    high, low = halves(jnp.concatenate([sum4(end_z), sum4(end_x)], axis=0))
    share = one(inv_hi, high) + (one(inv_hi, low) + one(inv_lo, high))
    out[x, z] = share.reshape(2, 256, 128)
    a = sent(send, recv, 4, Z, lambda to: out.at[x, z, 0], lambda to: out.at[x, z, 0])
    b = sent(send, recv, 5, X, lambda to: out.at[x, z, 1], lambda to: out.at[x, z, 1])
    seen[0, c] = lax.dot_general(
        jnp.ones((8, 128), F32), share * share, (((1,), (1,)), ((), ())),
        precision=lax.Precision.HIGHEST, preferred_element_type=F32,
    )
    all_of(sent(send, recv, 10, C, lambda to: seen.at[0, c], lambda to: seen.at[0, c]))
    seen[1, x] = seen[0, 0] + seen[0, 1]
    q = sent(send, recv, 11, X, lambda to: seen.at[1, x], lambda to: seen.at[1, x])
    all_of(a)
    a = sent(send, recv, 6, X, lambda to: out.at[x, :, 0], lambda to: out.at[x, :, 0])
    all_of(b)
    b = sent(send, recv, 7, Z, lambda to: out.at[:, z, 1], lambda to: out.at[:, z, 1])
    all_of(q)
    seen[2, z] = sum4(seen.at[1])
    q = sent(send, recv, 12, Z, lambda to: seen.at[2, z], lambda to: seen.at[2, z])
    left[...] = dot3(p_ref[...].reshape(RANK, RANK), inverse[...], ((1,), (1,)))
    all_of(q)
    seen[3, y] = sum4(seen.at[2])
    q = sent(send, recv, 13, Y, lambda to: seen.at[3, y], lambda to: seen.at[3, y])
    all_of(g)
    for n in range(8):
        g_turned[:, 512 * n : 512 * n + 512] = g_all[n // 2, n % 2].T
    all_of(q)
    scale[...] = jnp.sqrt(sum4(seen.at[3])) + EPSILON
    all_of(a)
    all_of(b)


def right_factors(part, grad_out, gram, left):
    return pl.pallas_call(
        right_kernel,
        out_shape=(
            jax.ShapeDtypeStruct((4, 4, 2, 256, 128), F32),
            jax.ShapeDtypeStruct((RANK, RANK), F32),
            jax.ShapeDtypeStruct((8, RANK), F32),
            jax.ShapeDtypeStruct((512, 4096), BF16),
        ),
        in_specs=[VMEM] * 4,
        out_specs=(VMEM,) * 4,
        scratch_shapes=[pltpu.VMEM((4, 4, 256, 128), F32)] * 2
        + [pltpu.VMEM((4, 256, 128), F32)] * 4
        + [
            pltpu.VMEM((4, 2, 512, 512), BF16),
            pltpu.VMEM((RANK, RANK), F32),
            pltpu.VMEM((RANK, RANK), F32),
            pltpu.VMEM((4, 4, 8, RANK), F32),
            pltpu.SemaphoreType.DMA((14, 3)),
            pltpu.SemaphoreType.DMA((14, 3)),
        ],
        compiler_params=pltpu.CompilerParams(
            collective_id=2, has_side_effects=True, vmem_limit_bytes=58 << 20
        ),
        cost_estimate=pl.CostEstimate(flops=1 << 34, bytes_accessed=128 << 20, transcendentals=0),
    )(part, grad_out, gram, left)


def final_kernel(a_ref, g_ref, m_ref, r_ref, l_ref, n_ref, momentum, right, update, low_ref, s_hi, s_lo):
    norms = n_ref[0:1, :]

    @pl.when(pl.program_id(0) == 0)
    def _():
        ortho = l_ref[...]
        low_ref[...] = (FEEDBACK * ortho).astype(BF16)
        s_hi[...], s_lo[...] = halves(ortho * (math.sqrt(DOUT * DIN / RANK) / norms))

    raw = jnp.concatenate([r_ref[0, k].reshape(RANK, 128) for k in range(2)], axis=1)
    r_hi, r_lo = halves(raw)
    buffer = m_ref[...] + one(g_ref[...], a_ref[...])
    momentum[...] = buffer - one(low_ref[...], r_hi)
    update[...] = (one(s_hi[...], r_hi) + (one(s_hi[...], r_lo) + one(s_lo[...], r_hi))).astype(BF16)
    right[...] = raw.T / norms


def final(activations, grads, momentum, right_t, left, norms):
    wide = 256
    tile = pl.BlockSpec((RANK, wide), lambda j: (0, j))
    return pl.pallas_call(
        final_kernel,
        grid=(2048 // wide,),
        in_specs=[
            pl.BlockSpec((4096, wide), lambda j: (0, j)),
            pl.BlockSpec((512, 4096), lambda j: (0, 0), pipeline_mode=pl.Buffered(1)),
            tile,
            pl.BlockSpec((1, 2, 2, 256, 128), lambda j: (j // 2, j % 2, 0, 0, 0)),
            pl.BlockSpec((RANK, RANK), lambda j: (0, 0)),
            pl.BlockSpec((8, RANK), lambda j: (0, 0)),
        ],
        out_specs=(tile, pl.BlockSpec((wide, RANK), lambda j: (j, 0)), tile),
        out_shape=(
            jax.ShapeDtypeStruct((RANK, 2048), F32),
            jax.ShapeDtypeStruct((2048, RANK), F32),
            jax.ShapeDtypeStruct((RANK, 2048), BF16),
        ),
        scratch_shapes=[pltpu.VMEM((RANK, RANK), BF16)] * 3,
        compiler_params=pltpu.CompilerParams(vmem_limit_bytes=60 << 20),
        cost_estimate=pl.CostEstimate(flops=1 << 34, bytes_accessed=40 << 20, transcendentals=0),
    )(activations, grads, momentum, right_t, left, norms)


def body(activations, grad_out, momentum, right_factor):
    all_activations = lax.all_gather(activations, WIDE, axis=0, tiled=True)
    part, left_factor, gram_matrix = chain(activations, grad_out, momentum, right_factor)
    right_t, ortho_left, norms, grads = right_factors(part, grad_out, gram_matrix, left_factor)
    return final(all_activations, grads, momentum, right_t, ortho_left, norms)


def solution(mesh):
    finer = Mesh(mesh.devices.reshape(4, 4, 4, 2), (X, Z, Y, C))
    in_specs = (P(WIDE, NARROW), P(NARROW, WIDE), P(WIDE, NARROW), P(NARROW, None))
    out_specs = (P(WIDE, NARROW), P(NARROW, None), P(WIDE, NARROW))
    return jax.shard_map(body, mesh=finer, in_specs=in_specs, out_specs=out_specs, check_vma=False)
```

```python
import math

import jax
import jax.numpy as jnp
from jax import lax
from jax.experimental import pallas as pl
from jax.experimental.pallas import tpu as pltpu
from jax.sharding import Mesh
from jax.sharding import PartitionSpec as P

DOUT = 8192
DIN = 16384
RANK = 512
X, Z, Y, C = "wide_0", "wide_1", "narrow_0", "narrow_1"
NARROW = (Y, C)
WIDE = (X, Z)
FEEDBACK = 0.05
EPSILON = 1e-06
F32 = jnp.float32
BF16 = jnp.bfloat16
VMEM = pl.BlockSpec(memory_space=pltpu.VMEM)
MESH = pl.DeviceIdType.MESH

def eliminated(rows):
    lane = lax.broadcasted_iota(jnp.int32, (8, 128), 1)
    sub = lax.broadcasted_iota(jnp.int32, (8, 128), 0)
    groups = len(rows)
    for p in range(groups):
        here = rows[p]
        cols = [jnp.broadcast_to(here[:, 8 * p + k : 8 * p + k + 1], (8, 128)) for k in range(8)]
        a = [[jnp.broadcast_to(cols[k][i : i + 1, :], (8, 128)) if k <= i else None for k in range(8)] for i in range(8)]
        low = [[None] * 8 for _ in range(8)]
        root = [None] * 8
        for k in range(8):
            root[k] = lax.rsqrt(a[k][k])
            for i in range(k + 1, 8):
                low[i][k] = a[i][k] * root[k]
            for i in range(k + 1, 8):
                for j in range(k + 1, i + 1):
                    a[i][j] = a[i][j] - low[i][k] * low[j][k]
        inside = (lane >= 8 * p) & (lane < 8 * p + 8)
        unit = jnp.where(lane == sub + 8 * p, 1.0, 0.0).astype(F32)
        source = jnp.where(inside, unit, here)
        y = []
        for k in range(8):
            value = jnp.broadcast_to(source[k : k + 1, :], (8, 128))
            for m in range(k):
                value = value - low[k][m] * y[m]
            y.append(value * root[k])
        done = y[0]
        for k in range(1, 8):
            done = jnp.where(sub == k, y[k], done)
        rows[p] = done
        for g in range(p + 1, groups):
            c = []
            total = jnp.where(inside, 0.0, rows[g])
            for k in range(8):
                value = jnp.broadcast_to(rows[g][:, 8 * p + k : 8 * p + k + 1], (8, 128))
                for m in range(k):
                    value = value - low[k][m] * c[m]
                c.append(value * root[k])
                total = total - c[k] * y[k]
            rows[g] = total
    return rows


def factored(s_ref, begin, end):
    highest = lax.Precision.HIGHEST
    row = lax.broadcasted_iota(jnp.int32, (128, 128), 0)
    col = lax.broadcasted_iota(jnp.int32, (128, 128), 1)
    tall = lax.broadcasted_iota(jnp.int32, (RANK, 128), 0)
    wide = lax.broadcasted_iota(jnp.int32, (128, RANK), 1)

    @pl.loop(begin, end)
    def _(b):
        o = pl.multiple_of(128 * b, 128)
        here = pl.ds(o, 128)
        rows = [s_ref[pl.ds(pl.multiple_of(o + 8 * g, 8), 8), here] for g in range(16)]
        inv = jnp.where(row >= col, jnp.concatenate(eliminated(rows), axis=0), 0.0)
        s_ref[here, here] = jnp.where(row == col, 1.0, 0.0).astype(F32)
        y = jnp.dot(inv, s_ref[here, :], precision=highest, preferred_element_type=F32)
        s_ref[here, :] = y
        s_ref[:, here] = jnp.where(tall >= o + 128, 0.0, s_ref[:, here])
        rest = jnp.where(wide >= o + 128, y, 0.0)
        s_ref[...] = s_ref[...] - lax.dot_general(
            rest, y, (((0,), (0,)), ((), ())), precision=highest, preferred_element_type=F32
        )


def lower_part(value):
    row = lax.broadcasted_iota(jnp.int32, value.shape, 0)
    col = lax.broadcasted_iota(jnp.int32, value.shape, 1)
    return jnp.where(row >= col, value, 0.0)


def halves(value):
    high = value.astype(BF16)
    return high, (value - high.astype(F32)).astype(BF16)


def one(left, right, dims=((1,), (0,))):
    return lax.dot_general(left, right, (dims, ((), ())), preferred_element_type=F32)


def dot3(left, right, dims=((1,), (0,))):
    a, b = halves(left)
    c, d = halves(right)
    return one(a, c, dims) + (one(a, d, dims) + one(b, c, dims))


def partner(axis, step):
    size = 2 if axis == C else 4
    return lax.rem(lax.axis_index(axis) + step, size)


ANY = pl.BlockSpec(memory_space=pl.ANY)


def line_peers(axes):
    peers = []
    for axis in axes:
        for step in range(1, 2 if axis == C else 4):
            peers.append({axis: partner(axis, step)})
    return peers


def hail(peer):
    pl.semaphore_signal(
        pltpu.get_barrier_semaphore(), inc=1, device_id=peer, device_id_type=MESH
    )


def greet(peers):
    for peer in peers:
        hail(peer)
    pl.semaphore_wait(pltpu.get_barrier_semaphore(), len(peers))


def sent(send, recv, phase, axis, source, target):
    copies = []
    for step in range(1, 2 if axis == C else 4):
        to = partner(axis, step)
        copy = pltpu.make_async_remote_copy(
            src_ref=source(to),
            dst_ref=target(to),
            send_sem=send.at[phase, step - 1],
            recv_sem=recv.at[phase, step - 1],
            device_id={axis: to},
            device_id_type=MESH,
        )
        copy.start()
        copies.append(copy)
    return copies


def all_of(copies):
    for copy in copies:
        copy.wait()


def sum4(ref):
    return (ref[0] + ref[1]) + (ref[2] + ref[3])


def hop(send, recv, phase, axis, step, source, target):
    copy = pltpu.make_async_remote_copy(
        src_ref=source,
        dst_ref=target,
        send_sem=send.at[phase, 0],
        recv_sem=recv.at[phase, 0],
        device_id={axis: partner(axis, step)},
        device_id_type=MESH,
    )
    copy.start()
    return copy


def sum_begun(send, recv, phase, axis, piece, relays, come):
    right, left, far = partner(axis, 1), partner(axis, 3), partner(axis, 2)
    return [
        hop(send, recv, phase, axis, 1, piece(far, 0), relays.at[0]),
        hop(send, recv, phase + 1, axis, 3, piece(far, 1), relays.at[1]),
        hop(send, recv, phase + 2, axis, 1, piece(right, 1), come.at[0, 2:4]),
        hop(send, recv, phase + 3, axis, 3, piece(left, 0), come.at[1, 0:2]),
    ]


def sum_relayed(send, recv, phase, axis, begun, piece, relays, passed, come):
    right, left = partner(axis, 1), partner(axis, 3)
    begun[0].wait()
    passed[0] = relays[0] + piece(right, 0)[...]
    first = hop(send, recv, phase + 4, axis, 1, passed.at[0], come.at[0, 0:2])
    begun[1].wait()
    passed[1] = relays[1] + piece(left, 1)[...]
    return begun[2:] + [first, hop(send, recv, phase + 5, axis, 3, passed.at[1], come.at[1, 2:4])]


def gather_begun(send, recv, phase, axis, piece):
    me = lax.axis_index(axis)
    return [
        hop(send, recv, phase, axis, 1, piece(me), piece(me)),
        hop(send, recv, phase + 1, axis, 3, piece(me), piece(me)),
    ]


def gather_relayed(send, recv, phase, axis, begun, part):
    right, left = partner(axis, 1), partner(axis, 3)
    begun[0].wait()
    first = hop(send, recv, phase + 2, axis, 1, part(left, 0), part(left, 0))
    begun[1].wait()
    return [first, hop(send, recv, phase + 3, axis, 3, part(right, 1), part(right, 1))]


def chain_kernel(
    a_ref, g_ref, m_ref, q_ref,
    solved, ortho, grads_out,
    wt, left, gram, q_hi, q_lo, g_mine, z_part, z_pair, z_half, z_seen, z_all,
    part, pair, half, share,
    block, gx, gz,
    v_part, v_x, v_z, v_sx, v_sz, v_ex, v_ez, v_all,
    relay_x, relay_z, pass_x, pass_z, come_x, come_z, end_x, end_z,
    g_all, g_turned, factor, inverse,
    send, recv, g_send, g_recv, out_sem,
):
    x, z, y, c = (lax.axis_index(a) for a in (X, Z, Y, C))
    first = ((0,), (0,))
    others = [(dy, dc) for dy in range(4) for dc in range(2) if dy or dc]
    greet(line_peers((X, Z)) + [{Y: partner(Y, dy), C: partner(C, dc)} for dy, dc in others])

    deals = []
    mine = pl.ds(2 * (2 * y + c), 2)
    for dy, dc in others:
        to_y, to_c = partner(Y, dy), partner(C, dc)
        deals.append(
            pltpu.make_async_remote_copy(
                src_ref=g_ref.at[:, to_c, to_y],
                dst_ref=g_mine.at[mine],
                send_sem=g_send.at[dy, dc],
                recv_sem=g_recv.at[dy, dc],
                device_id={Y: to_y, C: to_c},
                device_id_type=MESH,
            )
        )
        deals[-1].start()
    g_mine[mine] = g_ref[:, c, y]

    @pl.loop(0, 4)
    def _(i):
        rows = pl.ds(pl.multiple_of(512 * i, 512), 512)
        q_hi[rows, :], q_lo[rows, :] = halves(q_ref[rows, :])

    z_part[...] = (one(a_ref[...], q_hi[...]) + one(a_ref[...], q_lo[...])).reshape(2, 4, 32, RANK)
    all_of(sent(send, recv, 0, C, lambda to: z_part.at[to], lambda to: z_pair))
    z_half[...] = z_part[c] + z_pair[...]
    copies = sent(send, recv, 1, Y, lambda to: z_half.at[to], lambda to: z_seen.at[y])
    z_seen[y] = z_half[y]
    all_of(copies)
    z_all[x, z] = sum4(z_seen).reshape(2, 16, RANK)
    za = sent(send, recv, 15, Z, lambda to: z_all.at[x, z, 0], lambda to: z_all.at[x, z, 0])
    zb = sent(send, recv, 16, X, lambda to: z_all.at[x, z, 1], lambda to: z_all.at[x, z, 1])

    def momentum_left(begin, end):
        @pl.loop(begin, end)
        def _(i):
            rows = pl.ds(pl.multiple_of(128 * i, 128), 128)
            high, low = halves(m_ref[rows, :])
            total = one(high, q_hi[...]) + (one(low, q_hi[...]) + one(high, q_lo[...]))
            part[lax.div(i, 2), pl.ds(2 * lax.rem(i, 2), 2)] = total.reshape(2, 64, RANK)

    momentum_left(0, 1)
    all_of(za)
    za = sent(send, recv, 17, X, lambda to: z_all.at[x, :, 0], lambda to: z_all.at[x, :, 0])
    all_of(zb)
    zb = sent(send, recv, 18, Z, lambda to: z_all.at[:, z, 1], lambda to: z_all.at[:, z, 1])
    momentum_left(1, 4)
    for deal in deals:
        deal.wait()
    all_of(za)
    all_of(zb)
    high, low = halves(z_all[...].reshape(RANK, RANK))
    grads = g_mine[...].reshape(512, 512)
    gz_product = one(grads, high, first) + one(grads, low, first)
    part[...] = part[...] + gz_product.reshape(2, 4, 64, RANK)

    all_of(sent(send, recv, 2, C, lambda to: part.at[to], lambda to: pair))
    half[...] = part[c] + pair[...]
    copies = sent(send, recv, 3, Y, lambda to: half.at[to], lambda to: share.at[y])
    share[y] = half[y]
    all_of(copies)
    left[c, y] = sum4(share)
    all_of(sent(send, recv, 4, Y, lambda to: left.at[c, y], lambda to: left.at[c, y]))
    all_of(sent(send, recv, 5, C, lambda to: left.at[c], lambda to: left.at[c]))
    whole = left[...].reshape(RANK, RANK)
    p_hi, p_lo = halves(whole)

    v_part[...] = (one(grads, p_hi) + one(grads, p_lo)).reshape(4, 4, 2, 16, RANK)
    va = sent(send, recv, 11, X, lambda to: v_part.at[to, :, 0], lambda to: v_x.at[x])
    vb = sent(send, recv, 12, Z, lambda to: v_part.at[:, to, 1], lambda to: v_z.at[z])
    for index in range(4):
        @pl.when(y == index)
        def _():
            own = whole[:, 128 * index : 128 * index + 128]
            block[...] = dot3(own, whole, first).reshape(2, 4, 16, RANK)
    g = sent(send, recv, 6, X, lambda to: block.at[c, to], lambda to: gx.at[x])
    gx[x] = block[c, x]
    v_x[x] = v_part[x, :, 0]
    v_z[z] = v_part[:, z, 1]
    t_hi, t_lo = halves(whole.T)
    q_hi[0:RANK, :] = t_hi
    q_lo[0:RANK, :] = t_lo

    def momentum_right(begin, end):
        @pl.loop(begin, end)
        def _(j):
            columns = pl.ds(pl.multiple_of(256 * j, 256), 256)
            high, low = halves(m_ref[:, columns])
            left_hi, left_lo = q_hi[0:RANK, :], q_lo[0:RANK, :]
            total = one(left_hi, high) + (one(left_lo, high) + one(left_hi, low))
            for k in range(2):
                piece = total[:, 128 * k : 128 * k + 128].reshape(2, 256, 128)
                wt[lax.div(j, 2), 2 * lax.rem(j, 2) + k] = piece

    momentum_right(0, 2)
    all_of(va)
    v_sx[...] = sum4(v_x)
    va = sent(send, recv, 13, Z, lambda to: v_sx.at[to], lambda to: v_ez.at[z])
    all_of(vb)
    v_sz[...] = sum4(v_z)
    vb = sent(send, recv, 14, X, lambda to: v_sz.at[to], lambda to: v_ex.at[x])
    v_ez[z] = v_sx[z]
    v_ex[x] = v_sz[x]
    all_of(g)
    gz[z] = sum4(gx)
    g = sent(send, recv, 7, Z, lambda to: gz.at[z], lambda to: gz.at[z])
    momentum_right(2, 3)
    all_of(va)
    v_all[c, y, 0] = sum4(v_ez)
    all_of(vb)
    v_all[c, y, 1] = sum4(v_ex)
    v = sent(send, recv, 19, Y, lambda to: v_all.at[c, y], lambda to: v_all.at[c, y])
    all_of(g)
    gram[y, c, x] = sum4(gz)
    g = sent(send, recv, 8, X, lambda to: gram.at[y, c, x], lambda to: gram.at[y, c, x])
    momentum_right(3, 5)
    all_of(v)
    v = sent(send, recv, 20, C, lambda to: v_all.at[c], lambda to: v_all.at[c])
    all_of(g)
    g = sent(send, recv, 9, Y, lambda to: gram.at[y, c], lambda to: gram.at[y, c])
    momentum_right(5, 8)
    all_of(v)
    t_hi, t_lo = halves(v_all[...].reshape(256, RANK).T)
    q_hi[RANK : 2 * RANK, 0:256] = t_hi
    q_lo[RANK : 2 * RANK, 0:256] = t_lo
    all_of(g)
    g = sent(send, recv, 10, C, lambda to: gram.at[:, c], lambda to: gram.at[:, c])

    @pl.loop(0, 8)
    def _(j):
        columns = pl.ds(pl.multiple_of(256 * j, 256), 256)
        tokens = a_ref[:, columns]
        high, low = q_hi[RANK : 2 * RANK, 0:256], q_lo[RANK : 2 * RANK, 0:256]
        total = one(high, tokens) + one(low, tokens)
        for k in range(2):
            piece = total[:, 128 * k : 128 * k + 128].reshape(2, 256, 128)
            at = (lax.div(j, 2), 2 * lax.rem(j, 2) + k)
            wt[at] = wt[at] + piece

    def part_x(to, half):
        return wt.at[to, 2 * half : 2 * half + 2, 0]

    def part_z(to, half):
        return wt.at[2 * half : 2 * half + 2, to, 1]

    a = sum_begun(send, recv, 21, X, part_x, relay_x, come_x)
    b = sum_begun(send, recv, 27, Z, part_z, relay_z, come_z)
    all_of(g)
    g = sent(send, recv, 33, Y, lambda to: g_ref, lambda to: g_all.at[y, c])
    g_all[y, c] = g_ref[...]
    factor[...] = gram[...].reshape(RANK, RANK)
    factored(factor, 0, 2)
    a = sum_relayed(send, recv, 21, X, a, part_x, relay_x, pass_x, come_x)
    b = sum_relayed(send, recv, 27, Z, b, part_z, relay_z, pass_z, come_z)
    factored(factor, 2, 4)
    inverse[...] = lower_part(factor[...])
    all_of(a)
    sum_x = wt.at[x, :, 0]
    sum_x[...] = sum_x[...] + (come_x[0] + come_x[1])
    a = sent(send, recv, 34, Z, lambda to: wt.at[x, to, 0], lambda to: end_z.at[z])
    all_of(b)
    sum_z = wt.at[:, z, 1]
    sum_z[...] = sum_z[...] + (come_z[0] + come_z[1])
    b = sent(send, recv, 35, X, lambda to: wt.at[to, z, 1], lambda to: end_x.at[x])
    end_z[z] = wt[x, z, 0]
    end_x[x] = wt[x, z, 1]
    all_of(g)
    g = sent(send, recv, 36, C, lambda to: g_all.at[:, c], lambda to: g_all.at[:, c])
    inv_hi, inv_lo = halves(inverse[...])
    last = ((1,), (1,))
    ortho[...] = one(p_hi, inv_hi, last) + (one(p_hi, inv_lo, last) + one(p_lo, inv_hi, last))
    all_of(g)

    @pl.loop(0, 8)
    def _(n):
        g_turned[n] = g_all[lax.div(n, 2), lax.rem(n, 2)].reshape(512, 512).T

    copy = pltpu.make_async_copy(g_turned, grads_out, out_sem)
    copy.start()
    all_of(a)
    all_of(b)
    high, low = halves(jnp.concatenate([sum4(end_z), sum4(end_x)], axis=0))
    solved[...] = one(inv_hi, high) + (one(inv_hi, low) + one(inv_lo, high))
    copy.wait()


def chain(activations, grad_out, momentum, right_factor):
    big = [((4, 4, 2, 256, 128), F32), ((2, 4, 64, RANK), F32), ((4, 2, 4, 16, RANK), F32)]
    shapes = [
        ((2048, RANK), BF16), ((2048, RANK), BF16), ((16, 32, 512), BF16),
        ((2, 4, 32, RANK), F32), ((4, 32, RANK), F32), ((4, 32, RANK), F32), ((4, 32, RANK), F32),
        ((4, 4, 2, 16, RANK), F32),
        ((2, 4, 64, RANK), F32), ((4, 64, RANK), F32), ((4, 64, RANK), F32), ((4, 64, RANK), F32),
        ((2, 4, 16, RANK), F32), ((4, 16, RANK), F32), ((4, 16, RANK), F32),
        ((4, 4, 2, 16, RANK), F32), ((4, 4, 16, RANK), F32), ((4, 4, 16, RANK), F32),
        ((4, 16, RANK), F32), ((4, 16, RANK), F32), ((4, 16, RANK), F32), ((4, 16, RANK), F32),
        ((2, 4, 2, 16, RANK), F32),
        ((2, 2, 256, 128), F32), ((2, 2, 256, 128), F32),
        ((2, 2, 256, 128), F32), ((2, 2, 256, 128), F32),
        ((2, 4, 256, 128), F32), ((2, 4, 256, 128), F32),
        ((4, 256, 128), F32), ((4, 256, 128), F32),
        ((4, 2, 2, 2, 4, 32, 512), BF16), ((8, 512, 512), BF16),
        ((RANK, RANK), F32), ((RANK, RANK), F32),
    ]
    semaphores = [(37, 3), (37, 3), (4, 2), (4, 2), ()]
    return pl.pallas_call(
        chain_kernel,
        out_shape=(
            jax.ShapeDtypeStruct((RANK, 128), F32),
            jax.ShapeDtypeStruct((RANK, RANK), F32),
            jax.ShapeDtypeStruct((8, 512, 512), BF16),
        ),
        in_specs=[VMEM] * 4,
        out_specs=(VMEM, VMEM, ANY),
        scratch_shapes=[pltpu.VMEM(*s) for s in big + shapes]
        + [pltpu.SemaphoreType.DMA(s) for s in semaphores],
        compiler_params=pltpu.CompilerParams(
            collective_id=1, has_side_effects=True, vmem_limit_bytes=58 << 20
        ),
        cost_estimate=pl.CostEstimate(flops=1 << 34, bytes_accessed=128 << 20, transcendentals=0),
    )(activations, grad_out.reshape(2, 2, 4, 32, 512), momentum, right_factor)


def gather_kernel(
    share, tokens, turned, momentum,
    out, buffer, scale,
    g_all, m_all, slots, sums, seen, send, recv, load_sem, tile_sem, store_sem,
):
    x, z, y, c = (lax.axis_index(a) for a in (X, Z, Y, C))

    def tile(j):
        slot = lax.rem(j, 2)
        columns = pl.ds(pl.multiple_of(256 * j, 256), 256)
        return pltpu.make_async_copy(tokens.at[:, columns], slots.at[slot], tile_sem.at[slot])

    def store(j):
        slot = lax.rem(j, 2)
        columns = pl.ds(pl.multiple_of(256 * j, 256), 256)
        return pltpu.make_async_copy(sums.at[slot], buffer.at[:, columns], store_sem.at[slot])

    loads = [
        pltpu.make_async_copy(turned.at[n], g_all.at[:, 512 * n : 512 * n + 512], load_sem.at[n])
        for n in range(8)
    ]
    loads.append(pltpu.make_async_copy(momentum, m_all, load_sem.at[8]))
    for load in loads:
        load.start()
    tile(0).start()
    tile(1).start()
    greet(line_peers((X, Z, Y, C)))
    own = share[...]
    out[x, z] = own.reshape(2, 256, 128)
    a = sent(send, recv, 0, Z, lambda to: out.at[x, z, 0], lambda to: out.at[x, z, 0])
    b = sent(send, recv, 1, X, lambda to: out.at[x, z, 1], lambda to: out.at[x, z, 1])
    seen[0, c] = lax.dot_general(
        jnp.ones((8, 128), F32), own * own, (((1,), (1,)), ((), ())),
        precision=lax.Precision.HIGHEST, preferred_element_type=F32,
    )
    all_of(sent(send, recv, 2, C, lambda to: seen.at[0, c], lambda to: seen.at[0, c]))
    seen[1, x] = seen[0, 0] + seen[0, 1]
    q = sent(send, recv, 3, X, lambda to: seen.at[1, x], lambda to: seen.at[1, x])
    for load in loads:
        load.wait()
    all_of(q)
    seen[2, z] = sum4(seen.at[1])
    q = sent(send, recv, 4, Z, lambda to: seen.at[2, z], lambda to: seen.at[2, z])
    all_of(a)
    a = gather_begun(send, recv, 6, X, lambda at: out.at[at, :, 0])
    all_of(b)
    b = gather_begun(send, recv, 10, Z, lambda at: out.at[:, at, 1])
    all_of(q)
    seen[3, y] = sum4(seen.at[2])
    q = sent(send, recv, 5, Y, lambda to: seen.at[3, y], lambda to: seen.at[3, y])

    def gradient(begin, end):
        @pl.loop(begin, end)
        def _(j):
            slot = lax.rem(j, 2)
            columns = pl.ds(pl.multiple_of(256 * j, 256), 256)
            tile(j).wait()

            @pl.when(j >= 2)
            def _():
                store(j - 2).wait()

            sums[slot] = m_all[:, columns] + one(g_all[...], slots[slot])
            store(j).start()

            @pl.when(j < 6)
            def _():
                tile(j + 2).start()

    gradient(0, 8)
    a = gather_relayed(send, recv, 6, X, a, lambda at, h: out.at[at, 2 * h : 2 * h + 2, 0])
    b = gather_relayed(send, recv, 10, Z, b, lambda at, h: out.at[2 * h : 2 * h + 2, at, 1])
    all_of(q)
    scale[...] = jnp.sqrt(sum4(seen.at[3])) + EPSILON
    store(6).wait()
    store(7).wait()
    all_of(a)
    all_of(b)


def gathered(share, activations, grads, momentum):
    return pl.pallas_call(
        gather_kernel,
        out_shape=(
            jax.ShapeDtypeStruct((4, 4, 2, 256, 128), F32),
            jax.ShapeDtypeStruct((RANK, 2048), F32),
            jax.ShapeDtypeStruct((8, RANK), F32),
        ),
        in_specs=[VMEM, ANY, ANY, ANY],
        out_specs=(VMEM, ANY, VMEM),
        scratch_shapes=[
            pltpu.VMEM((512, 4096), BF16),
            pltpu.VMEM((RANK, 2048), F32),
            pltpu.VMEM((2, 4096, 256), BF16),
            pltpu.VMEM((2, RANK, 256), F32),
            pltpu.VMEM((4, 4, 8, RANK), F32),
            pltpu.SemaphoreType.DMA((14, 3)),
            pltpu.SemaphoreType.DMA((14, 3)),
            pltpu.SemaphoreType.DMA((9,)),
            pltpu.SemaphoreType.DMA((2,)),
            pltpu.SemaphoreType.DMA((2,)),
        ],
        compiler_params=pltpu.CompilerParams(
            collective_id=2, has_side_effects=True, vmem_limit_bytes=58 << 20
        ),
        cost_estimate=pl.CostEstimate(flops=1 << 34, bytes_accessed=128 << 20, transcendentals=0),
    )(share, activations, grads, momentum)


def final_kernel(b_ref, r_ref, l_ref, n_ref, momentum, right, update, low_ref, s_hi, s_lo, inv_ref):
    @pl.when(pl.program_id(0) == 0)
    def _():
        ortho = l_ref[...]
        inv_ref[...] = 1.0 / n_ref[...]
        low_ref[...] = (FEEDBACK * ortho).astype(BF16)
        s_hi[...], s_lo[...] = halves(ortho * (math.sqrt(DOUT * DIN / RANK) * inv_ref[0:1, :]))

    raw = jnp.concatenate([r_ref[0, k].reshape(RANK, 128) for k in range(2)], axis=1)
    r_hi, r_lo = halves(raw)
    momentum[...] = b_ref[...] - one(low_ref[...], r_hi)
    update[...] = (one(s_hi[...], r_hi) + (one(s_hi[...], r_lo) + one(s_lo[...], r_hi))).astype(BF16)
    right[...] = raw.T * inv_ref[0:1, :]


def final(buffer, right_t, left, norms):
    wide = 256
    tile = pl.BlockSpec((RANK, wide), lambda j: (0, j))
    return pl.pallas_call(
        final_kernel,
        grid=(2048 // wide,),
        in_specs=[
            tile,
            pl.BlockSpec((1, 2, 2, 256, 128), lambda j: (j // 2, j % 2, 0, 0, 0)),
            pl.BlockSpec((RANK, RANK), lambda j: (0, 0)),
            pl.BlockSpec((8, RANK), lambda j: (0, 0)),
        ],
        out_specs=(tile, pl.BlockSpec((wide, RANK), lambda j: (j, 0)), tile),
        out_shape=(
            jax.ShapeDtypeStruct((RANK, 2048), F32),
            jax.ShapeDtypeStruct((2048, RANK), F32),
            jax.ShapeDtypeStruct((RANK, 2048), BF16),
        ),
        scratch_shapes=[pltpu.VMEM((RANK, RANK), BF16)] * 3 + [pltpu.VMEM((8, RANK), F32)],
        compiler_params=pltpu.CompilerParams(vmem_limit_bytes=60 << 20),
        cost_estimate=pl.CostEstimate(flops=1 << 32, bytes_accessed=20 << 20, transcendentals=0),
    )(buffer, right_t, left, norms)


def body(activations, grad_out, momentum, right_factor):
    all_activations = lax.all_gather(activations, WIDE, axis=0, tiled=True)
    share, ortho_left, grads = chain(activations, grad_out, momentum, right_factor)
    right_t, buffer, norms = gathered(share, all_activations, grads, momentum)
    return final(buffer, right_t, ortho_left, norms)


def solution(mesh):
    finer = Mesh(mesh.devices.reshape(4, 4, 4, 2), (X, Z, Y, C))
    in_specs = (P(WIDE, NARROW), P(NARROW, WIDE), P(WIDE, NARROW), P(NARROW, None))
    out_specs = (P(WIDE, NARROW), P(NARROW, None), P(WIDE, NARROW))
    return jax.shard_map(body, mesh=finer, in_specs=in_specs, out_specs=out_specs, check_vma=False)
```

```python
import math

import jax
import jax.numpy as jnp
from jax import lax
from jax.experimental import pallas as pl
from jax.experimental.pallas import tpu as pltpu
from jax.sharding import Mesh
from jax.sharding import PartitionSpec as P

DOUT = 8192
DIN = 16384
RANK = 512
X, Z, Y, C = "wide_0", "wide_1", "narrow_0", "narrow_1"
NARROW = (Y, C)
WIDE = (X, Z)
FEEDBACK = 0.05
EPSILON = 1e-06
F32 = jnp.float32
BF16 = jnp.bfloat16
VMEM = pl.BlockSpec(memory_space=pltpu.VMEM)
MESH = pl.DeviceIdType.MESH

def eliminated(rows):
    lane = lax.broadcasted_iota(jnp.int32, (8, 128), 1)
    sub = lax.broadcasted_iota(jnp.int32, (8, 128), 0)
    groups = len(rows)
    for p in range(groups):
        here = rows[p]
        cols = [jnp.broadcast_to(here[:, 8 * p + k : 8 * p + k + 1], (8, 128)) for k in range(8)]
        a = [[jnp.broadcast_to(cols[k][i : i + 1, :], (8, 128)) if k <= i else None for k in range(8)] for i in range(8)]
        low = [[None] * 8 for _ in range(8)]
        root = [None] * 8
        for k in range(8):
            root[k] = lax.rsqrt(a[k][k])
            for i in range(k + 1, 8):
                low[i][k] = a[i][k] * root[k]
            for i in range(k + 1, 8):
                for j in range(k + 1, i + 1):
                    a[i][j] = a[i][j] - low[i][k] * low[j][k]
        inside = (lane >= 8 * p) & (lane < 8 * p + 8)
        unit = jnp.where(lane == sub + 8 * p, 1.0, 0.0).astype(F32)
        source = jnp.where(inside, unit, here)
        y = []
        for k in range(8):
            value = jnp.broadcast_to(source[k : k + 1, :], (8, 128))
            for m in range(k):
                value = value - low[k][m] * y[m]
            y.append(value * root[k])
        done = y[0]
        for k in range(1, 8):
            done = jnp.where(sub == k, y[k], done)
        rows[p] = done
        for g in range(p + 1, groups):
            c = []
            total = jnp.where(inside, 0.0, rows[g])
            for k in range(8):
                value = jnp.broadcast_to(rows[g][:, 8 * p + k : 8 * p + k + 1], (8, 128))
                for m in range(k):
                    value = value - low[k][m] * c[m]
                c.append(value * root[k])
                total = total - c[k] * y[k]
            rows[g] = total
    return rows


def factored(s_ref, begin, end):
    highest = lax.Precision.HIGHEST
    row = lax.broadcasted_iota(jnp.int32, (128, 128), 0)
    col = lax.broadcasted_iota(jnp.int32, (128, 128), 1)
    tall = lax.broadcasted_iota(jnp.int32, (RANK, 128), 0)
    wide = lax.broadcasted_iota(jnp.int32, (128, RANK), 1)

    @pl.loop(begin, end)
    def _(b):
        o = pl.multiple_of(128 * b, 128)
        here = pl.ds(o, 128)
        rows = [s_ref[pl.ds(pl.multiple_of(o + 8 * g, 8), 8), here] for g in range(16)]
        inv = jnp.where(row >= col, jnp.concatenate(eliminated(rows), axis=0), 0.0)
        s_ref[here, here] = jnp.where(row == col, 1.0, 0.0).astype(F32)
        y = jnp.dot(inv, s_ref[here, :], precision=highest, preferred_element_type=F32)
        s_ref[here, :] = y
        s_ref[:, here] = jnp.where(tall >= o + 128, 0.0, s_ref[:, here])
        rest = jnp.where(wide >= o + 128, y, 0.0)
        s_ref[...] = s_ref[...] - lax.dot_general(
            rest, y, (((0,), (0,)), ((), ())), precision=highest, preferred_element_type=F32
        )


def lower_part(value):
    row = lax.broadcasted_iota(jnp.int32, value.shape, 0)
    col = lax.broadcasted_iota(jnp.int32, value.shape, 1)
    return jnp.where(row >= col, value, 0.0)


def halves(value):
    high = value.astype(BF16)
    return high, (value - high.astype(F32)).astype(BF16)


def one(left, right, dims=((1,), (0,))):
    return lax.dot_general(left, right, (dims, ((), ())), preferred_element_type=F32)


def dot3(left, right, dims=((1,), (0,))):
    a, b = halves(left)
    c, d = halves(right)
    return one(a, c, dims) + (one(a, d, dims) + one(b, c, dims))


def partner(axis, step):
    size = 2 if axis == C else 4
    return lax.rem(lax.axis_index(axis) + step, size)


ANY = pl.BlockSpec(memory_space=pl.ANY)


def line_peers(axes):
    peers = []
    for axis in axes:
        for step in range(1, 2 if axis == C else 4):
            peers.append({axis: partner(axis, step)})
    return peers


def hail(peer):
    pl.semaphore_signal(
        pltpu.get_barrier_semaphore(), inc=1, device_id=peer, device_id_type=MESH
    )


def greet(peers):
    for peer in peers:
        hail(peer)
    pl.semaphore_wait(pltpu.get_barrier_semaphore(), len(peers))


def sent(send, recv, phase, axis, source, target):
    copies = []
    for step in range(1, 2 if axis == C else 4):
        to = partner(axis, step)
        copy = pltpu.make_async_remote_copy(
            src_ref=source(to),
            dst_ref=target(to),
            send_sem=send.at[phase, step - 1],
            recv_sem=recv.at[phase, step - 1],
            device_id={axis: to},
            device_id_type=MESH,
        )
        copy.start()
        copies.append(copy)
    return copies


def all_of(copies):
    for copy in copies:
        copy.wait()


def sum4(ref):
    return (ref[0] + ref[1]) + (ref[2] + ref[3])


def hop(send, recv, phase, axis, step, source, target):
    copy = pltpu.make_async_remote_copy(
        src_ref=source,
        dst_ref=target,
        send_sem=send.at[phase, 0],
        recv_sem=recv.at[phase, 0],
        device_id={axis: partner(axis, step)},
        device_id_type=MESH,
    )
    copy.start()
    return copy


def sum_begun(send, recv, phase, axis, piece, relays, come):
    right, left, far = partner(axis, 1), partner(axis, 3), partner(axis, 2)
    return [
        hop(send, recv, phase, axis, 1, piece(far, 0), relays.at[0]),
        hop(send, recv, phase + 1, axis, 3, piece(far, 1), relays.at[1]),
        hop(send, recv, phase + 2, axis, 1, piece(right, 1), come.at[0, 2:4]),
        hop(send, recv, phase + 3, axis, 3, piece(left, 0), come.at[1, 0:2]),
    ]


def sum_relayed(send, recv, phase, axis, begun, piece, relays, passed, come):
    right, left = partner(axis, 1), partner(axis, 3)
    begun[0].wait()
    passed[0] = relays[0] + piece(right, 0)[...]
    first = hop(send, recv, phase + 4, axis, 1, passed.at[0], come.at[0, 0:2])
    begun[1].wait()
    passed[1] = relays[1] + piece(left, 1)[...]
    return begun[2:] + [first, hop(send, recv, phase + 5, axis, 3, passed.at[1], come.at[1, 2:4])]


def gather_begun(send, recv, phase, axis, piece):
    me = lax.axis_index(axis)
    return [
        hop(send, recv, phase, axis, 1, piece(me), piece(me)),
        hop(send, recv, phase + 1, axis, 3, piece(me), piece(me)),
    ]


def gather_relayed(send, recv, phase, axis, begun, part):
    right, left = partner(axis, 1), partner(axis, 3)
    begun[0].wait()
    first = hop(send, recv, phase + 2, axis, 1, part(left, 0), part(left, 0))
    begun[1].wait()
    return [first, hop(send, recv, phase + 3, axis, 3, part(right, 1), part(right, 1))]


def chain_kernel(
    a_ref, g_ref, m_ref, q_ref,
    out, ortho, grads_out, scale,
    wt, left, gram, q_hi, q_lo, g_mine, z_part, z_pair, z_half, z_seen, z_all,
    part, pair, half, share,
    block, gx, gz,
    v_part, v_x, v_z, v_sx, v_sz, v_ex, v_ez, v_all,
    relay_x, relay_z, pass_x, pass_z, come_x, come_z, end_x, end_z,
    g_all, g_turned, factor, inverse, seen,
    send, recv, g_send, g_recv, out_sem,
):
    x, z, y, c = (lax.axis_index(a) for a in (X, Z, Y, C))
    first = ((0,), (0,))
    others = [(dy, dc) for dy in range(4) for dc in range(2) if dy or dc]
    greet(line_peers((X, Z)) + [{Y: partner(Y, dy), C: partner(C, dc)} for dy, dc in others])

    deals = []
    mine = pl.ds(2 * (2 * y + c), 2)
    for dy, dc in others:
        to_y, to_c = partner(Y, dy), partner(C, dc)
        deals.append(
            pltpu.make_async_remote_copy(
                src_ref=g_ref.at[:, to_c, to_y],
                dst_ref=g_mine.at[mine],
                send_sem=g_send.at[dy, dc],
                recv_sem=g_recv.at[dy, dc],
                device_id={Y: to_y, C: to_c},
                device_id_type=MESH,
            )
        )
        deals[-1].start()
    g_mine[mine] = g_ref[:, c, y]

    @pl.loop(0, 4)
    def _(i):
        rows = pl.ds(pl.multiple_of(512 * i, 512), 512)
        q_hi[rows, :], q_lo[rows, :] = halves(q_ref[rows, :])

    z_part[...] = (one(a_ref[...], q_hi[...]) + one(a_ref[...], q_lo[...])).reshape(2, 4, 32, RANK)
    all_of(sent(send, recv, 0, C, lambda to: z_part.at[to], lambda to: z_pair))
    z_half[...] = z_part[c] + z_pair[...]
    copies = sent(send, recv, 1, Y, lambda to: z_half.at[to], lambda to: z_seen.at[y])
    z_seen[y] = z_half[y]
    all_of(copies)
    z_all[x, z] = sum4(z_seen).reshape(2, 16, RANK)
    za = sent(send, recv, 15, Z, lambda to: z_all.at[x, z, 0], lambda to: z_all.at[x, z, 0])
    zb = sent(send, recv, 16, X, lambda to: z_all.at[x, z, 1], lambda to: z_all.at[x, z, 1])

    def momentum_left(begin, end):
        @pl.loop(begin, end)
        def _(i):
            rows = pl.ds(pl.multiple_of(128 * i, 128), 128)
            high, low = halves(m_ref[rows, :])
            total = one(high, q_hi[...]) + (one(low, q_hi[...]) + one(high, q_lo[...]))
            part[lax.div(i, 2), pl.ds(2 * lax.rem(i, 2), 2)] = total.reshape(2, 64, RANK)

    momentum_left(0, 1)
    all_of(za)
    za = sent(send, recv, 17, X, lambda to: z_all.at[x, :, 0], lambda to: z_all.at[x, :, 0])
    all_of(zb)
    zb = sent(send, recv, 18, Z, lambda to: z_all.at[:, z, 1], lambda to: z_all.at[:, z, 1])
    momentum_left(1, 4)
    for deal in deals:
        deal.wait()
    all_of(za)
    all_of(zb)
    high, low = halves(z_all[...].reshape(RANK, RANK))
    grads = g_mine[...].reshape(512, 512)
    gz_product = one(grads, high, first) + one(grads, low, first)
    part[...] = part[...] + gz_product.reshape(2, 4, 64, RANK)

    all_of(sent(send, recv, 2, C, lambda to: part.at[to], lambda to: pair))
    half[...] = part[c] + pair[...]
    copies = sent(send, recv, 3, Y, lambda to: half.at[to], lambda to: share.at[y])
    share[y] = half[y]
    all_of(copies)
    left[c, y] = sum4(share)
    all_of(sent(send, recv, 4, Y, lambda to: left.at[c, y], lambda to: left.at[c, y]))
    all_of(sent(send, recv, 5, C, lambda to: left.at[c], lambda to: left.at[c]))
    whole = left[...].reshape(RANK, RANK)
    p_hi, p_lo = halves(whole)

    v_part[...] = (one(grads, p_hi) + one(grads, p_lo)).reshape(4, 4, 2, 16, RANK)
    va = sent(send, recv, 11, X, lambda to: v_part.at[to, :, 0], lambda to: v_x.at[x])
    vb = sent(send, recv, 12, Z, lambda to: v_part.at[:, to, 1], lambda to: v_z.at[z])
    for index in range(4):
        @pl.when(y == index)
        def _():
            own = whole[:, 128 * index : 128 * index + 128]
            block[...] = dot3(own, whole, first).reshape(2, 4, 16, RANK)
    g = sent(send, recv, 6, X, lambda to: block.at[c, to], lambda to: gx.at[x])
    gx[x] = block[c, x]
    v_x[x] = v_part[x, :, 0]
    v_z[z] = v_part[:, z, 1]
    t_hi, t_lo = halves(whole.T)
    q_hi[0:RANK, :] = t_hi
    q_lo[0:RANK, :] = t_lo

    def momentum_right(begin, end):
        @pl.loop(begin, end)
        def _(j):
            columns = pl.ds(pl.multiple_of(256 * j, 256), 256)
            high, low = halves(m_ref[:, columns])
            left_hi, left_lo = q_hi[0:RANK, :], q_lo[0:RANK, :]
            total = one(left_hi, high) + (one(left_lo, high) + one(left_hi, low))
            for k in range(2):
                piece = total[:, 128 * k : 128 * k + 128].reshape(2, 256, 128)
                wt[lax.div(j, 2), 2 * lax.rem(j, 2) + k] = piece

    momentum_right(0, 2)
    all_of(va)
    v_sx[...] = sum4(v_x)
    va = sent(send, recv, 13, Z, lambda to: v_sx.at[to], lambda to: v_ez.at[z])
    all_of(vb)
    v_sz[...] = sum4(v_z)
    vb = sent(send, recv, 14, X, lambda to: v_sz.at[to], lambda to: v_ex.at[x])
    v_ez[z] = v_sx[z]
    v_ex[x] = v_sz[x]
    all_of(g)
    gz[z] = sum4(gx)
    g = sent(send, recv, 7, Z, lambda to: gz.at[z], lambda to: gz.at[z])
    momentum_right(2, 3)
    all_of(va)
    v_all[c, y, 0] = sum4(v_ez)
    all_of(vb)
    v_all[c, y, 1] = sum4(v_ex)
    v = sent(send, recv, 19, Y, lambda to: v_all.at[c, y], lambda to: v_all.at[c, y])
    all_of(g)
    gram[y, c, x] = sum4(gz)
    g = sent(send, recv, 8, X, lambda to: gram.at[y, c, x], lambda to: gram.at[y, c, x])
    momentum_right(3, 5)
    all_of(v)
    v = sent(send, recv, 20, C, lambda to: v_all.at[c], lambda to: v_all.at[c])
    all_of(g)
    g = sent(send, recv, 9, Y, lambda to: gram.at[y, c], lambda to: gram.at[y, c])
    momentum_right(5, 8)
    all_of(v)
    t_hi, t_lo = halves(v_all[...].reshape(256, RANK).T)
    q_hi[RANK : 2 * RANK, 0:256] = t_hi
    q_lo[RANK : 2 * RANK, 0:256] = t_lo
    all_of(g)
    g = sent(send, recv, 10, C, lambda to: gram.at[:, c], lambda to: gram.at[:, c])

    @pl.loop(0, 8)
    def _(j):
        columns = pl.ds(pl.multiple_of(256 * j, 256), 256)
        tokens = a_ref[:, columns]
        high, low = q_hi[RANK : 2 * RANK, 0:256], q_lo[RANK : 2 * RANK, 0:256]
        total = one(high, tokens) + one(low, tokens)
        for k in range(2):
            piece = total[:, 128 * k : 128 * k + 128].reshape(2, 256, 128)
            at = (lax.div(j, 2), 2 * lax.rem(j, 2) + k)
            wt[at] = wt[at] + piece

    def part_x(to, half):
        return wt.at[to, 2 * half : 2 * half + 2, 0]

    def part_z(to, half):
        return wt.at[2 * half : 2 * half + 2, to, 1]

    a = sum_begun(send, recv, 21, X, part_x, relay_x, come_x)
    b = sum_begun(send, recv, 27, Z, part_z, relay_z, come_z)
    all_of(g)
    g = sent(send, recv, 33, Y, lambda to: g_ref, lambda to: g_all.at[y, c])
    g_all[y, c] = g_ref[...]
    factor[...] = gram[...].reshape(RANK, RANK)
    factored(factor, 0, 2)
    a = sum_relayed(send, recv, 21, X, a, part_x, relay_x, pass_x, come_x)
    b = sum_relayed(send, recv, 27, Z, b, part_z, relay_z, pass_z, come_z)
    factored(factor, 2, 4)
    inverse[...] = lower_part(factor[...])
    all_of(a)
    sum_x = wt.at[x, :, 0]
    sum_x[...] = sum_x[...] + (come_x[0] + come_x[1])
    a = sent(send, recv, 34, Z, lambda to: wt.at[x, to, 0], lambda to: end_z.at[z])
    all_of(b)
    sum_z = wt.at[:, z, 1]
    sum_z[...] = sum_z[...] + (come_z[0] + come_z[1])
    b = sent(send, recv, 35, X, lambda to: wt.at[to, z, 1], lambda to: end_x.at[x])
    end_z[z] = wt[x, z, 0]
    end_x[x] = wt[x, z, 1]
    all_of(g)
    g = sent(send, recv, 36, C, lambda to: g_all.at[:, c], lambda to: g_all.at[:, c])
    inv_hi, inv_lo = halves(inverse[...])
    last = ((1,), (1,))
    all_of(g)

    @pl.loop(0, 8)
    def _(n):
        g_turned[n] = g_all[lax.div(n, 2), lax.rem(n, 2)].reshape(512, 512).T

    copy = pltpu.make_async_copy(g_turned, grads_out, out_sem)
    copy.start()
    all_of(a)
    all_of(b)
    high, low = halves(jnp.concatenate([sum4(end_z), sum4(end_x)], axis=0))
    own = one(inv_hi, high) + (one(inv_hi, low) + one(inv_lo, high))
    out[x, z] = own.reshape(2, 256, 128)
    a = sent(send, recv, 37, Z, lambda to: out.at[x, z, 0], lambda to: out.at[x, z, 0])
    b = sent(send, recv, 38, X, lambda to: out.at[x, z, 1], lambda to: out.at[x, z, 1])
    seen[0, c] = lax.dot_general(
        jnp.ones((8, 128), F32), own * own, (((1,), (1,)), ((), ())),
        precision=lax.Precision.HIGHEST, preferred_element_type=F32,
    )
    all_of(sent(send, recv, 39, C, lambda to: seen.at[0, c], lambda to: seen.at[0, c]))
    seen[1, x] = seen[0, 0] + seen[0, 1]
    q = sent(send, recv, 40, X, lambda to: seen.at[1, x], lambda to: seen.at[1, x])
    all_of(q)
    seen[2, z] = sum4(seen.at[1])
    q = sent(send, recv, 41, Z, lambda to: seen.at[2, z], lambda to: seen.at[2, z])
    all_of(a)
    a = gather_begun(send, recv, 43, X, lambda at: out.at[at, :, 0])
    all_of(b)
    b = gather_begun(send, recv, 47, Z, lambda at: out.at[:, at, 1])
    all_of(q)
    seen[3, y] = sum4(seen.at[2])
    q = sent(send, recv, 42, Y, lambda to: seen.at[3, y], lambda to: seen.at[3, y])
    ortho[...] = one(p_hi, inv_hi, last) + (one(p_hi, inv_lo, last) + one(p_lo, inv_hi, last))
    a = gather_relayed(send, recv, 43, X, a, lambda at, h: out.at[at, 2 * h : 2 * h + 2, 0])
    b = gather_relayed(send, recv, 47, Z, b, lambda at, h: out.at[2 * h : 2 * h + 2, at, 1])
    all_of(q)
    scale[...] = jnp.sqrt(sum4(seen.at[3])) + EPSILON
    copy.wait()
    all_of(a)
    all_of(b)


def chain(activations, grad_out, momentum, right_factor):
    big = [((4, 4, 2, 256, 128), F32), ((2, 4, 64, RANK), F32), ((4, 2, 4, 16, RANK), F32)]
    shapes = [
        ((2048, RANK), BF16), ((2048, RANK), BF16), ((16, 32, 512), BF16),
        ((2, 4, 32, RANK), F32), ((4, 32, RANK), F32), ((4, 32, RANK), F32), ((4, 32, RANK), F32),
        ((4, 4, 2, 16, RANK), F32),
        ((2, 4, 64, RANK), F32), ((4, 64, RANK), F32), ((4, 64, RANK), F32), ((4, 64, RANK), F32),
        ((2, 4, 16, RANK), F32), ((4, 16, RANK), F32), ((4, 16, RANK), F32),
        ((4, 4, 2, 16, RANK), F32), ((4, 4, 16, RANK), F32), ((4, 4, 16, RANK), F32),
        ((4, 16, RANK), F32), ((4, 16, RANK), F32), ((4, 16, RANK), F32), ((4, 16, RANK), F32),
        ((2, 4, 2, 16, RANK), F32),
        ((2, 2, 256, 128), F32), ((2, 2, 256, 128), F32),
        ((2, 2, 256, 128), F32), ((2, 2, 256, 128), F32),
        ((2, 4, 256, 128), F32), ((2, 4, 256, 128), F32),
        ((4, 256, 128), F32), ((4, 256, 128), F32),
        ((4, 2, 2, 2, 4, 32, 512), BF16), ((8, 512, 512), BF16),
        ((RANK, RANK), F32), ((RANK, RANK), F32), ((4, 4, 8, RANK), F32),
    ]
    semaphores = [(51, 3), (51, 3), (4, 2), (4, 2), ()]
    return pl.pallas_call(
        chain_kernel,
        out_shape=(
            jax.ShapeDtypeStruct((4, 4, 2, 256, 128), F32),
            jax.ShapeDtypeStruct((RANK, RANK), F32),
            jax.ShapeDtypeStruct((8, 512, 512), BF16),
            jax.ShapeDtypeStruct((8, RANK), F32),
        ),
        in_specs=[VMEM] * 4,
        out_specs=(VMEM, VMEM, ANY, VMEM),
        scratch_shapes=[pltpu.VMEM(*s) for s in big + shapes]
        + [pltpu.SemaphoreType.DMA(s) for s in semaphores],
        compiler_params=pltpu.CompilerParams(
            collective_id=1, has_side_effects=True, vmem_limit_bytes=58 << 20
        ),
        cost_estimate=pl.CostEstimate(flops=1 << 34, bytes_accessed=128 << 20, transcendentals=0),
    )(activations, grad_out.reshape(2, 2, 4, 32, 512), momentum, right_factor)


def final_kernel(a_ref, g_ref, m_ref, r_ref, l_ref, n_ref, momentum, right, update, low_ref, s_hi, s_lo, inv_ref):
    @pl.when(pl.program_id(0) == 0)
    def _():
        ortho = l_ref[...]
        inv_ref[...] = 1.0 / n_ref[...]
        low_ref[...] = (FEEDBACK * ortho).astype(BF16)
        s_hi[...], s_lo[...] = halves(ortho * (math.sqrt(DOUT * DIN / RANK) * inv_ref[0:1, :]))

    raw = jnp.concatenate([r_ref[0, k].reshape(RANK, 128) for k in range(2)], axis=1)
    r_hi, r_lo = halves(raw)
    buffer = m_ref[...] - one(low_ref[...], r_hi)
    for n in range(8):
        buffer = buffer + one(g_ref[n], a_ref[512 * n : 512 * n + 512, :])
    momentum[...] = buffer
    update[...] = (one(s_hi[...], r_hi) + (one(s_hi[...], r_lo) + one(s_lo[...], r_hi))).astype(BF16)
    right[...] = raw.T * inv_ref[0:1, :]


def final(activations, grads, momentum, right_t, left, norms):
    wide = 256
    tile = pl.BlockSpec((RANK, wide), lambda j: (0, j))
    return pl.pallas_call(
        final_kernel,
        grid=(2048 // wide,),
        in_specs=[
            pl.BlockSpec((4096, wide), lambda j: (0, j)),
            pl.BlockSpec((8, 512, 512), lambda j: (0, 0, 0), pipeline_mode=pl.Buffered(1)),
            tile,
            pl.BlockSpec((1, 2, 2, 256, 128), lambda j: (j // 2, j % 2, 0, 0, 0)),
            pl.BlockSpec((RANK, RANK), lambda j: (0, 0)),
            pl.BlockSpec((8, RANK), lambda j: (0, 0)),
        ],
        out_specs=(tile, pl.BlockSpec((wide, RANK), lambda j: (j, 0)), tile),
        out_shape=(
            jax.ShapeDtypeStruct((RANK, 2048), F32),
            jax.ShapeDtypeStruct((2048, RANK), F32),
            jax.ShapeDtypeStruct((RANK, 2048), BF16),
        ),
        scratch_shapes=[pltpu.VMEM((RANK, RANK), BF16)] * 3 + [pltpu.VMEM((8, RANK), F32)],
        compiler_params=pltpu.CompilerParams(vmem_limit_bytes=60 << 20),
        cost_estimate=pl.CostEstimate(flops=1 << 32, bytes_accessed=20 << 20, transcendentals=0),
    )(activations, grads, momentum, right_t, left, norms)


def body(activations, grad_out, momentum, right_factor):
    all_activations = lax.all_gather(activations, WIDE, axis=0, tiled=True)
    right_t, ortho_left, grads, norms = chain(activations, grad_out, momentum, right_factor)
    return final(all_activations, grads, momentum, right_t, ortho_left, norms)


def solution(mesh):
    finer = Mesh(mesh.devices.reshape(4, 4, 4, 2), (X, Z, Y, C))
    in_specs = (P(WIDE, NARROW), P(NARROW, WIDE), P(WIDE, NARROW), P(NARROW, None))
    out_specs = (P(WIDE, NARROW), P(NARROW, None), P(WIDE, NARROW))
    return jax.shard_map(body, mesh=finer, in_specs=in_specs, out_specs=out_specs, check_vma=False)
```

```python
import math

import jax
import jax.numpy as jnp
from jax import lax
from jax.experimental import pallas as pl
from jax.experimental.pallas import tpu as pltpu
from jax.sharding import Mesh
from jax.sharding import PartitionSpec as P

DOUT = 8192
DIN = 16384
RANK = 512
X, Z, Y, C = "wide_0", "wide_1", "narrow_0", "narrow_1"
NARROW = (Y, C)
WIDE = (X, Z)
FEEDBACK = 0.05
EPSILON = 1e-06
F32 = jnp.float32
BF16 = jnp.bfloat16
VMEM = pl.BlockSpec(memory_space=pltpu.VMEM)
MESH = pl.DeviceIdType.MESH

def eliminated(rows):
    lane = lax.broadcasted_iota(jnp.int32, (8, 128), 1)
    sub = lax.broadcasted_iota(jnp.int32, (8, 128), 0)
    groups = len(rows)
    for p in range(groups):
        here = rows[p]
        cols = [jnp.broadcast_to(here[:, 8 * p + k : 8 * p + k + 1], (8, 128)) for k in range(8)]
        a = [[jnp.broadcast_to(cols[k][i : i + 1, :], (8, 128)) if k <= i else None for k in range(8)] for i in range(8)]
        low = [[None] * 8 for _ in range(8)]
        root = [None] * 8
        for k in range(8):
            root[k] = lax.rsqrt(a[k][k])
            for i in range(k + 1, 8):
                low[i][k] = a[i][k] * root[k]
            for i in range(k + 1, 8):
                for j in range(k + 1, i + 1):
                    a[i][j] = a[i][j] - low[i][k] * low[j][k]
        inside = (lane >= 8 * p) & (lane < 8 * p + 8)
        unit = jnp.where(lane == sub + 8 * p, 1.0, 0.0).astype(F32)
        source = jnp.where(inside, unit, here)
        y = []
        for k in range(8):
            value = jnp.broadcast_to(source[k : k + 1, :], (8, 128))
            for m in range(k):
                value = value - low[k][m] * y[m]
            y.append(value * root[k])
        done = y[0]
        for k in range(1, 8):
            done = jnp.where(sub == k, y[k], done)
        rows[p] = done
        for g in range(p + 1, groups):
            c = []
            total = jnp.where(inside, 0.0, rows[g])
            for k in range(8):
                value = jnp.broadcast_to(rows[g][:, 8 * p + k : 8 * p + k + 1], (8, 128))
                for m in range(k):
                    value = value - low[k][m] * c[m]
                c.append(value * root[k])
                total = total - c[k] * y[k]
            rows[g] = total
    return rows


def factored(s_ref, begin, end):
    highest = lax.Precision.HIGHEST
    row = lax.broadcasted_iota(jnp.int32, (128, 128), 0)
    col = lax.broadcasted_iota(jnp.int32, (128, 128), 1)
    tall = lax.broadcasted_iota(jnp.int32, (RANK, 128), 0)
    wide = lax.broadcasted_iota(jnp.int32, (128, RANK), 1)

    @pl.loop(begin, end)
    def _(b):
        o = pl.multiple_of(128 * b, 128)
        here = pl.ds(o, 128)
        rows = [s_ref[pl.ds(pl.multiple_of(o + 8 * g, 8), 8), here] for g in range(16)]
        inv = jnp.where(row >= col, jnp.concatenate(eliminated(rows), axis=0), 0.0)
        s_ref[here, here] = jnp.where(row == col, 1.0, 0.0).astype(F32)
        y = jnp.dot(inv, s_ref[here, :], precision=highest, preferred_element_type=F32)
        s_ref[here, :] = y
        s_ref[:, here] = jnp.where(tall >= o + 128, 0.0, s_ref[:, here])
        rest = jnp.where(wide >= o + 128, y, 0.0)
        s_ref[...] = s_ref[...] - lax.dot_general(
            rest, y, (((0,), (0,)), ((), ())), precision=highest, preferred_element_type=F32
        )


def lower_part(value):
    row = lax.broadcasted_iota(jnp.int32, value.shape, 0)
    col = lax.broadcasted_iota(jnp.int32, value.shape, 1)
    return jnp.where(row >= col, value, 0.0)


def halves(value):
    high = value.astype(BF16)
    return high, (value - high.astype(F32)).astype(BF16)


def one(left, right, dims=((1,), (0,))):
    return lax.dot_general(left, right, (dims, ((), ())), preferred_element_type=F32)


def dot3(left, right, dims=((1,), (0,))):
    a, b = halves(left)
    c, d = halves(right)
    return one(a, c, dims) + (one(a, d, dims) + one(b, c, dims))


def partner(axis, step):
    size = 2 if axis == C else 4
    return lax.rem(lax.axis_index(axis) + step, size)


ANY = pl.BlockSpec(memory_space=pl.ANY)
HBM = pl.BlockSpec(memory_space=pltpu.HBM)


def line_peers(axes):
    peers = []
    for axis in axes:
        for step in range(1, 2 if axis == C else 4):
            peers.append({axis: partner(axis, step)})
    return peers


def hail(peer):
    pl.semaphore_signal(
        pltpu.get_barrier_semaphore(), inc=1, device_id=peer, device_id_type=MESH
    )


def greet(peers):
    for peer in peers:
        hail(peer)
    pl.semaphore_wait(pltpu.get_barrier_semaphore(), len(peers))


def sent(send, recv, phase, axis, source, target):
    copies = []
    for step in range(1, 2 if axis == C else 4):
        to = partner(axis, step)
        copy = pltpu.make_async_remote_copy(
            src_ref=source(to),
            dst_ref=target(to),
            send_sem=send.at[phase, step - 1],
            recv_sem=recv.at[phase, step - 1],
            device_id={axis: to},
            device_id_type=MESH,
        )
        copy.start()
        copies.append(copy)
    return copies


def all_of(copies):
    for copy in copies:
        copy.wait()


def sum4(ref):
    return (ref[0] + ref[1]) + (ref[2] + ref[3])


def hop(send, recv, phase, axis, step, source, target):
    copy = pltpu.make_async_remote_copy(
        src_ref=source,
        dst_ref=target,
        send_sem=send.at[phase, 0],
        recv_sem=recv.at[phase, 0],
        device_id={axis: partner(axis, step)},
        device_id_type=MESH,
    )
    copy.start()
    return copy


def sum_begun(send, recv, phase, axis, piece, relays, come):
    right, left, far = partner(axis, 1), partner(axis, 3), partner(axis, 2)
    return [
        hop(send, recv, phase, axis, 1, piece(far, 0), relays.at[0]),
        hop(send, recv, phase + 1, axis, 3, piece(far, 1), relays.at[1]),
        hop(send, recv, phase + 2, axis, 1, piece(right, 1), come.at[0, 2:4]),
        hop(send, recv, phase + 3, axis, 3, piece(left, 0), come.at[1, 0:2]),
    ]


def sum_relayed(send, recv, phase, axis, begun, piece, relays, passed, come):
    right, left = partner(axis, 1), partner(axis, 3)
    begun[0].wait()
    passed[0] = relays[0] + piece(right, 0)[...]
    first = hop(send, recv, phase + 4, axis, 1, passed.at[0], come.at[0, 0:2])
    begun[1].wait()
    passed[1] = relays[1] + piece(left, 1)[...]
    return begun[2:] + [first, hop(send, recv, phase + 5, axis, 3, passed.at[1], come.at[1, 2:4])]


def gather_begun(send, recv, phase, axis, piece):
    me = lax.axis_index(axis)
    return [
        hop(send, recv, phase, axis, 1, piece(me), piece(me)),
        hop(send, recv, phase + 1, axis, 3, piece(me), piece(me)),
    ]


def gather_relayed(send, recv, phase, axis, begun, part):
    right, left = partner(axis, 1), partner(axis, 3)
    begun[0].wait()
    first = hop(send, recv, phase + 2, axis, 1, part(left, 0), part(left, 0))
    begun[1].wait()
    return [first, hop(send, recv, phase + 3, axis, 3, part(right, 1), part(right, 1))]


def chain_kernel(
    a_ref, g_ref, m_ref, q_ref,
    solved, ortho, grads_out,
    wt, left, gram, q_hi, q_lo, g_mine, z_part, z_pair, z_half, z_seen, z_all,
    part, pair, half, share,
    block, gx, gz,
    v_part, v_x, v_z, v_sx, v_sz, v_ex, v_ez, v_all,
    relay_x, relay_z, pass_x, pass_z, come_x, come_z, end_x, end_z,
    g_all, g_turned, factor, inverse,
    send, recv, g_send, g_recv, out_sem,
):
    x, z, y, c = (lax.axis_index(a) for a in (X, Z, Y, C))
    first = ((0,), (0,))
    others = [(dy, dc) for dy in range(4) for dc in range(2) if dy or dc]
    greet(line_peers((X, Z)) + [{Y: partner(Y, dy), C: partner(C, dc)} for dy, dc in others])

    deals = []
    mine = pl.ds(2 * (2 * y + c), 2)
    for dy, dc in others:
        to_y, to_c = partner(Y, dy), partner(C, dc)
        deals.append(
            pltpu.make_async_remote_copy(
                src_ref=g_ref.at[:, to_c, to_y],
                dst_ref=g_mine.at[mine],
                send_sem=g_send.at[dy, dc],
                recv_sem=g_recv.at[dy, dc],
                device_id={Y: to_y, C: to_c},
                device_id_type=MESH,
            )
        )
        deals[-1].start()
    g_mine[mine] = g_ref[:, c, y]

    @pl.loop(0, 4)
    def _(i):
        rows = pl.ds(pl.multiple_of(512 * i, 512), 512)
        q_hi[rows, :], q_lo[rows, :] = halves(q_ref[rows, :])

    z_part[...] = (one(a_ref[...], q_hi[...]) + one(a_ref[...], q_lo[...])).reshape(2, 4, 32, RANK)
    all_of(sent(send, recv, 0, C, lambda to: z_part.at[to], lambda to: z_pair))
    z_half[...] = z_part[c] + z_pair[...]
    copies = sent(send, recv, 1, Y, lambda to: z_half.at[to], lambda to: z_seen.at[y])
    z_seen[y] = z_half[y]
    all_of(copies)
    z_all[x, z] = sum4(z_seen).reshape(2, 16, RANK)
    za = sent(send, recv, 15, Z, lambda to: z_all.at[x, z, 0], lambda to: z_all.at[x, z, 0])
    zb = sent(send, recv, 16, X, lambda to: z_all.at[x, z, 1], lambda to: z_all.at[x, z, 1])

    def momentum_left(begin, end):
        @pl.loop(begin, end)
        def _(i):
            rows = pl.ds(pl.multiple_of(128 * i, 128), 128)
            high, low = halves(m_ref[rows, :])
            total = one(high, q_hi[...]) + (one(low, q_hi[...]) + one(high, q_lo[...]))
            part[lax.div(i, 2), pl.ds(2 * lax.rem(i, 2), 2)] = total.reshape(2, 64, RANK)

    momentum_left(0, 1)
    all_of(za)
    za = sent(send, recv, 17, X, lambda to: z_all.at[x, :, 0], lambda to: z_all.at[x, :, 0])
    all_of(zb)
    zb = sent(send, recv, 18, Z, lambda to: z_all.at[:, z, 1], lambda to: z_all.at[:, z, 1])
    momentum_left(1, 4)
    for deal in deals:
        deal.wait()
    all_of(za)
    all_of(zb)
    high, low = halves(z_all[...].reshape(RANK, RANK))
    grads = g_mine[...].reshape(512, 512)
    gz_product = one(grads, high, first) + one(grads, low, first)
    part[...] = part[...] + gz_product.reshape(2, 4, 64, RANK)

    all_of(sent(send, recv, 2, C, lambda to: part.at[to], lambda to: pair))
    half[...] = part[c] + pair[...]
    copies = sent(send, recv, 3, Y, lambda to: half.at[to], lambda to: share.at[y])
    share[y] = half[y]
    all_of(copies)
    left[c, y] = sum4(share)
    all_of(sent(send, recv, 4, Y, lambda to: left.at[c, y], lambda to: left.at[c, y]))
    all_of(sent(send, recv, 5, C, lambda to: left.at[c], lambda to: left.at[c]))
    whole = left[...].reshape(RANK, RANK)
    p_hi, p_lo = halves(whole)

    v_part[...] = (one(grads, p_hi) + one(grads, p_lo)).reshape(4, 4, 2, 16, RANK)
    va = sent(send, recv, 11, X, lambda to: v_part.at[to, :, 0], lambda to: v_x.at[x])
    vb = sent(send, recv, 12, Z, lambda to: v_part.at[:, to, 1], lambda to: v_z.at[z])
    for index in range(4):
        @pl.when(y == index)
        def _():
            own = whole[:, 128 * index : 128 * index + 128]
            block[...] = dot3(own, whole, first).reshape(2, 4, 16, RANK)
    g = sent(send, recv, 6, X, lambda to: block.at[c, to], lambda to: gx.at[x])
    gx[x] = block[c, x]
    v_x[x] = v_part[x, :, 0]
    v_z[z] = v_part[:, z, 1]
    t_hi, t_lo = halves(whole.T)
    q_hi[0:RANK, :] = t_hi
    q_lo[0:RANK, :] = t_lo

    def momentum_right(begin, end):
        @pl.loop(begin, end)
        def _(j):
            columns = pl.ds(pl.multiple_of(256 * j, 256), 256)
            high, low = halves(m_ref[:, columns])
            left_hi, left_lo = q_hi[0:RANK, :], q_lo[0:RANK, :]
            total = one(left_hi, high) + (one(left_lo, high) + one(left_hi, low))
            for k in range(2):
                piece = total[:, 128 * k : 128 * k + 128].reshape(2, 256, 128)
                wt[lax.div(j, 2), 2 * lax.rem(j, 2) + k] = piece

    momentum_right(0, 2)
    all_of(va)
    v_sx[...] = sum4(v_x)
    va = sent(send, recv, 13, Z, lambda to: v_sx.at[to], lambda to: v_ez.at[z])
    all_of(vb)
    v_sz[...] = sum4(v_z)
    vb = sent(send, recv, 14, X, lambda to: v_sz.at[to], lambda to: v_ex.at[x])
    v_ez[z] = v_sx[z]
    v_ex[x] = v_sz[x]
    all_of(g)
    gz[z] = sum4(gx)
    g = sent(send, recv, 7, Z, lambda to: gz.at[z], lambda to: gz.at[z])
    momentum_right(2, 3)
    all_of(va)
    v_all[c, y, 0] = sum4(v_ez)
    all_of(vb)
    v_all[c, y, 1] = sum4(v_ex)
    v = sent(send, recv, 19, Y, lambda to: v_all.at[c, y], lambda to: v_all.at[c, y])
    all_of(g)
    gram[y, c, x] = sum4(gz)
    g = sent(send, recv, 8, X, lambda to: gram.at[y, c, x], lambda to: gram.at[y, c, x])
    momentum_right(3, 5)
    all_of(v)
    v = sent(send, recv, 20, C, lambda to: v_all.at[c], lambda to: v_all.at[c])
    all_of(g)
    g = sent(send, recv, 9, Y, lambda to: gram.at[y, c], lambda to: gram.at[y, c])
    momentum_right(5, 8)
    all_of(v)
    t_hi, t_lo = halves(v_all[...].reshape(256, RANK).T)
    q_hi[RANK : 2 * RANK, 0:256] = t_hi
    q_lo[RANK : 2 * RANK, 0:256] = t_lo
    all_of(g)
    g = sent(send, recv, 10, C, lambda to: gram.at[:, c], lambda to: gram.at[:, c])

    @pl.loop(0, 8)
    def _(j):
        columns = pl.ds(pl.multiple_of(256 * j, 256), 256)
        tokens = a_ref[:, columns]
        high, low = q_hi[RANK : 2 * RANK, 0:256], q_lo[RANK : 2 * RANK, 0:256]
        total = one(high, tokens) + one(low, tokens)
        for k in range(2):
            piece = total[:, 128 * k : 128 * k + 128].reshape(2, 256, 128)
            at = (lax.div(j, 2), 2 * lax.rem(j, 2) + k)
            wt[at] = wt[at] + piece

    def part_x(to, half):
        return wt.at[to, 2 * half : 2 * half + 2, 0]

    def part_z(to, half):
        return wt.at[2 * half : 2 * half + 2, to, 1]

    a = sum_begun(send, recv, 21, X, part_x, relay_x, come_x)
    b = sum_begun(send, recv, 27, Z, part_z, relay_z, come_z)
    all_of(g)
    g = sent(send, recv, 33, Y, lambda to: g_ref, lambda to: g_all.at[y, c])
    g_all[y, c] = g_ref[...]
    factor[...] = gram[...].reshape(RANK, RANK)
    factored(factor, 0, 2)
    a = sum_relayed(send, recv, 21, X, a, part_x, relay_x, pass_x, come_x)
    b = sum_relayed(send, recv, 27, Z, b, part_z, relay_z, pass_z, come_z)
    factored(factor, 2, 4)
    inverse[...] = lower_part(factor[...])
    all_of(a)
    sum_x = wt.at[x, :, 0]
    sum_x[...] = sum_x[...] + (come_x[0] + come_x[1])
    a = sent(send, recv, 34, Z, lambda to: wt.at[x, to, 0], lambda to: end_z.at[z])
    all_of(b)
    sum_z = wt.at[:, z, 1]
    sum_z[...] = sum_z[...] + (come_z[0] + come_z[1])
    b = sent(send, recv, 35, X, lambda to: wt.at[to, z, 1], lambda to: end_x.at[x])
    end_z[z] = wt[x, z, 0]
    end_x[x] = wt[x, z, 1]
    all_of(g)
    g = sent(send, recv, 36, C, lambda to: g_all.at[:, c], lambda to: g_all.at[:, c])
    inv_hi, inv_lo = halves(inverse[...])
    last = ((1,), (1,))
    ortho[...] = one(p_hi, inv_hi, last) + (one(p_hi, inv_lo, last) + one(p_lo, inv_hi, last))
    all_of(g)

    @pl.loop(0, 8)
    def _(n):
        g_turned[n] = g_all[lax.div(n, 2), lax.rem(n, 2)].reshape(512, 512).T

    copy = pltpu.make_async_copy(g_turned, grads_out, out_sem)
    copy.start()
    all_of(a)
    all_of(b)
    high, low = halves(jnp.concatenate([sum4(end_z), sum4(end_x)], axis=0))
    solved[...] = one(inv_hi, high) + (one(inv_hi, low) + one(inv_lo, high))
    copy.wait()


def chain(activations, grad_out, momentum, right_factor):
    big = [((4, 4, 2, 256, 128), F32), ((2, 4, 64, RANK), F32), ((4, 2, 4, 16, RANK), F32)]
    shapes = [
        ((2048, RANK), BF16), ((2048, RANK), BF16), ((16, 32, 512), BF16),
        ((2, 4, 32, RANK), F32), ((4, 32, RANK), F32), ((4, 32, RANK), F32), ((4, 32, RANK), F32),
        ((4, 4, 2, 16, RANK), F32),
        ((2, 4, 64, RANK), F32), ((4, 64, RANK), F32), ((4, 64, RANK), F32), ((4, 64, RANK), F32),
        ((2, 4, 16, RANK), F32), ((4, 16, RANK), F32), ((4, 16, RANK), F32),
        ((4, 4, 2, 16, RANK), F32), ((4, 4, 16, RANK), F32), ((4, 4, 16, RANK), F32),
        ((4, 16, RANK), F32), ((4, 16, RANK), F32), ((4, 16, RANK), F32), ((4, 16, RANK), F32),
        ((2, 4, 2, 16, RANK), F32),
        ((2, 2, 256, 128), F32), ((2, 2, 256, 128), F32),
        ((2, 2, 256, 128), F32), ((2, 2, 256, 128), F32),
        ((2, 4, 256, 128), F32), ((2, 4, 256, 128), F32),
        ((4, 256, 128), F32), ((4, 256, 128), F32),
        ((4, 2, 2, 2, 4, 32, 512), BF16), ((8, 512, 512), BF16),
        ((RANK, RANK), F32), ((RANK, RANK), F32),
    ]
    semaphores = [(37, 3), (37, 3), (4, 2), (4, 2), ()]
    return pl.pallas_call(
        chain_kernel,
        out_shape=(
            jax.ShapeDtypeStruct((RANK, 128), F32),
            jax.ShapeDtypeStruct((RANK, RANK), F32),
            jax.ShapeDtypeStruct((8, 512, 512), BF16),
        ),
        in_specs=[VMEM] * 4,
        out_specs=(VMEM, VMEM, ANY),
        scratch_shapes=[pltpu.VMEM(*s) for s in big + shapes]
        + [pltpu.SemaphoreType.DMA(s) for s in semaphores],
        compiler_params=pltpu.CompilerParams(
            collective_id=1, has_side_effects=True, vmem_limit_bytes=58 << 20
        ),
        cost_estimate=pl.CostEstimate(flops=1 << 34, bytes_accessed=128 << 20, transcendentals=0),
    )(activations, grad_out.reshape(2, 2, 4, 32, 512), momentum, right_factor)


def gather_kernel(
    share, tokens, turned, momentum,
    out, buffer, scale,
    g_all, m_all, slots, sums, seen, send, recv, load_sem, tile_sem, store_sem,
):
    x, z, y, c = (lax.axis_index(a) for a in (X, Z, Y, C))

    def tile(j):
        slot = lax.rem(j, 2)
        columns = pl.ds(pl.multiple_of(256 * j, 256), 256)
        return pltpu.make_async_copy(tokens.at[:, columns], slots.at[slot], tile_sem.at[slot])

    def store(j):
        slot = lax.rem(j, 2)
        columns = pl.ds(pl.multiple_of(256 * j, 256), 256)
        return pltpu.make_async_copy(sums.at[slot], buffer.at[:, columns], store_sem.at[slot])

    loads = [
        pltpu.make_async_copy(turned.at[n], g_all.at[:, 512 * n : 512 * n + 512], load_sem.at[n])
        for n in range(8)
    ]
    loads.append(pltpu.make_async_copy(momentum, m_all, load_sem.at[8]))
    for load in loads:
        load.start()
    tile(0).start()
    tile(1).start()
    greet(line_peers((X, Z, Y, C)))
    own = share[...]
    out[x, z] = own.reshape(2, 256, 128)
    a = sent(send, recv, 0, Z, lambda to: out.at[x, z, 0], lambda to: out.at[x, z, 0])
    b = sent(send, recv, 1, X, lambda to: out.at[x, z, 1], lambda to: out.at[x, z, 1])
    seen[0, c] = lax.dot_general(
        jnp.ones((8, 128), F32), own * own, (((1,), (1,)), ((), ())),
        precision=lax.Precision.HIGHEST, preferred_element_type=F32,
    )
    all_of(sent(send, recv, 2, C, lambda to: seen.at[0, c], lambda to: seen.at[0, c]))
    seen[1, x] = seen[0, 0] + seen[0, 1]
    q = sent(send, recv, 3, X, lambda to: seen.at[1, x], lambda to: seen.at[1, x])
    for load in loads:
        load.wait()
    all_of(q)
    seen[2, z] = sum4(seen.at[1])
    q = sent(send, recv, 4, Z, lambda to: seen.at[2, z], lambda to: seen.at[2, z])
    all_of(a)
    a = gather_begun(send, recv, 6, X, lambda at: out.at[at, :, 0])
    all_of(b)
    b = gather_begun(send, recv, 10, Z, lambda at: out.at[:, at, 1])
    all_of(q)
    seen[3, y] = sum4(seen.at[2])
    q = sent(send, recv, 5, Y, lambda to: seen.at[3, y], lambda to: seen.at[3, y])

    def gradient(begin, end):
        @pl.loop(begin, end)
        def _(j):
            slot = lax.rem(j, 2)
            columns = pl.ds(pl.multiple_of(256 * j, 256), 256)
            tile(j).wait()

            @pl.when(j >= 2)
            def _():
                store(j - 2).wait()

            sums[slot] = m_all[:, columns] + one(g_all[...], slots[slot])
            store(j).start()

            @pl.when(j < 6)
            def _():
                tile(j + 2).start()

    gradient(0, 8)
    a = gather_relayed(send, recv, 6, X, a, lambda at, h: out.at[at, 2 * h : 2 * h + 2, 0])
    b = gather_relayed(send, recv, 10, Z, b, lambda at, h: out.at[2 * h : 2 * h + 2, at, 1])
    all_of(q)
    scale[...] = jnp.sqrt(sum4(seen.at[3])) + EPSILON
    store(6).wait()
    store(7).wait()
    all_of(a)
    all_of(b)


def gathered(share, activations, grads, momentum):
    return pl.pallas_call(
        gather_kernel,
        out_shape=(
            jax.ShapeDtypeStruct((4, 4, 2, 256, 128), F32),
            jax.ShapeDtypeStruct((RANK, 2048), F32),
            jax.ShapeDtypeStruct((8, RANK), F32),
        ),
        in_specs=[VMEM, HBM, HBM, HBM],
        out_specs=(VMEM, ANY, VMEM),
        scratch_shapes=[
            pltpu.VMEM((512, 4096), BF16),
            pltpu.VMEM((RANK, 2048), F32),
            pltpu.VMEM((2, 4096, 256), BF16),
            pltpu.VMEM((2, RANK, 256), F32),
            pltpu.VMEM((4, 4, 8, RANK), F32),
            pltpu.SemaphoreType.DMA((14, 3)),
            pltpu.SemaphoreType.DMA((14, 3)),
            pltpu.SemaphoreType.DMA((9,)),
            pltpu.SemaphoreType.DMA((2,)),
            pltpu.SemaphoreType.DMA((2,)),
        ],
        compiler_params=pltpu.CompilerParams(
            collective_id=2, has_side_effects=True, vmem_limit_bytes=42 << 20
        ),
        cost_estimate=pl.CostEstimate(flops=1 << 34, bytes_accessed=128 << 20, transcendentals=0),
    )(share, activations, grads, momentum)


def final_kernel(b_ref, r_ref, l_ref, n_ref, momentum, right, update, low_ref, s_hi, s_lo, inv_ref):
    @pl.when(pl.program_id(0) == 0)
    def _():
        ortho = l_ref[...]
        inv_ref[...] = 1.0 / n_ref[...]
        low_ref[...] = (FEEDBACK * ortho).astype(BF16)
        s_hi[...], s_lo[...] = halves(ortho * (math.sqrt(DOUT * DIN / RANK) * inv_ref[0:1, :]))

    raw = jnp.concatenate([r_ref[0, k].reshape(RANK, 128) for k in range(4)], axis=1)
    r_hi, r_lo = halves(raw)
    momentum[...] = b_ref[...] - one(low_ref[...], r_hi)
    update[...] = (one(s_hi[...], r_hi) + (one(s_hi[...], r_lo) + one(s_lo[...], r_hi))).astype(BF16)
    right[...] = raw.T * inv_ref[0:1, :]


def final(buffer, right_t, left, norms):
    wide = 512
    tile = pl.BlockSpec((RANK, wide), lambda j: (0, j))
    return pl.pallas_call(
        final_kernel,
        grid=(2048 // wide,),
        in_specs=[
            tile,
            pl.BlockSpec((1, 4, 2, 256, 128), lambda j: (j, 0, 0, 0, 0)),
            pl.BlockSpec((RANK, RANK), lambda j: (0, 0)),
            pl.BlockSpec((8, RANK), lambda j: (0, 0)),
        ],
        out_specs=(tile, pl.BlockSpec((wide, RANK), lambda j: (j, 0)), tile),
        out_shape=(
            jax.ShapeDtypeStruct((RANK, 2048), F32),
            jax.ShapeDtypeStruct((2048, RANK), F32),
            jax.ShapeDtypeStruct((RANK, 2048), BF16),
        ),
        scratch_shapes=[pltpu.VMEM((RANK, RANK), BF16)] * 3 + [pltpu.VMEM((8, RANK), F32)],
        compiler_params=pltpu.CompilerParams(vmem_limit_bytes=24 << 20),
        cost_estimate=pl.CostEstimate(flops=1 << 32, bytes_accessed=20 << 20, transcendentals=0),
    )(buffer, right_t, left, norms)


def body(activations, grad_out, momentum, right_factor):
    all_activations = lax.all_gather(activations, WIDE, axis=0, tiled=True)
    share, ortho_left, grads = chain(activations, grad_out, momentum, right_factor)
    right_t, buffer, norms = gathered(share, all_activations, grads, momentum)
    return final(buffer, right_t, ortho_left, norms)


def solution(mesh):
    finer = Mesh(mesh.devices.reshape(4, 4, 4, 2), (X, Z, Y, C))
    in_specs = (P(WIDE, NARROW), P(NARROW, WIDE), P(WIDE, NARROW), P(NARROW, None))
    out_specs = (P(WIDE, NARROW), P(NARROW, None), P(WIDE, NARROW))
    return jax.shard_map(body, mesh=finer, in_specs=in_specs, out_specs=out_specs, check_vma=False)
```

```python
import math

import jax
import jax.numpy as jnp
from jax import lax
from jax.experimental import pallas as pl
from jax.experimental.pallas import tpu as pltpu
from jax.sharding import Mesh
from jax.sharding import PartitionSpec as P

DOUT = 8192
DIN = 16384
RANK = 512
X, Z, Y, C = "wide_0", "wide_1", "narrow_0", "narrow_1"
NARROW = (Y, C)
WIDE = (X, Z)
FEEDBACK = 0.05
EPSILON = 1e-06
F32 = jnp.float32
BF16 = jnp.bfloat16
VMEM = pl.BlockSpec(memory_space=pltpu.VMEM)
MESH = pl.DeviceIdType.MESH

def eliminated(rows):
    lane = lax.broadcasted_iota(jnp.int32, (8, 128), 1)
    sub = lax.broadcasted_iota(jnp.int32, (8, 128), 0)
    groups = len(rows)
    for p in range(groups):
        here = rows[p]
        cols = [jnp.broadcast_to(here[:, 8 * p + k : 8 * p + k + 1], (8, 128)) for k in range(8)]
        a = [[jnp.broadcast_to(cols[k][i : i + 1, :], (8, 128)) if k <= i else None for k in range(8)] for i in range(8)]
        low = [[None] * 8 for _ in range(8)]
        root = [None] * 8
        for k in range(8):
            root[k] = lax.rsqrt(a[k][k])
            for i in range(k + 1, 8):
                low[i][k] = a[i][k] * root[k]
            for i in range(k + 1, 8):
                for j in range(k + 1, i + 1):
                    a[i][j] = a[i][j] - low[i][k] * low[j][k]
        inside = (lane >= 8 * p) & (lane < 8 * p + 8)
        unit = jnp.where(lane == sub + 8 * p, 1.0, 0.0).astype(F32)
        source = jnp.where(inside, unit, here)
        y = []
        for k in range(8):
            value = jnp.broadcast_to(source[k : k + 1, :], (8, 128))
            for m in range(k):
                value = value - low[k][m] * y[m]
            y.append(value * root[k])
        done = y[0]
        for k in range(1, 8):
            done = jnp.where(sub == k, y[k], done)
        rows[p] = done
        for g in range(p + 1, groups):
            c = []
            total = jnp.where(inside, 0.0, rows[g])
            for k in range(8):
                value = jnp.broadcast_to(rows[g][:, 8 * p + k : 8 * p + k + 1], (8, 128))
                for m in range(k):
                    value = value - low[k][m] * c[m]
                c.append(value * root[k])
                total = total - c[k] * y[k]
            rows[g] = total
    return rows


def factored(s_ref, begin, end):
    highest = lax.Precision.HIGHEST
    row = lax.broadcasted_iota(jnp.int32, (128, 128), 0)
    col = lax.broadcasted_iota(jnp.int32, (128, 128), 1)
    tall = lax.broadcasted_iota(jnp.int32, (RANK, 128), 0)
    wide = lax.broadcasted_iota(jnp.int32, (128, RANK), 1)

    @pl.loop(begin, end)
    def _(b):
        o = pl.multiple_of(128 * b, 128)
        here = pl.ds(o, 128)
        rows = [s_ref[pl.ds(pl.multiple_of(o + 8 * g, 8), 8), here] for g in range(16)]
        inv = jnp.where(row >= col, jnp.concatenate(eliminated(rows), axis=0), 0.0)
        s_ref[here, here] = jnp.where(row == col, 1.0, 0.0).astype(F32)
        y = jnp.dot(inv, s_ref[here, :], precision=highest, preferred_element_type=F32)
        s_ref[here, :] = y
        s_ref[:, here] = jnp.where(tall >= o + 128, 0.0, s_ref[:, here])
        rest = jnp.where(wide >= o + 128, y, 0.0)
        s_ref[...] = s_ref[...] - lax.dot_general(
            rest, y, (((0,), (0,)), ((), ())), precision=highest, preferred_element_type=F32
        )


def lower_part(value):
    row = lax.broadcasted_iota(jnp.int32, value.shape, 0)
    col = lax.broadcasted_iota(jnp.int32, value.shape, 1)
    return jnp.where(row >= col, value, 0.0)


def halves(value):
    high = value.astype(BF16)
    return high, (value - high.astype(F32)).astype(BF16)


def one(left, right, dims=((1,), (0,))):
    return lax.dot_general(left, right, (dims, ((), ())), preferred_element_type=F32)


def dot3(left, right, dims=((1,), (0,))):
    a, b = halves(left)
    c, d = halves(right)
    return one(a, c, dims) + (one(a, d, dims) + one(b, c, dims))


def partner(axis, step):
    size = 2 if axis == C else 4
    return lax.rem(lax.axis_index(axis) + step, size)


ANY = pl.BlockSpec(memory_space=pl.ANY)
HBM = pl.BlockSpec(memory_space=pltpu.HBM)


def line_peers(axes):
    peers = []
    for axis in axes:
        for step in range(1, 2 if axis == C else 4):
            peers.append({axis: partner(axis, step)})
    return peers


def hail(peer):
    pl.semaphore_signal(
        pltpu.get_barrier_semaphore(), inc=1, device_id=peer, device_id_type=MESH
    )


def greet(peers):
    for peer in peers:
        hail(peer)
    pl.semaphore_wait(pltpu.get_barrier_semaphore(), len(peers))


def sent(send, recv, phase, axis, source, target):
    copies = []
    for step in range(1, 2 if axis == C else 4):
        to = partner(axis, step)
        copy = pltpu.make_async_remote_copy(
            src_ref=source(to),
            dst_ref=target(to),
            send_sem=send.at[phase, step - 1],
            recv_sem=recv.at[phase, step - 1],
            device_id={axis: to},
            device_id_type=MESH,
        )
        copy.start()
        copies.append(copy)
    return copies


def all_of(copies):
    for copy in copies:
        copy.wait()


def sum4(ref):
    return (ref[0] + ref[1]) + (ref[2] + ref[3])


def hop(send, recv, phase, axis, step, source, target):
    copy = pltpu.make_async_remote_copy(
        src_ref=source,
        dst_ref=target,
        send_sem=send.at[phase, 0],
        recv_sem=recv.at[phase, 0],
        device_id={axis: partner(axis, step)},
        device_id_type=MESH,
    )
    copy.start()
    return copy


def sum_begun(send, recv, phase, axis, piece, relays, come):
    right, left, far = partner(axis, 1), partner(axis, 3), partner(axis, 2)
    return [
        hop(send, recv, phase, axis, 1, piece(far, 0), relays.at[0]),
        hop(send, recv, phase + 1, axis, 3, piece(far, 1), relays.at[1]),
        hop(send, recv, phase + 2, axis, 1, piece(right, 1), come.at[0, 2:4]),
        hop(send, recv, phase + 3, axis, 3, piece(left, 0), come.at[1, 0:2]),
    ]


def sum_relayed(send, recv, phase, axis, begun, piece, relays, passed, come):
    right, left = partner(axis, 1), partner(axis, 3)
    begun[0].wait()
    passed[0] = relays[0] + piece(right, 0)[...]
    first = hop(send, recv, phase + 4, axis, 1, passed.at[0], come.at[0, 0:2])
    begun[1].wait()
    passed[1] = relays[1] + piece(left, 1)[...]
    return begun[2:] + [first, hop(send, recv, phase + 5, axis, 3, passed.at[1], come.at[1, 2:4])]


def gather_begun(send, recv, phase, axis, piece):
    me = lax.axis_index(axis)
    return [
        hop(send, recv, phase, axis, 1, piece(me), piece(me)),
        hop(send, recv, phase + 1, axis, 3, piece(me), piece(me)),
    ]


def gather_relayed(send, recv, phase, axis, begun, part):
    right, left = partner(axis, 1), partner(axis, 3)
    begun[0].wait()
    first = hop(send, recv, phase + 2, axis, 1, part(left, 0), part(left, 0))
    begun[1].wait()
    return [first, hop(send, recv, phase + 3, axis, 3, part(right, 1), part(right, 1))]


def chain_kernel(
    a_ref, g_ref, m_ref, q_ref,
    solved, ortho, grads_out,
    wt, left, gram, q_hi, q_lo, g_mine, z_part, z_pair, z_half, z_seen, z_all,
    part, pair, half, share,
    block, gx, gz,
    v_part, v_x, v_z, v_sx, v_sz, v_ex, v_ez, v_all,
    relay_x, relay_z, pass_x, pass_z, come_x, come_z, end_x, end_z,
    g_all, g_turned, factor, inverse,
    send, recv, g_send, g_recv, out_sem,
):
    x, z, y, c = (lax.axis_index(a) for a in (X, Z, Y, C))
    first = ((0,), (0,))
    others = [(dy, dc) for dy in range(4) for dc in range(2) if dy or dc]
    greet(line_peers((X, Z)) + [{Y: partner(Y, dy), C: partner(C, dc)} for dy, dc in others])

    deals = []
    mine = pl.ds(2 * (2 * y + c), 2)
    for dy, dc in others:
        to_y, to_c = partner(Y, dy), partner(C, dc)
        deals.append(
            pltpu.make_async_remote_copy(
                src_ref=g_ref.at[:, to_c, to_y],
                dst_ref=g_mine.at[mine],
                send_sem=g_send.at[dy, dc],
                recv_sem=g_recv.at[dy, dc],
                device_id={Y: to_y, C: to_c},
                device_id_type=MESH,
            )
        )
        deals[-1].start()
    g_mine[mine] = g_ref[:, c, y]

    @pl.loop(0, 4)
    def _(i):
        rows = pl.ds(pl.multiple_of(512 * i, 512), 512)
        q_hi[rows, :], q_lo[rows, :] = halves(q_ref[rows, :])

    z_part[...] = (one(a_ref[...], q_hi[...]) + one(a_ref[...], q_lo[...])).reshape(2, 4, 32, RANK)
    all_of(sent(send, recv, 0, C, lambda to: z_part.at[to], lambda to: z_pair))
    z_half[...] = z_part[c] + z_pair[...]
    copies = sent(send, recv, 1, Y, lambda to: z_half.at[to], lambda to: z_seen.at[y])
    z_seen[y] = z_half[y]
    all_of(copies)
    z_all[x, z] = sum4(z_seen).reshape(2, 16, RANK)
    za = sent(send, recv, 15, Z, lambda to: z_all.at[x, z, 0], lambda to: z_all.at[x, z, 0])
    zb = sent(send, recv, 16, X, lambda to: z_all.at[x, z, 1], lambda to: z_all.at[x, z, 1])

    def momentum_left(begin, end):
        @pl.loop(begin, end)
        def _(i):
            rows = pl.ds(pl.multiple_of(128 * i, 128), 128)
            high, low = halves(m_ref[rows, :])
            total = one(high, q_hi[...]) + (one(low, q_hi[...]) + one(high, q_lo[...]))
            part[lax.div(i, 2), pl.ds(2 * lax.rem(i, 2), 2)] = total.reshape(2, 64, RANK)

    momentum_left(0, 1)
    all_of(za)
    za = sent(send, recv, 17, X, lambda to: z_all.at[x, :, 0], lambda to: z_all.at[x, :, 0])
    all_of(zb)
    zb = sent(send, recv, 18, Z, lambda to: z_all.at[:, z, 1], lambda to: z_all.at[:, z, 1])
    momentum_left(1, 4)
    for deal in deals:
        deal.wait()
    all_of(za)
    all_of(zb)
    high, low = halves(z_all[...].reshape(RANK, RANK))
    grads = g_mine[...].reshape(512, 512)
    gz_product = one(grads, high, first) + one(grads, low, first)
    part[...] = part[...] + gz_product.reshape(2, 4, 64, RANK)

    all_of(sent(send, recv, 2, C, lambda to: part.at[to], lambda to: pair))
    half[...] = part[c] + pair[...]
    copies = sent(send, recv, 3, Y, lambda to: half.at[to], lambda to: share.at[y])
    share[y] = half[y]
    all_of(copies)
    left[c, y] = sum4(share)
    all_of(sent(send, recv, 4, Y, lambda to: left.at[c, y], lambda to: left.at[c, y]))
    all_of(sent(send, recv, 5, C, lambda to: left.at[c], lambda to: left.at[c]))
    whole = left[...].reshape(RANK, RANK)
    p_hi, p_lo = halves(whole)

    v_part[...] = (one(grads, p_hi) + one(grads, p_lo)).reshape(4, 4, 2, 16, RANK)
    va = sent(send, recv, 11, X, lambda to: v_part.at[to, :, 0], lambda to: v_x.at[x])
    vb = sent(send, recv, 12, Z, lambda to: v_part.at[:, to, 1], lambda to: v_z.at[z])
    for index in range(4):
        @pl.when(y == index)
        def _():
            own = whole[:, 128 * index : 128 * index + 128]
            block[...] = dot3(own, whole, first).reshape(2, 4, 16, RANK)
    g = sent(send, recv, 6, X, lambda to: block.at[c, to], lambda to: gx.at[x])
    gx[x] = block[c, x]
    v_x[x] = v_part[x, :, 0]
    v_z[z] = v_part[:, z, 1]
    t_hi, t_lo = halves(whole.T)
    q_hi[0:RANK, :] = t_hi
    q_lo[0:RANK, :] = t_lo

    def momentum_right(begin, end):
        @pl.loop(begin, end)
        def _(j):
            columns = pl.ds(pl.multiple_of(256 * j, 256), 256)
            high, low = halves(m_ref[:, columns])
            left_hi, left_lo = q_hi[0:RANK, :], q_lo[0:RANK, :]
            total = one(left_hi, high) + (one(left_lo, high) + one(left_hi, low))
            for k in range(2):
                piece = total[:, 128 * k : 128 * k + 128].reshape(2, 256, 128)
                wt[lax.div(j, 2), 2 * lax.rem(j, 2) + k] = piece

    momentum_right(0, 2)
    all_of(va)
    v_sx[...] = sum4(v_x)
    va = sent(send, recv, 13, Z, lambda to: v_sx.at[to], lambda to: v_ez.at[z])
    all_of(vb)
    v_sz[...] = sum4(v_z)
    vb = sent(send, recv, 14, X, lambda to: v_sz.at[to], lambda to: v_ex.at[x])
    v_ez[z] = v_sx[z]
    v_ex[x] = v_sz[x]
    all_of(g)
    gz[z] = sum4(gx)
    g = sent(send, recv, 7, Z, lambda to: gz.at[z], lambda to: gz.at[z])
    momentum_right(2, 3)
    all_of(va)
    v_all[c, y, 0] = sum4(v_ez)
    all_of(vb)
    v_all[c, y, 1] = sum4(v_ex)
    v = sent(send, recv, 19, Y, lambda to: v_all.at[c, y], lambda to: v_all.at[c, y])
    all_of(g)
    gram[y, c, x] = sum4(gz)
    g = sent(send, recv, 8, X, lambda to: gram.at[y, c, x], lambda to: gram.at[y, c, x])
    momentum_right(3, 5)
    all_of(v)
    v = sent(send, recv, 20, C, lambda to: v_all.at[c], lambda to: v_all.at[c])
    all_of(g)
    g = sent(send, recv, 9, Y, lambda to: gram.at[y, c], lambda to: gram.at[y, c])
    momentum_right(5, 8)
    all_of(v)
    t_hi, t_lo = halves(v_all[...].reshape(256, RANK).T)
    q_hi[RANK : 2 * RANK, 0:256] = t_hi
    q_lo[RANK : 2 * RANK, 0:256] = t_lo
    all_of(g)
    g = sent(send, recv, 10, C, lambda to: gram.at[:, c], lambda to: gram.at[:, c])

    @pl.loop(0, 8)
    def _(j):
        columns = pl.ds(pl.multiple_of(256 * j, 256), 256)
        tokens = a_ref[:, columns]
        high, low = q_hi[RANK : 2 * RANK, 0:256], q_lo[RANK : 2 * RANK, 0:256]
        total = one(high, tokens) + one(low, tokens)
        for k in range(2):
            piece = total[:, 128 * k : 128 * k + 128].reshape(2, 256, 128)
            at = (lax.div(j, 2), 2 * lax.rem(j, 2) + k)
            wt[at] = wt[at] + piece

    def part_x(to, half):
        return wt.at[to, 2 * half : 2 * half + 2, 0]

    def part_z(to, half):
        return wt.at[2 * half : 2 * half + 2, to, 1]

    a = sum_begun(send, recv, 21, X, part_x, relay_x, come_x)
    b = sum_begun(send, recv, 27, Z, part_z, relay_z, come_z)
    all_of(g)
    g = sent(send, recv, 33, Y, lambda to: g_ref, lambda to: g_all.at[y, c])
    g_all[y, c] = g_ref[...]
    factor[...] = gram[...].reshape(RANK, RANK)
    factored(factor, 0, 2)
    a = sum_relayed(send, recv, 21, X, a, part_x, relay_x, pass_x, come_x)
    b = sum_relayed(send, recv, 27, Z, b, part_z, relay_z, pass_z, come_z)
    factored(factor, 2, 4)
    inverse[...] = lower_part(factor[...])
    all_of(a)
    sum_x = wt.at[x, :, 0]
    sum_x[...] = sum_x[...] + (come_x[0] + come_x[1])
    a = sent(send, recv, 34, Z, lambda to: wt.at[x, to, 0], lambda to: end_z.at[z])
    all_of(b)
    sum_z = wt.at[:, z, 1]
    sum_z[...] = sum_z[...] + (come_z[0] + come_z[1])
    b = sent(send, recv, 35, X, lambda to: wt.at[to, z, 1], lambda to: end_x.at[x])
    end_z[z] = wt[x, z, 0]
    end_x[x] = wt[x, z, 1]
    all_of(g)
    g = sent(send, recv, 36, C, lambda to: g_all.at[:, c], lambda to: g_all.at[:, c])
    inv_hi, inv_lo = halves(inverse[...])
    last = ((1,), (1,))
    ortho[...] = one(p_hi, inv_hi, last) + (one(p_hi, inv_lo, last) + one(p_lo, inv_hi, last))
    all_of(g)

    @pl.loop(0, 8)
    def _(n):
        g_turned[n] = g_all[lax.div(n, 2), lax.rem(n, 2)].reshape(512, 512).T

    copy = pltpu.make_async_copy(g_turned, grads_out, out_sem)
    copy.start()
    all_of(a)
    all_of(b)
    high, low = halves(jnp.concatenate([sum4(end_z), sum4(end_x)], axis=0))
    solved[...] = one(inv_hi, high) + (one(inv_hi, low) + one(inv_lo, high))
    copy.wait()


def chain(activations, grad_out, momentum, right_factor):
    big = [((4, 4, 2, 256, 128), F32), ((2, 4, 64, RANK), F32), ((4, 2, 4, 16, RANK), F32)]
    shapes = [
        ((2048, RANK), BF16), ((2048, RANK), BF16), ((16, 32, 512), BF16),
        ((2, 4, 32, RANK), F32), ((4, 32, RANK), F32), ((4, 32, RANK), F32), ((4, 32, RANK), F32),
        ((4, 4, 2, 16, RANK), F32),
        ((2, 4, 64, RANK), F32), ((4, 64, RANK), F32), ((4, 64, RANK), F32), ((4, 64, RANK), F32),
        ((2, 4, 16, RANK), F32), ((4, 16, RANK), F32), ((4, 16, RANK), F32),
        ((4, 4, 2, 16, RANK), F32), ((4, 4, 16, RANK), F32), ((4, 4, 16, RANK), F32),
        ((4, 16, RANK), F32), ((4, 16, RANK), F32), ((4, 16, RANK), F32), ((4, 16, RANK), F32),
        ((2, 4, 2, 16, RANK), F32),
        ((2, 2, 256, 128), F32), ((2, 2, 256, 128), F32),
        ((2, 2, 256, 128), F32), ((2, 2, 256, 128), F32),
        ((2, 4, 256, 128), F32), ((2, 4, 256, 128), F32),
        ((4, 256, 128), F32), ((4, 256, 128), F32),
        ((4, 2, 2, 2, 4, 32, 512), BF16), ((8, 512, 512), BF16),
        ((RANK, RANK), F32), ((RANK, RANK), F32),
    ]
    semaphores = [(37, 3), (37, 3), (4, 2), (4, 2), ()]
    return pl.pallas_call(
        chain_kernel,
        out_shape=(
            jax.ShapeDtypeStruct((RANK, 128), F32),
            jax.ShapeDtypeStruct((RANK, RANK), F32),
            jax.ShapeDtypeStruct((8, 512, 512), BF16),
        ),
        in_specs=[VMEM] * 4,
        out_specs=(VMEM, VMEM, ANY),
        scratch_shapes=[pltpu.VMEM(*s) for s in big + shapes]
        + [pltpu.SemaphoreType.DMA(s) for s in semaphores],
        compiler_params=pltpu.CompilerParams(
            collective_id=1, has_side_effects=True, vmem_limit_bytes=58 << 20
        ),
        cost_estimate=pl.CostEstimate(flops=1 << 34, bytes_accessed=128 << 20, transcendentals=0),
    )(activations, grad_out.reshape(2, 2, 4, 32, 512), momentum, right_factor)


def gather_kernel(
    share, tokens, turned, momentum,
    out, buffer, scale,
    g_all, m_all, slots, sums, seen, send, recv, load_sem, tile_sem, store_sem,
):
    x, z, y, c = (lax.axis_index(a) for a in (X, Z, Y, C))

    def tile(j):
        slot = lax.rem(j, 2)
        columns = pl.ds(pl.multiple_of(256 * j, 256), 256)
        return pltpu.make_async_copy(tokens.at[:, columns], slots.at[slot], tile_sem.at[slot])

    def store(j):
        slot = lax.rem(j, 2)
        columns = pl.ds(pl.multiple_of(256 * j, 256), 256)
        return pltpu.make_async_copy(sums.at[slot], buffer.at[:, columns], store_sem.at[slot])

    loads = [
        pltpu.make_async_copy(turned.at[n], g_all.at[:, 512 * n : 512 * n + 512], load_sem.at[n])
        for n in range(8)
    ]
    loads.append(pltpu.make_async_copy(momentum, m_all, load_sem.at[8]))
    for load in loads:
        load.start()
    tile(0).start()
    tile(1).start()
    greet(line_peers((X, Z, Y, C)))
    own = share[...]
    out[x, z] = own.reshape(2, 256, 128)
    a = sent(send, recv, 0, Z, lambda to: out.at[x, z, 0], lambda to: out.at[x, z, 0])
    b = sent(send, recv, 1, X, lambda to: out.at[x, z, 1], lambda to: out.at[x, z, 1])
    seen[0, c] = lax.dot_general(
        jnp.ones((8, 128), F32), own * own, (((1,), (1,)), ((), ())),
        precision=lax.Precision.HIGHEST, preferred_element_type=F32,
    )
    all_of(sent(send, recv, 2, C, lambda to: seen.at[0, c], lambda to: seen.at[0, c]))
    seen[1, x] = seen[0, 0] + seen[0, 1]
    q = sent(send, recv, 3, X, lambda to: seen.at[1, x], lambda to: seen.at[1, x])
    for load in loads:
        load.wait()
    all_of(q)
    seen[2, z] = sum4(seen.at[1])
    q = sent(send, recv, 4, Z, lambda to: seen.at[2, z], lambda to: seen.at[2, z])
    all_of(a)
    a = gather_begun(send, recv, 6, X, lambda at: out.at[at, :, 0])
    all_of(b)
    b = gather_begun(send, recv, 10, Z, lambda at: out.at[:, at, 1])
    all_of(q)
    seen[3, y] = sum4(seen.at[2])
    q = sent(send, recv, 5, Y, lambda to: seen.at[3, y], lambda to: seen.at[3, y])

    def gradient(begin, end):
        @pl.loop(begin, end)
        def _(j):
            slot = lax.rem(j, 2)
            columns = pl.ds(pl.multiple_of(256 * j, 256), 256)
            tile(j).wait()

            @pl.when(j >= 2)
            def _():
                store(j - 2).wait()

            sums[slot] = m_all[:, columns] + one(g_all[...], slots[slot])
            store(j).start()

            @pl.when(j < 6)
            def _():
                tile(j + 2).start()

    gradient(0, 6)
    a = gather_relayed(send, recv, 6, X, a, lambda at, h: out.at[at, 2 * h : 2 * h + 2, 0])
    b = gather_relayed(send, recv, 10, Z, b, lambda at, h: out.at[2 * h : 2 * h + 2, at, 1])
    gradient(6, 8)
    all_of(q)
    scale[...] = jnp.sqrt(sum4(seen.at[3])) + EPSILON
    store(6).wait()
    store(7).wait()
    all_of(a)
    all_of(b)


def gathered(share, activations, grads, momentum):
    return pl.pallas_call(
        gather_kernel,
        out_shape=(
            jax.ShapeDtypeStruct((4, 4, 2, 256, 128), F32),
            jax.ShapeDtypeStruct((RANK, 2048), F32),
            jax.ShapeDtypeStruct((8, RANK), F32),
        ),
        in_specs=[VMEM, HBM, HBM, HBM],
        out_specs=(VMEM, ANY, VMEM),
        scratch_shapes=[
            pltpu.VMEM((512, 4096), BF16),
            pltpu.VMEM((RANK, 2048), F32),
            pltpu.VMEM((2, 4096, 256), BF16),
            pltpu.VMEM((2, RANK, 256), F32),
            pltpu.VMEM((4, 4, 8, RANK), F32),
            pltpu.SemaphoreType.DMA((14, 3)),
            pltpu.SemaphoreType.DMA((14, 3)),
            pltpu.SemaphoreType.DMA((9,)),
            pltpu.SemaphoreType.DMA((2,)),
            pltpu.SemaphoreType.DMA((2,)),
        ],
        compiler_params=pltpu.CompilerParams(
            collective_id=2, has_side_effects=True, vmem_limit_bytes=42 << 20
        ),
        cost_estimate=pl.CostEstimate(flops=1 << 34, bytes_accessed=128 << 20, transcendentals=0),
    )(share, activations, grads, momentum)


def final_kernel(b_ref, r_ref, l_ref, n_ref, momentum, right, update, low_ref, s_hi, s_lo, inv_ref):
    @pl.when(pl.program_id(0) == 0)
    def _():
        ortho = l_ref[...]
        inv_ref[...] = 1.0 / n_ref[...]
        low_ref[...] = (FEEDBACK * ortho).astype(BF16)
        s_hi[...], s_lo[...] = halves(ortho * (math.sqrt(DOUT * DIN / RANK) * inv_ref[0:1, :]))

    raw = jnp.concatenate([r_ref[0, k].reshape(RANK, 128) for k in range(4)], axis=1)
    r_hi, r_lo = halves(raw)
    momentum[...] = b_ref[...] - one(low_ref[...], r_hi)
    update[...] = (one(s_hi[...], r_hi) + (one(s_hi[...], r_lo) + one(s_lo[...], r_hi))).astype(BF16)
    right[...] = raw.T * inv_ref[0:1, :]


def final(buffer, right_t, left, norms):
    wide = 512
    tile = pl.BlockSpec((RANK, wide), lambda j: (0, j))
    return pl.pallas_call(
        final_kernel,
        grid=(2048 // wide,),
        in_specs=[
            tile,
            pl.BlockSpec((1, 4, 2, 256, 128), lambda j: (j, 0, 0, 0, 0)),
            pl.BlockSpec((RANK, RANK), lambda j: (0, 0)),
            pl.BlockSpec((8, RANK), lambda j: (0, 0)),
        ],
        out_specs=(tile, pl.BlockSpec((wide, RANK), lambda j: (j, 0)), tile),
        out_shape=(
            jax.ShapeDtypeStruct((RANK, 2048), F32),
            jax.ShapeDtypeStruct((2048, RANK), F32),
            jax.ShapeDtypeStruct((RANK, 2048), BF16),
        ),
        scratch_shapes=[pltpu.VMEM((RANK, RANK), BF16)] * 3 + [pltpu.VMEM((8, RANK), F32)],
        compiler_params=pltpu.CompilerParams(vmem_limit_bytes=24 << 20),
        cost_estimate=pl.CostEstimate(flops=1 << 32, bytes_accessed=20 << 20, transcendentals=0),
    )(buffer, right_t, left, norms)


def body(activations, grad_out, momentum, right_factor):
    all_activations = lax.all_gather(activations, WIDE, axis=0, tiled=True)
    share, ortho_left, grads = chain(activations, grad_out, momentum, right_factor)
    right_t, buffer, norms = gathered(share, all_activations, grads, momentum)
    return final(buffer, right_t, ortho_left, norms)


def solution(mesh):
    finer = Mesh(mesh.devices.reshape(4, 4, 4, 2), (X, Z, Y, C))
    in_specs = (P(WIDE, NARROW), P(NARROW, WIDE), P(WIDE, NARROW), P(NARROW, None))
    out_specs = (P(WIDE, NARROW), P(NARROW, None), P(WIDE, NARROW))
    return jax.shard_map(body, mesh=finer, in_specs=in_specs, out_specs=out_specs, check_vma=False)
```
